32 devices in a mesh: expert: 4 (over y, x), context: 4 (over z), dp: 2 (over core).
Axes of the slice: x: 2, y: 2, z: 4, core: 2. Of those that a mesh axis runs over, the one named last changes fastest.
Arguments:
- tokens: bfloat16 [8, 580, 768], P(('expert', 'dp'), 'context'), may hold values from -6 to 6
- cotangent: float32 [8, 580, 768], P(('expert', 'dp'), 'context'), may hold values from -6 to 6
- first_gain: bfloat16 [768], P(('expert', 'context', 'dp')), may hold values from 0.099609375 to 1.8984375
- first_attend: bfloat16 [768, 2304], P(('expert', 'context', 'dp')), may hold values from -0.21875 to 0.21875
- first_output: bfloat16 [768, 768], P(('expert', 'context', 'dp')), may hold values from -0.875 to 0.875
- second_gain: bfloat16 [768], P(('expert', 'context', 'dp')), may hold values from 0.099609375 to 1.8984375
- widen_in: bfloat16 [768, 3072], P(('expert', 'context', 'dp')), may hold values from -0.21875 to 0.21875
- widen_out: bfloat16 [3072, 768], P(('expert', 'context', 'dp')), may hold values from -0.15625 to 0.15625
- third_gain: bfloat16 [768], P(('expert', 'context', 'dp')), may hold values from 0.099609375 to 1.8984375
- second_attend: bfloat16 [768, 2304], P(('expert', 'context', 'dp')), may hold values from -0.21875 to 0.21875
- second_output: bfloat16 [768, 768], P(('expert', 'context', 'dp')), may hold values from -0.875 to 0.875
- fourth_gain: bfloat16 [768], P(('expert', 'context', 'dp')), may hold values from 0.099609375 to 1.8984375
- router: bfloat16 [768, 4], P(('expert', 'context', 'dp')), may hold values from -0.15625 to 0.15625
- expert_in: bfloat16 [4, 768, 3072], P('expert', None, 'dp'), may hold values from -0.21875 to 0.21875
- expert_out: bfloat16 [4, 3072, 768], P('expert', 'dp'), may hold values from -0.3125 to 0.3125
- routes: int32 [8, 580, 2], P(('expert', 'dp'), 'context'), may hold values from 0 to 3, as said below
- buffer_slot: int32 [8, 580, 2], P(('expert', 'dp'), 'context'), may hold values from 0 to 91, as said below
Outputs:
- activations: float32 [8, 580, 768], P(('expert', 'dp'), 'context')
- token_slope: float32 [8, 580, 768], P(('expert', 'dp'), 'context')
- first_gain_slope: float32 [768], P(('expert', 'context', 'dp'))
- first_attend_slope: float32 [768, 2304], P(('expert', 'context', 'dp'))
- first_output_slope: float32 [768, 768], P(('expert', 'context', 'dp'))
- second_gain_slope: float32 [768], P(('expert', 'context', 'dp'))
- widen_in_slope: float32 [768, 3072], P(('expert', 'context', 'dp'))
- widen_out_slope: float32 [3072, 768], P(('expert', 'context', 'dp'))
- third_gain_slope: float32 [768], P(('expert', 'context', 'dp'))
- second_attend_slope: float32 [768, 2304], P(('expert', 'context', 'dp'))
- second_output_slope: float32 [768, 768], P(('expert', 'context', 'dp'))
- fourth_gain_slope: float32 [768], P(('expert', 'context', 'dp'))
- router_slope: float32 [768, 4], P(('expert', 'context', 'dp'))
- expert_in_slope: float32 [4, 768, 3072], P('expert', None, 'dp')
- expert_out_slope: float32 [4, 3072, 768], P('expert', 'dp')
The draws below stay inside these ranges and needn't reach their ends.
Inputs may be any that keep to these rules, and one draw needn't show every extreme that they name: `routes`: the 2 experts of a slot differ. `buffer_slot`: within the 145 slots of one device, the kept pairs of each expert hold the rows 0, 1, ... in turn, each once; padding slots and dropped pairs hold 91; in every draw some expert gets all 91 rows from every device.
All inputs are finite; a program needn't handle non-finite values.
Results may differ from the reference program's by a relative error of at most 0.02.
Values may be sent and summed in bfloat16 or wider, within the bound.
No kernel may reach another device: no remote copies, remote signals or barrier semaphores. Data moves between devices by JAX's collectives and lax.ppermute only.
A program may use at most 256 MiB of HBM per device.

```python
import jax
import jax.numpy as jnp
from jax import lax

D = 768
HEADS = 12
HEAD_DIM = 64
FF = 3072
TOP = 2
IMG_DEV = 1
BLK = 145
SLOTS = 580
LONG = 1
IMAGES = 8
EXPERTS = 4
CAP = 91
N_CONTEXT = 4


def device_order(values_in):
    groups = IMAGES // IMG_DEV
    blocks = SLOTS // BLK
    trailing = values_in.shape[2:]
    divided = values_in.reshape((groups, IMG_DEV, blocks, BLK) + trailing)
    swapped = jnp.moveaxis(divided, 2, 1)
    return swapped.reshape((groups * blocks, IMG_DEV * BLK) + trailing)


def image_order(values_in):
    groups = IMAGES // IMG_DEV
    blocks = SLOTS // BLK
    trailing = values_in.shape[2:]
    divided = values_in.reshape((groups, blocks, IMG_DEV, BLK) + trailing)
    swapped = jnp.moveaxis(divided, 1, 2)
    return swapped.reshape((IMAGES, SLOTS) + trailing)


def route_pairs(key):
    score_key, order_key, hot_key, tilt_key = jax.random.split(key, 4)
    tilted = jax.random.permutation(tilt_key, EXPERTS).astype(jnp.int32) + EXPERTS
    noise_draw = jax.random.randint(score_key, (IMAGES, SLOTS, EXPERTS), 0, 4096, dtype=jnp.int32)
    scores = noise_draw * tilted * EXPERTS + jnp.arange(EXPERTS, dtype=jnp.int32)
    top_two = device_order(lax.top_k(scores, TOP)[1].astype(jnp.int32))
    owners = top_two.shape[0]
    per_owner = top_two.shape[1]
    local_index = jnp.arange(per_owner, dtype=jnp.int32)[None, :]
    block_index = (jnp.arange(owners, dtype=jnp.int32) % (SLOTS // BLK))[:, None]
    usable = (block_index < LONG) | (local_index % BLK < BLK - 1)
    forced = usable & (local_index < min(per_owner, 2 * CAP))
    hot_expert = jax.random.randint(hot_key, (), 0, EXPERTS, dtype=jnp.int32)
    first_pick = top_two[..., 0]
    other_pick = jnp.where(first_pick == hot_expert, top_two[..., 1], first_pick)
    second_pick = jnp.where(forced, other_pick, top_two[..., 1])
    first_pick = jnp.where(forced, hot_expert, first_pick)
    chosen = jnp.stack([first_pick, second_pick], -1)
    pair_ids = chosen.reshape(owners, per_owner * TOP)
    live_pair = jnp.repeat(usable, TOP, axis=1)
    order_draw = jax.random.randint(order_key, (owners, per_owner * TOP), 0, 4096, dtype=jnp.int32)
    order_draw = order_draw * (per_owner * TOP) + jnp.arange(per_owner * TOP, dtype=jnp.int32)
    matches = (pair_ids[:, :, None] == pair_ids[:, None, :]) & live_pair[:, None, :]
    matches = matches & (order_draw[:, None, :] < order_draw[:, :, None])
    earlier = jnp.sum(matches.astype(jnp.int32), axis=2)
    slot_ids = jnp.where(live_pair, jnp.minimum(earlier, CAP), CAP).reshape(owners, per_owner, TOP)
    return (image_order(chosen), image_order(slot_ids.astype(jnp.int32)))


def draw_routes(key, part):
    shared = route_pairs(key)
    return shared[0]


def draw_buffer_slot(key, part):
    shared = route_pairs(key)
    return shared[1]


def block_scale(key, shape, pieces, smallest, top_value):
    def one(dim, parts):
        steps = jax.random.uniform(jax.random.fold_in(jax.random.fold_in(key, 6), dim), (parts,), jnp.float32, smallest / len(pieces), top_value / len(pieces))
        return jnp.repeat(jnp.exp(steps), shape[dim] // parts).reshape((-1,) + (1,) * (len(shape) - dim - 1))

    gain = one(*pieces[0])
    for cut in pieces[1:]:
        gain = gain * one(*cut)
    return gain


def normal_values(stream_key, shape, width, reach, pieces=(), kind=jnp.bfloat16):
    level = block_scale(stream_key, shape, pieces, -0.22, 0.18) if pieces else 1.0
    values = jax.random.normal(stream_key, shape, jnp.float32) * width * level
    return jnp.minimum(jnp.maximum(values, -reach), reach).astype(kind)


def setup_inputs(seed: int = 0) -> dict:
    streams_of = jax.random.split(jax.random.key(seed), 18)
    tokens = normal_values(streams_of[0], (IMAGES, SLOTS, D), 1.0, 6.0, ((0, 8), (1, 4)))
    cotangent = normal_values(streams_of[1], (IMAGES, SLOTS, D), 1.0, 6.0, ((0, 8), (1, 4)), jnp.float32)
    first_gain = jnp.clip(1.0 + 0.18 * jax.random.normal(streams_of[2], (D,), jnp.float32), 0.099609375, 1.8984375).astype(jnp.bfloat16)
    first_attend = normal_values(streams_of[3], (D, 3 * D), D ** -0.5, 0.21875, ((0, 32),))
    first_output = normal_values(streams_of[4], (D, D), (D // 16) ** -0.5, 0.875, ((0, 32),))
    second_gain = jnp.clip(1.0 + 0.18 * jax.random.normal(streams_of[5], (D,), jnp.float32), 0.099609375, 1.8984375).astype(jnp.bfloat16)
    widen_in = normal_values(streams_of[6], (D, FF), D ** -0.5, 0.21875, ((0, 32),))
    widen_out = normal_values(streams_of[7], (FF, D), (FF // 2) ** -0.5, 0.15625, ((0, 32),))
    third_gain = jnp.clip(1.0 + 0.18 * jax.random.normal(streams_of[8], (D,), jnp.float32), 0.099609375, 1.8984375).astype(jnp.bfloat16)
    second_attend = normal_values(streams_of[9], (D, 3 * D), D ** -0.5, 0.21875, ((0, 32),))
    second_output = normal_values(streams_of[10], (D, D), (D // 16) ** -0.5, 0.875, ((0, 32),))
    fourth_gain = jnp.clip(1.0 + 0.18 * jax.random.normal(streams_of[11], (D,), jnp.float32), 0.099609375, 1.8984375).astype(jnp.bfloat16)
    router = normal_values(streams_of[12], (D, EXPERTS), (2 * D) ** -0.5, 0.15625, ((0, 32),))
    expert_in = normal_values(streams_of[13], (EXPERTS, D, FF), D ** -0.5, 0.21875, ((0, 4), (2, 2)))
    expert_out = normal_values(streams_of[14], (EXPERTS, FF, D), (max(1, 2 * FF // (EXPERTS * EXPERTS))) ** -0.5, 0.3125, ((0, 4), (1, 2)))
    routes = draw_routes(jax.random.fold_in(streams_of[17], 71), 0)
    buffer_slot = draw_buffer_slot(jax.random.fold_in(streams_of[17], 71), 0)
    return {"tokens": tokens, "cotangent": cotangent, "first_gain": first_gain, "first_attend": first_attend, "first_output": first_output, "second_gain": second_gain, "widen_in": widen_in, "widen_out": widen_out, "third_gain": third_gain, "second_attend": second_attend, "second_output": second_output, "fourth_gain": fourth_gain, "router": router, "expert_in": expert_in, "expert_out": expert_out, "routes": routes, "buffer_slot": buffer_slot}


@jax.custom_vjp
def low(v):
    return lax.optimization_barrier(v.astype(jnp.bfloat16)).astype(jnp.float32)

@jax.custom_vjp
def low_back(v):
    return v

def low_keep(v):
    return (low(v), None)

def low_pass(kept, grad):
    return (grad,)

def back_keep(v):
    return (v, None)

def back_low(kept, grad):
    return (low(grad),)
low.defvjp(low_keep, low_pass)
low_back.defvjp(back_keep, back_low)
highest = lax.Precision.HIGHEST

def valid_slots():
    position = jnp.arange(SLOTS, dtype=jnp.int32)
    return (position // BLK < LONG) | (position % BLK < BLK - 1)

def layer_norm(stream, norm_gain):
    centre = stream - lax.optimization_barrier(jnp.mean(stream, -1, keepdims=True))
    spread = lax.optimization_barrier(jnp.mean(centre * centre, -1, keepdims=True))
    return centre * lax.rsqrt(spread + 1e-06) * norm_gain

def attend(stream, norm_gain, mixing, output, usable):
    images = stream.shape[0]
    normed = low(layer_norm(stream, norm_gain))
    packed = low(low_back(jnp.einsum('isd,de->ise', normed, mixing, precision=highest)))
    queries = packed[..., :D].reshape(images, SLOTS, HEADS, HEAD_DIM)
    keys_all = packed[..., D:2 * D].reshape(images, SLOTS, HEADS, HEAD_DIM)
    values_all = packed[..., 2 * D:].reshape(images, SLOTS, HEADS, HEAD_DIM)
    scores = low_back(jnp.einsum('iqhd,ikhd->ihqk', queries, keys_all, precision=highest) * 0.125)
    scores = jnp.where(usable[None, None, None, :], scores, -1000000000.0)
    shares = jax.nn.softmax(scores, axis=-1)
    blended = jnp.einsum('ihqk,ikhd->iqhd', low(shares), values_all, precision=highest)
    blended = low(low_back(blended.reshape(images, SLOTS, D)))
    branch = low_back(jnp.einsum('isd,de->ise', blended, output, precision=highest))
    return stream + branch

def feed_forward(stream, norm_gain, weight_in, weight_out):
    normed = low(layer_norm(stream, norm_gain))
    hidden = low_back(jnp.einsum('isd,df->isf', normed, weight_in, precision=highest))
    active = low(jax.nn.gelu(hidden))
    branch = low_back(jnp.einsum('isf,fd->isd', active, weight_out, precision=highest))
    return stream + branch

def by_device(values_in):
    groups = IMAGES // IMG_DEV
    trailing = values_in.shape[3:]
    divided = values_in.reshape((groups, IMG_DEV, N_CONTEXT, BLK) + trailing)
    swapped = jnp.moveaxis(divided, 2, 1)
    return swapped.reshape((groups * N_CONTEXT, IMG_DEV * BLK) + trailing)

def by_image(values_in):
    groups = IMAGES // IMG_DEV
    trailing = values_in.shape[2:]
    divided = values_in.reshape((groups, N_CONTEXT, IMG_DEV, BLK) + trailing)
    swapped = jnp.moveaxis(divided, 1, 2)
    return swapped.reshape((IMAGES, SLOTS) + trailing)

def forward(tokens, first_gain, first_attend, first_output, second_gain, widen_in, widen_out, third_gain, second_attend, second_output, fourth_gain, router, expert_in, expert_out, routes, buffer_slot):
    usable = valid_slots()
    groups = IMAGES // IMG_DEV
    owners_all = groups * N_CONTEXT
    grouped = tokens.reshape(groups, IMG_DEV, SLOTS, D)

    def dense_part(images_block):
        stream = attend(images_block, first_gain, first_attend, first_output, usable)
        stream = feed_forward(stream, second_gain, widen_in, widen_out)
        stream = attend(stream, third_gain, second_attend, second_output, usable)
        normed = low(layer_norm(stream, fourth_gain))
        logits = low_back(jnp.einsum('isd,de->ise', normed, router, precision=highest))
        return (stream, normed, logits)
    stream, normed, logits = lax.map(jax.checkpoint(dense_part), grouped)
    local_stream = by_device(stream)
    local_normed = by_device(normed)
    gates_all = jax.nn.softmax(by_device(logits), axis=-1)
    chosen = by_device(routes.reshape(groups, IMG_DEV, SLOTS, TOP))
    placed_slot = by_device(buffer_slot.reshape(groups, IMG_DEV, SLOTS, TOP))
    gate_values = jnp.take_along_axis(gates_all, chosen, axis=-1)
    target = jnp.where(placed_slot < CAP, chosen * CAP + placed_slot, EXPERTS * CAP).astype(jnp.int32)
    owners = jnp.arange(owners_all, dtype=jnp.int32)[:, None, None]
    copies = jnp.broadcast_to(local_normed[:, :, None, :], target.shape + (D,))
    buffer = jnp.zeros((owners_all, EXPERTS * CAP + 1, D), jnp.float32).at[owners, target].add(copies)
    per_expert = jnp.moveaxis(buffer[:, :EXPERTS * CAP].reshape(owners_all, EXPERTS, CAP, D), 1, 0)

    def expert(inputs):
        arrived, weight_in, weight_out = inputs
        flattened = arrived.reshape(-1, D)
        active = low(jax.nn.gelu(low_back(jnp.dot(flattened, weight_in, precision=highest))))
        result = low(low_back(jnp.dot(active, weight_out, precision=highest)))
        return result.reshape(arrived.shape)
    returned = lax.map(jax.checkpoint(expert), (per_expert, expert_in, expert_out))
    returned = jnp.moveaxis(returned, 0, 1).reshape(owners_all, EXPERTS * CAP, D)
    returned = jnp.concatenate([returned, jnp.zeros((owners_all, 1, D), jnp.float32)], axis=1)
    picked = returned[owners, target]
    mixed_sum = lax.optimization_barrier(jnp.sum(gate_values[..., None] * picked, axis=2))
    result = by_image(local_stream + mixed_sum)
    return result * usable.astype(jnp.float32)[None, :, None]

def reference(tokens, cotangent, first_gain, first_attend, first_output, second_gain, widen_in, widen_out, third_gain, second_attend, second_output, fourth_gain, router, expert_in, expert_out, routes, buffer_slot):
    floats = [array_in.astype(jnp.float32) for array_in in (tokens, first_gain, first_attend, first_output, second_gain, widen_in, widen_out, third_gain, second_attend, second_output, fourth_gain, router, expert_in, expert_out)]

    def wrapped(*values_in):
        return forward(*values_in, routes, buffer_slot)
    result, pullback = jax.vjp(wrapped, *floats)
    slopes = pullback(cotangent.astype(jnp.float32))
    return (result, slopes[0], slopes[1], slopes[2], slopes[3], slopes[4], slopes[5], slopes[6], slopes[7], slopes[8], slopes[9], slopes[10], slopes[11], slopes[12], slopes[13])
```

```python
import functools

import jax
import jax.numpy as jnp
from jax import lax
from jax.sharding import PartitionSpec as P

HEADS = 12
HEAD_DIM = 64
LEN = 577
TOP = 2
ALL = ("expert", "context", "dp")
CHIPS = ("expert", "context")
BF = jnp.bfloat16
F32 = jnp.float32


def up16(n):
    return (n + 15) // 16 * 16


def dot(a, b):
    return jnp.dot(a, b, preferred_element_type=F32)


def dot_t(a, b):
    return lax.dot_general(a, b, (((1,), (1,)), ((), ())), preferred_element_type=F32)


def t_dot(a, b):
    return lax.dot_general(a, b, (((0,), (0,)), ((), ())), preferred_element_type=F32)


class Links:
    def __init__(self, mesh):
        self.E = mesh.shape["expert"]
        self.C = mesh.shape["context"]
        self.D = mesh.shape["dp"]
        assert self.C == 4 and self.D == 2 and self.E % 2 == 0
        self.fast = self.E == 4
        flat = lambda e, c, d: (e * self.C + c) * self.D + d
        self.team = [
            (flat(e, c, d), flat((e // 2) * 2 + c // 2, 2 * (e % 2) + d, c % 2))
            for e in range(self.E)
            for c in range(self.C)
            for d in range(self.D)
        ]

    def move(self, x):
        return lax.ppermute(x, ALL, self.team)

    def xor(self, x, axis, j):
        n = {"expert": self.E, "context": self.C, "dp": self.D}[axis]
        return lax.ppermute(x, axis, [(i, i ^ j) for i in range(n)])

    def sib(self, x):
        return self.xor(x, "dp", 1)

    def partner(self, x):
        return self.xor(x, "expert", 1)

    def gather(self, x, first):
        if not self.fast:
            return lax.all_gather(x, CHIPS, axis=0, tiled=True)
        c = lax.axis_index("context")
        e = lax.axis_index("expert")
        parts = jnp.stack([x] + [self.xor(x, "context", j) for j in range(1, 4)])
        own = jnp.concatenate(
            [lax.dynamic_index_in_dim(parts, c ^ k, 0, False) for k in range(4)], 0
        )
        second = 3 - first
        blocks = {0: own, first: self.xor(own, "expert", first)}
        blocks[second] = self.xor(own, "expert", second)
        blocks[3] = self.xor(blocks[first], "expert", second)
        stacked = jnp.stack([blocks[j] for j in range(4)])
        return jnp.concatenate(
            [lax.dynamic_index_in_dim(stacked, e ^ k, 0, False) for k in range(4)], 0
        )

    def scatter(self, g, first):
        if not self.fast:
            return lax.psum_scatter(g.astype(BF), CHIPS, scatter_dimension=0, tiled=True).astype(F32)
        c = lax.axis_index("context")
        e = lax.axis_index("expert")
        n = g.shape[1]
        g = g.astype(BF).reshape(4, -1, n)
        second = 3 - first
        blk = [lax.dynamic_index_in_dim(g, e ^ j, 0, False) for j in range(4)]
        r0 = self.xor(blk[first], "expert", first)
        r1 = self.xor(blk[3], "expert", first)
        s1 = (blk[second].astype(F32) + r1.astype(F32)).astype(BF)
        r2 = self.xor(s1, "expert", second)
        s0 = (blk[0].astype(F32) + r0.astype(F32) + r2.astype(F32)).astype(BF)
        s0 = s0.reshape(4, -1, n)
        total = lax.dynamic_index_in_dim(s0, c, 0, False).astype(F32)
        for j in range(1, 4):
            piece = lax.dynamic_index_in_dim(s0, c ^ j, 0, False)
            total = total + self.xor(piece, "context", j).astype(F32)
        return total

    def total(self, x):
        if not self.fast:
            return lax.psum(x, ALL)
        x = x + self.xor(x, "dp", 1)
        x = x + self.xor(x, "expert", 1)
        x = x + self.xor(x, "expert", 2)
        x = x + self.xor(x, "context", 1)
        return x + self.xor(x, "context", 2)

    def swap_blocks(self, x):
        if not self.fast:
            return lax.all_to_all(x, "expert", 0, 0, tiled=True)
        return jnp.stack([x[0]] + [self.xor(x[j], "expert", j) for j in range(1, 4)])


def norm_parts(x):
    mean = jnp.mean(x, -1, keepdims=True)
    centre = x - mean
    scale = lax.rsqrt(jnp.mean(centre * centre, -1, keepdims=True) + 1e-06)
    return centre * scale, scale


def layer_norm(x, gain):
    return (norm_parts(x)[0] * gain).astype(BF)


def layer_norm_back(x, gain, slope):
    unit, scale = norm_parts(x)
    gain_slope = jnp.sum(slope * unit, 0)
    inner = slope * gain
    inner = inner - jnp.mean(inner, -1, keepdims=True) - unit * jnp.mean(inner * unit, -1, keepdims=True)
    return inner * scale, gain_slope


def gelu_both(h):
    k = 0.7978845608028654
    t = jnp.tanh(k * (h + 0.044715 * h * h * h))
    return 0.5 * h * (1 + t), 0.5 * (1 + t) + 0.5 * h * (1 - t * t) * k * (1 + 3 * 0.044715 * h * h)


def lane_rows(links, mine, d):
    keep = lax.dynamic_index_in_dim(mine, d, 0, False)
    give = lax.dynamic_index_in_dim(mine, 1 - d, 0, False)
    got = links.sib(give)
    return jnp.where(d == 0, jnp.concatenate([keep, got], 0), jnp.concatenate([got, keep], 0))


def in_order(d, own, other):
    return jnp.where(d == 0, jnp.stack([own, other]), jnp.stack([other, own]))


def body(links, *args):
    (tokens, cotangent, g1, w1, p1, g2, win, wout, g3, w3, p3, g4, router, ein, eout, routes, slots) = args
    e = lax.axis_index("expert")
    d = lax.axis_index("dp")
    blk_len, feat = tokens.shape[1:]
    rows = up16(blk_len)
    half = feat // 2
    chips = links.E * links.C
    rdev = w1.shape[0]
    ff = win.shape[1]
    lane_ff = ff // 2
    longest = LEN - (blk_len - 1) * links.C
    experts = router.shape[1]
    cap = max(2, (5 * TOP * blk_len + 4 * experts - 1) // (4 * experts))
    cap_rows = up16(cap)
    blk = 2 * (e % 2) + d

    def pad(x):
        return jnp.pad(x, ((0, rows - blk_len), (0, 0)))

    small = jnp.concatenate([g1[:, None], g2[:, None], g3[:, None], g4[:, None], router], 1)
    small = in_order(d, small, links.sib(small)).reshape(2 * rdev, -1)
    small = links.gather(small, 1)
    gains = small[:, :4].T.astype(F32)
    router_all = small[:, 4:]

    x0 = pad(links.move(tokens[0])).astype(F32)

    def attend_weights(w, p):
        w = w.reshape(rdev, 3, 2, half).transpose(2, 0, 1, 3).reshape(2, rdev, 3 * half)
        w = lane_rows(links, w, d)
        qk = links.gather(w[:, : 2 * half], 1)
        v = links.gather(w[:, 2 * half :], 2)
        p = links.gather(p, 2).reshape(2, chips // 2, rdev, feat)
        own = lax.dynamic_index_in_dim(p, d, 0, False)
        other = links.sib(lax.dynamic_index_in_dim(p, 1 - d, 0, False))
        p = in_order(d, own, other).transpose(1, 0, 2, 3).reshape(half, feat)
        return qk, v, p

    def widen_weights():
        hid = ff // (2 * chips)
        w = win.reshape(rdev, chips, 2, hid).transpose(2, 0, 1, 3).reshape(2, rdev, lane_ff)
        return links.gather(lane_rows(links, w, d), 1), links.gather(wout, 2)

    wt1 = attend_weights(w1, p1)
    wt2 = widen_weights()
    wt3 = attend_weights(w3, p3)
    ein_own, eout_own = ein[0], eout[0]
    ein_sib, eout_sib = links.sib(ein_own), links.sib(eout_own)

    pos = jnp.arange(rows, dtype=jnp.int32)

    def valid(b):
        return (pos < blk_len) & ((b < longest) | (pos < blk_len - 1))

    key_ok = jnp.concatenate([valid(blk ^ j) for j in range(4)])
    present = valid(blk).astype(F32)[:, None]
    up = pad(links.move(cotangent[0])) * present
    index = links.move(jnp.concatenate([routes[0], slots[0]], 1))
    index = jnp.pad(index, ((0, rows - blk_len), (0, 0)), constant_values=cap)
    chosen, slot = index[:, :TOP], index[:, TOP:]

    heads = lambda t: t.reshape(t.shape[0], -1, HEAD_DIM)

    def both(t):
        return jnp.concatenate([t, links.sib(t)], 0)

    def reduce_pair(partial):
        return partial[:rows] + links.sib(partial[rows:].astype(BF)).astype(F32)

    def attend_forward(x, gain, wt):
        qk_w, v_w, p_w = wt
        normed = both(layer_norm(x, gain))
        qk = dot(normed, qk_w).astype(BF)
        v = dot(normed, v_w).astype(BF)
        q = qk[:, :half]
        kv = jnp.concatenate([qk[:, half:], v], 1)
        kv = jnp.concatenate([kv, links.partner(kv)], 0)
        s = jnp.einsum("qhd,khd->hqk", heads(q), heads(kv[:, :half]), preferred_element_type=F32) * 0.125
        s = jnp.where(key_ok[None, None, :], s, -1e9)
        top = jnp.max(s, -1, keepdims=True)
        ex = jnp.exp(s - top)
        total = jnp.sum(ex, -1, keepdims=True)
        lse = top + jnp.log(total)
        shares = (ex / total).astype(BF)
        blended = jnp.einsum("hqk,khd->qhd", shares, heads(kv[:, half:]), preferred_element_type=F32)
        blended = blended.reshape(2 * rows, half).astype(BF)
        return x + reduce_pair(dot(blended, p_w)), (x, normed, q, kv, lse, blended)

    def attend_backward(u, kept, gain, wt):
        x, normed, q, kv, lse, blended = kept
        qk_w, v_w, p_w = wt
        u_low = both(u.astype(BF))
        p_slope = t_dot(blended, u_low)
        b_slope = heads(dot_t(u_low, p_w).astype(BF))
        keys, values = heads(kv[:, :half]), heads(kv[:, half:])
        s = jnp.einsum("qhd,khd->hqk", heads(q), keys, preferred_element_type=F32) * 0.125
        s = jnp.where(key_ok[None, None, :], s, -1e9)
        shares = jnp.exp(s - lse)
        ss = jnp.einsum("qhd,khd->hqk", b_slope, values, preferred_element_type=F32)
        ss = (shares * (ss - jnp.sum(shares * ss, -1, keepdims=True))).astype(BF)
        q_slope = jnp.einsum("hqk,khd->qhd", ss, keys, preferred_element_type=F32) * 0.125
        k_slope = jnp.einsum("hqk,qhd->khd", ss, heads(q), preferred_element_type=F32) * 0.125
        v_slope = jnp.einsum("hqk,qhd->khd", shares.astype(BF), b_slope, preferred_element_type=F32)
        kv_slope = jnp.concatenate([k_slope.reshape(-1, half), v_slope.reshape(-1, half)], 1)
        got = links.partner(kv_slope[2 * rows :].astype(BF)).astype(F32)
        kv_slope = (kv_slope[: 2 * rows] + got).astype(BF)
        qk_slope = jnp.concatenate([q_slope.reshape(-1, half).astype(BF), kv_slope[:, :half]], 1)
        v_slope = kv_slope[:, half:]
        n_slope = dot_t(qk_slope, qk_w) + dot_t(v_slope, v_w)
        dx, g_slope = layer_norm_back(x, gain, reduce_pair(n_slope))
        return u + dx, g_slope, (t_dot(normed, qk_slope), t_dot(normed, v_slope), p_slope)

    def attend_owner(slopes):
        qk, v, p = slopes
        w = jnp.concatenate([links.scatter(qk, 1), links.scatter(v, 2)], 1)
        w = w.reshape(2, rdev, 3 * half)
        mine = lax.dynamic_index_in_dim(w, d, 0, False)
        got = links.sib(lax.dynamic_index_in_dim(w, 1 - d, 0, False))
        w = in_order(d, mine, got).reshape(2, rdev, 3, half).transpose(1, 2, 0, 3).reshape(rdev, 3 * feat)
        p = p.astype(BF).reshape(chips // 2, 2, rdev, feat)
        own = lax.dynamic_index_in_dim(p, d, 1, False)
        got = links.sib(lax.dynamic_index_in_dim(p, 1 - d, 1, False))
        p = in_order(d, own, got).reshape(chips * rdev, feat)
        return w, links.scatter(p, 2)

    def widen_owner(slope_in, slope_out):
        w = links.scatter(slope_in, 1).reshape(2, rdev, lane_ff)
        mine = lax.dynamic_index_in_dim(w, d, 0, False)
        got = links.sib(lax.dynamic_index_in_dim(w, 1 - d, 0, False))
        w = in_order(d, mine, got).reshape(2, rdev, chips, -1).transpose(1, 2, 0, 3).reshape(rdev, ff)
        return w, links.scatter(slope_out, 2)

    x1, kept1 = attend_forward(x0, gains[0], wt1)
    normed2 = both(layer_norm(x1, gains[1]))
    hidden = dot(normed2, wt2[0])
    active = gelu_both(hidden)[0].astype(BF)
    x2 = x1 + reduce_pair(dot(active, wt2[1]))
    x3, kept3 = attend_forward(x2, gains[2], wt3)

    moe = layer_norm(x3, gains[3])
    gates_all = jax.nn.softmax(dot(moe, router_all), axis=-1)
    expert_ids = jnp.arange(experts, dtype=jnp.int32)
    match = (chosen[:, :, None] == expert_ids).astype(F32)
    gate = jnp.sum(gates_all[:, None, :] * match, -1)
    place = chosen ^ e if links.fast else chosen
    target = jnp.where(slot < cap, place * cap_rows + slot, experts * cap_rows)
    pick = (target[:, :, None] == jnp.arange(experts * cap_rows, dtype=jnp.int32)).astype(BF)
    pick0, pick1 = pick[:, 0], pick[:, 1]
    sent = t_dot(pick0 + pick1, moe).astype(BF)
    slope0 = (gate[:, 0:1] * up).astype(BF)
    slope1 = (gate[:, 1:2] * up).astype(BF)
    sent_slope = (t_dot(pick0, slope0) + t_dot(pick1, slope1)).astype(BF)
    blocks = lambda a, b: jnp.stack([a.reshape(experts, cap_rows, feat), b.reshape(experts, cap_rows, feat)], 1)
    came = links.swap_blocks(blocks(sent, sent_slope))
    e_rows = came[:, 0].reshape(-1, feat)
    e_slope = came[:, 1].reshape(-1, feat)

    def expert_half(w_in, w_out):
        h = dot(e_rows, w_in)
        act, dact = gelu_both(h)
        act = act.astype(BF)
        result = dot(act, w_out)
        hs = (dact * dot_t(e_slope, w_out)).astype(BF)
        return result, dot_t(hs, w_in), t_dot(e_rows, hs), t_dot(act, e_slope)

    half_a = expert_half(ein_own, eout_own)
    half_b = expert_half(ein_sib, eout_sib)
    back = links.swap_blocks(blocks((half_a[0] + half_b[0]).astype(BF), (half_a[1] + half_b[1]).astype(BF)))
    result = back[:, 0].reshape(-1, feat)
    row_slope = back[:, 1].reshape(-1, feat)
    e_sums = []
    for k in (2, 3):
        mine = half_a[k] + links.sib(half_b[k].astype(BF)).astype(F32)
        e_sums.append(lax.psum(mine.astype(BF), "context").astype(F32))

    picked0, picked1 = dot(pick0, result), dot(pick1, result)
    acts = (x3 + gate[:, 0:1] * picked0 + gate[:, 1:2] * picked1) * present
    gate_slope = jnp.stack([jnp.sum(up * picked0, -1), jnp.sum(up * picked1, -1)], 1)
    all_slope = jnp.sum(gate_slope[:, :, None] * match, 1)
    logit_slope = gates_all * (all_slope - jnp.sum(gates_all * all_slope, -1, keepdims=True))
    logit_slope = logit_slope.astype(BF)
    router_slope = t_dot(moe, logit_slope)
    n_slope = dot(pick0 + pick1, row_slope) + dot_t(logit_slope, router_all)
    dx, g4_slope = layer_norm_back(x3, gains[3], n_slope)
    u = up + dx

    u, g3_slope, slopes3 = attend_backward(u, kept3, gains[2], wt3)
    u_low = both(u.astype(BF))
    wout_slope = t_dot(active, u_low)
    h_slope = (gelu_both(hidden)[1] * dot_t(u_low, wt2[1])).astype(BF)
    win_slope = t_dot(normed2, h_slope)
    dx, g2_slope = layer_norm_back(x1, gains[1], reduce_pair(dot_t(h_slope, wt2[0])))
    u = u + dx
    u, g1_slope, slopes1 = attend_backward(u, kept1, gains[0], wt1)

    w3_out, p3_out = attend_owner(slopes3)
    win_out, wout_out = widen_owner(win_slope, wout_slope)
    w1_out, p1_out = attend_owner(slopes1)
    small = jnp.concatenate([jnp.stack([g1_slope, g2_slope, g3_slope, g4_slope]), router_slope.T], 0)
    small = links.total(small)
    flat = (e * links.C + lax.axis_index("context")) * 2 + d
    small = small.reshape(-1, 2 * chips, rdev)
    small = lax.dynamic_index_in_dim(small, flat, 1, False)

    acts = links.move(acts[:blk_len])[None]
    token_slope = links.move(u[:blk_len])[None]
    return (
        acts, token_slope, small[0], w1_out, p1_out, small[1], win_out, wout_out,
        small[2], w3_out, p3_out, small[3], small[4:].T, e_sums[0][None], e_sums[1][None],
    )


def solution(mesh):
    links = Links(mesh)
    tok = P(("expert", "dp"), "context", None)
    vec, mat = P(ALL), P(ALL, None)
    ein, eout = P("expert", None, "dp"), P("expert", "dp", None)
    dense = (vec, mat, mat, vec, mat, mat, vec, mat, mat, vec, mat, ein, eout)
    return jax.shard_map(
        functools.partial(body, links),
        mesh=mesh,
        in_specs=(tok, tok) + dense + (tok, tok),
        out_specs=(tok, tok) + dense,
        check_vma=False,
    )
```

```python
import functools

import jax
import jax.numpy as jnp
from jax import lax
from jax.sharding import PartitionSpec as P

HEADS = 12
HEAD_DIM = 64
LEN = 577
TOP = 2
ALL = ("expert", "context", "dp")
CHIPS = ("expert", "context")
BF = jnp.bfloat16
F32 = jnp.float32


def up16(n):
    return (n + 15) // 16 * 16


def dot(a, b):
    return jnp.dot(a, b, preferred_element_type=F32)


def dot_t(a, b):
    return lax.dot_general(a, b, (((1,), (1,)), ((), ())), preferred_element_type=F32)


def t_dot(a, b):
    return lax.dot_general(a, b, (((0,), (0,)), ((), ())), preferred_element_type=F32)


class Links:
    def __init__(self, mesh):
        self.E = mesh.shape["expert"]
        self.C = mesh.shape["context"]
        self.D = mesh.shape["dp"]
        assert self.C == 4 and self.D == 2 and self.E % 2 == 0
        self.fast = self.E == 4
        self.chips = self.E * self.C
        flat = lambda e, c, d: (e * self.C + c) * self.D + d
        self.team = [
            (flat(e, c, d), flat((e // 2) * 2 + c // 2, 2 * (e % 2) + d, c % 2))
            for e in range(self.E)
            for c in range(self.C)
            for d in range(self.D)
        ]
        self.to_lane = [(f, (f % self.chips) * 2 + f // self.chips) for f in range(2 * self.chips)]
        self.from_lane = [(b, a) for a, b in self.to_lane]

    def move(self, x):
        return lax.ppermute(x, ALL, self.team)

    def xor(self, x, axis, j):
        n = {"expert": self.E, "context": self.C, "dp": self.D}[axis]
        return lax.ppermute(x, axis, [(i, i ^ j) for i in range(n)])

    def sib(self, x):
        return self.xor(x, "dp", 1)

    def partner(self, x):
        return self.xor(x, "expert", 1)

    def column(self, x):
        c = lax.axis_index("context")
        got = self.xor(x, "context", 1)
        x = jnp.where(c & 1 == 1, jnp.stack([got, x]), jnp.stack([x, got]))
        got = self.xor(x, "context", 2)
        return jnp.where(c & 2 == 2, jnp.concatenate([got, x]), jnp.concatenate([x, got]))

    def plane(self, x, first):
        second = 3 - first
        got = self.xor(x, "expert", first)
        far = self.xor(jnp.stack([x, got]), "expert", second)
        blocks = {0: x, first: got, second: far[0], 3: far[1]}
        return [blocks[j] for j in range(4)]

    def plane_sum(self, blk, first):
        second = 3 - first
        got = self.xor(jnp.stack([blk[first], blk[3]]), "expert", first).astype(F32)
        far = self.xor((blk[second].astype(F32) + got[1]).astype(BF), "expert", second)
        return blk[0].astype(F32) + got[0] + far.astype(F32)

    def column_sum(self, x):
        c = lax.axis_index("context")
        low, high = x[:2], x[2:]
        give = jnp.where(c & 2 == 2, low, high).astype(BF)
        x = jnp.where(c & 2 == 2, high, low) + self.xor(give, "context", 2).astype(F32)
        give = jnp.where(c & 1 == 1, x[0], x[1]).astype(BF)
        return jnp.where(c & 1 == 1, x[1], x[0]) + self.xor(give, "context", 1).astype(F32)

    def total(self, x):
        if not self.fast:
            return lax.psum(x, ALL)
        x = x + self.xor(x, "dp", 1)
        x = x + self.xor(x, "expert", 1)
        x = x + self.xor(x, "expert", 2)
        x = x + self.xor(x, "context", 1)
        return x + self.xor(x, "context", 2)

    def swap_blocks(self, x):
        if not self.fast:
            return list(lax.all_to_all(jnp.stack(x), "expert", 0, 0, tiled=True))
        return [x[0]] + [self.xor(x[j], "expert", j) for j in range(1, 4)]


def norm_parts(x):
    mean = jnp.mean(x, -1, keepdims=True)
    centre = x - mean
    scale = lax.rsqrt(jnp.mean(centre * centre, -1, keepdims=True) + 1e-06)
    return centre * scale, scale


def layer_norm(x, gain):
    return (norm_parts(x)[0] * gain).astype(BF)


def layer_norm_back(x, gain, slope, own):
    unit, scale = norm_parts(x)
    gain_slope = jnp.sum(slope[:own] * unit[:own], 0)
    inner = slope * gain
    inner = inner - jnp.mean(inner, -1, keepdims=True) - unit * jnp.mean(inner * unit, -1, keepdims=True)
    return inner * scale, gain_slope


def gelu_both(h):
    k = 0.7978845608028654
    t = jnp.tanh(k * (h + 0.044715 * h * h * h))
    return 0.5 * h * (1 + t), 0.5 * (1 + t) + 0.5 * h * (1 - t * t) * k * (1 + 3 * 0.044715 * h * h)


def lane_rows(links, mine, d):
    keep = lax.dynamic_index_in_dim(mine, d, 0, False)
    got = links.sib(lax.dynamic_index_in_dim(mine, 1 - d, 0, False))
    return jnp.where(d == 0, jnp.concatenate([keep, got], 0), jnp.concatenate([got, keep], 0))


def in_order(d, own, other):
    return jnp.where(d == 0, jnp.stack([own, other]), jnp.stack([other, own]))


class Weights:
    def __init__(self, links, rdev, feat, ff, experts):
        self.links, self.rdev, self.feat, self.ff, self.experts = links, rdev, feat, ff, experts
        self.e = lax.axis_index("expert")
        self.d = lax.axis_index("dp")
        self.half = feat // 2
        self.lane_ff = ff // 2

    def assemble(self, blocks):
        if not self.links.fast:
            return blocks
        stacked = jnp.stack(blocks)
        return jnp.concatenate(
            [lax.dynamic_index_in_dim(stacked, self.e ^ k, 0, False) for k in range(4)], 0
        )

    def split_attend(self, w):
        w = w.reshape(self.rdev, 3, 2, self.half).transpose(2, 0, 1, 3)
        return w.reshape(2, self.rdev, 3 * self.half)

    def split_widen(self, w):
        w = w.reshape(self.rdev, self.links.chips, 2, 2, -1).transpose(2, 0, 3, 1, 4)
        return w.reshape(2, self.rdev, self.lane_ff)

    def pack_attend(self, w, p, small):
        p = jnp.concatenate([p[:, : self.half], p[:, self.half :]], 0)
        parts = [w, p]
        if small is not None:
            parts.append(jnp.pad(small, ((0, 0), (0, 128 - small.shape[1]))))
        return jnp.concatenate(parts, 1)

    def pack_widen(self, w, wout):
        h = wout.shape[0] // 2
        return w, jnp.concatenate([wout[:h], wout[h:]], 1)

    def spread_attend(self, quad, first=1):
        f, h, r = self.feat, self.half, self.rdev
        n = quad.shape[0]
        qk = quad[..., :f].reshape(-1, f)
        v = quad[..., f : f + h].reshape(-1, h)
        p = quad[..., f + h : 2 * f].reshape(n, 2, r, h)
        left, right = p[:, 0].reshape(-1, h), p[:, 1].reshape(-1, h)
        rows = [v, left, right]
        has_small = quad.shape[2] > 2 * f
        if has_small:
            small = quad[..., 2 * f :].reshape(3, -1, 128)
            rows.append(jnp.concatenate([small[0], small[1], small[2]], 1))
        b = jnp.concatenate(rows, 0)
        if self.links.fast:
            a, b = self.links.plane(qk, first), self.links.plane(b, 3 - first)
            n1, n2 = v.shape[0], v.shape[0] + left.shape[0]
            n3 = n2 + left.shape[0]
            qk = self.assemble(a)
            v = self.assemble([t[:n1] for t in b])
            p = jnp.concatenate(
                [self.assemble([t[n1:n2] for t in b]), self.assemble([t[n2:n3] for t in b])], 1
            )
            if has_small:
                sm = [
                    jnp.concatenate([t[n3:, :128], t[n3:, 128:256], t[n3:, 256:]], 0) for t in b
                ]
                small = self.assemble(sm)
        else:
            p = jnp.concatenate([left, right], 1)
            if has_small:
                small = small.reshape(-1, 128)
        return (qk, v, p, small) if has_small else (qk, v, p)

    def spread_widen(self, quad_in, quad_out, first=1):
        f = self.feat
        out = []
        for i in range(2):
            a = quad_in[..., i * f : (i + 1) * f].reshape(-1, f)
            b = quad_out[..., i * f : (i + 1) * f].reshape(-1, f)
            if self.links.fast:
                n = a.shape[0]
                t = self.links.plane(jnp.concatenate([a, b], 0), first if i == 0 else 3 - first)
                out.append((self.assemble([x[:n] for x in t]), self.assemble([x[n:] for x in t])))
            else:
                out.append((a, b))
        return out

    def gather_column(self, buf):
        if self.links.fast:
            return self.links.column(buf)
        return lax.all_gather(buf, CHIPS, axis=0, tiled=False)

    def blocks(self, g):
        g = g.astype(BF).reshape(4, -1, g.shape[1])
        return [lax.dynamic_index_in_dim(g, self.e ^ j, 0, False) for j in range(4)]

    def owner_attend(self, qk, v, p, first=1):
        f, h, r, d = self.feat, self.half, self.rdev, self.d
        if self.links.fast:
            qk = self.links.plane_sum(self.blocks(qk), first)
            vb, lb, rb = self.blocks(v), self.blocks(p[:, :h]), self.blocks(p[:, h:])
            b = self.links.plane_sum(
                [jnp.concatenate(t, 0) for t in zip(vb, lb, rb)], 3 - first
            )
            n1 = 8 * r
            v, left, right = b[:n1], b[n1 : n1 + 4 * r], b[n1 + 4 * r :]
        else:
            left, right = p[:, :h], p[:, h:]
        qk, v = qk.reshape(-1, 2 * r, f), v.reshape(-1, 2 * r, h)
        p = jnp.concatenate([left.reshape(-1, r, h), right.reshape(-1, r, h)], 1)
        buf = jnp.concatenate([qk, v, p], 2)
        if self.links.fast:
            buf = self.links.column_sum(buf)
        else:
            buf = lax.psum_scatter(buf.astype(BF), CHIPS, scatter_dimension=0, tiled=False)
            buf = buf.astype(F32)
        w = buf[:, : f + h].reshape(2, r, f + h)
        p = jnp.concatenate([buf[:r, f + h :], buf[r:, f + h :]], 1)
        p = lax.ppermute(p, ALL, self.links.from_lane)
        mine = lax.dynamic_index_in_dim(w, d, 0, False)
        got = self.links.sib(lax.dynamic_index_in_dim(w, 1 - d, 0, False))
        w = in_order(d, mine, got).reshape(2, r, 3, h).transpose(1, 2, 0, 3).reshape(r, 3 * f)
        return w, p

    def owner_widen(self, halves, first=1):
        f, r, d = self.feat, self.rdev, self.d
        ins, outs = [], []
        for i, (a, b) in enumerate(halves):
            if self.links.fast:
                ab, bb = self.blocks(a), self.blocks(b)
                t = self.links.plane_sum(
                    [jnp.concatenate(x, 0) for x in zip(ab, bb)], first if i == 0 else 3 - first
                )
                a, b = t[: 8 * r], t[8 * r :]
            ins.append(a.reshape(-1, 2 * r, f))
            outs.append(b.reshape(-1, b.shape[0] // (4 if self.links.fast else self.links.chips), f))
        if self.links.fast:
            buf = self.links.column_sum(jnp.concatenate(ins + outs, 2))
            ins, outs = buf[:, : 2 * f], buf[:, 2 * f :]
        else:
            buf = [jnp.concatenate(ins, 2).astype(BF), jnp.concatenate(outs, 2).astype(BF)]
            ins, outs = [
                lax.psum_scatter(t, CHIPS, scatter_dimension=0, tiled=False).astype(F32) for t in buf
            ]
        w = ins.reshape(2, r, 2 * f)
        mine = lax.dynamic_index_in_dim(w, d, 0, False)
        got = self.links.sib(lax.dynamic_index_in_dim(w, 1 - d, 0, False))
        w = in_order(d, mine, got).reshape(2, r, 2, self.links.chips, -1)
        w = w.transpose(1, 3, 0, 2, 4).reshape(r, self.ff)
        return w, jnp.concatenate([outs[:, :f], outs[:, f:]], 0)


def body(links, *args):
    (tokens, cotangent, g1, w1, p1, g2, win, wout, g3, w3, p3, g4, router, ein, eout, routes, slots) = args
    e = lax.axis_index("expert")
    d = lax.axis_index("dp")
    blk_len, feat = tokens.shape[1:]
    rows = up16(blk_len)
    half = feat // 2
    rdev = w1.shape[0]
    ff = win.shape[1]
    longest = LEN - (blk_len - 1) * links.C
    experts = router.shape[1]
    cap = max(2, (5 * TOP * blk_len + 4 * experts - 1) // (4 * experts))
    cap_rows = up16(cap)
    blk = 2 * (e % 2) + d
    wt = Weights(links, rdev, feat, ff, experts)

    def pad(x):
        return jnp.pad(x, ((0, rows - blk_len), (0, 0)))

    def sib_cat(x):
        return jnp.concatenate([x, links.sib(x)], 0)

    small = jnp.concatenate([g1[:, None], g2[:, None], g3[:, None], g4[:, None], router], 1)
    gsm = small.shape[1]
    lane1 = jnp.concatenate(
        [wt.split_attend(w1), jnp.broadcast_to(small[None], (2, rdev, gsm))], 2
    )
    lane1 = lane_rows(links, lane1, d)
    ps = lax.ppermute(jnp.concatenate([p1, p3], 0), ALL, links.to_lane)
    x0 = sib_cat(pad(links.move(tokens[0]))).astype(F32)
    quad1 = wt.gather_column(
        wt.pack_attend(lane1[:, : 3 * half], ps[:rdev], lane1[:, 3 * half :])
    )
    wqk1, wv1, wp1, small = wt.spread_attend(quad1)
    gains = small[:, :4].T.astype(F32)
    router_all = small[:, 4:gsm]

    later = jnp.concatenate([wt.split_widen(win), wt.split_attend(w3)], 2)
    later = lane_rows(links, later, d)
    w_in, w_out = wt.pack_widen(later[:, : ff // 2], wout)
    if w_in.shape == w_out.shape:
        buf = jnp.concatenate([w_in, w_out, wt.pack_attend(later[:, ff // 2 :], ps[rdev:], None)], 1)
        buf, quad1 = lax.optimization_barrier((buf, quad1))
        quad = wt.gather_column(buf)
        quad2, quad3 = (quad[..., : ff // 2], quad[..., ff // 2 : ff]), quad[..., ff:]
    else:
        quad2 = wt.gather_column(w_in), wt.gather_column(w_out)
        quad3 = wt.gather_column(wt.pack_attend(later[:, ff // 2 :], ps[rdev:], None))
    wff = wt.spread_widen(*quad2)
    wqk3, wv3, wp3 = wt.spread_attend(quad3)

    ein_own, eout_own = ein[0], eout[0]
    ein_sib, eout_sib = links.sib(ein_own), links.sib(eout_own)

    pos = jnp.arange(rows, dtype=jnp.int32)

    def valid(b):
        return (pos < blk_len) & ((b < longest) | (pos < blk_len - 1))

    key_ok = jnp.concatenate([valid(blk ^ j) for j in range(4)])
    present = valid(blk).astype(F32)[:, None]
    up = pad(links.move(cotangent[0])) * present
    index = links.move(jnp.concatenate([routes[0], slots[0]], 1))
    index = jnp.pad(index, ((0, rows - blk_len), (0, 0)), constant_values=cap)
    chosen, slot = index[:, :TOP], index[:, TOP:]

    heads = lambda t: t.reshape(t.shape[0], -1, HEAD_DIM)

    def add_pair(x, partial, n):
        low = partial.astype(BF)
        if n == rows:
            return x[:rows] + partial[:rows] + links.sib(low[rows:]).astype(F32)
        got = links.sib(low)
        got = jnp.concatenate([got[rows:], got[:rows]], 0)
        return x + partial + got.astype(F32)

    def attend_forward(x, gain, wqk, wv, wp, n):
        normed = layer_norm(x, gain)
        qk = dot(normed, wqk).astype(BF)
        v = dot(normed, wv).astype(BF)
        q = qk[:, :half]
        kv = jnp.concatenate([qk[:, half:], v], 1)
        kv = jnp.concatenate([kv, links.partner(kv)], 0)
        s = jnp.einsum("qhd,khd->hqk", heads(q), heads(kv[:, :half]), preferred_element_type=F32) * 0.125
        s = jnp.where(key_ok[None, None, :], s, -1e9)
        top = jnp.max(s, -1, keepdims=True)
        ex = jnp.exp(s - top)
        total = jnp.sum(ex, -1, keepdims=True)
        lse = top + jnp.log(total)
        shares = (ex / total).astype(BF)
        blended = jnp.einsum("hqk,khd->qhd", shares, heads(kv[:, half:]), preferred_element_type=F32)
        blended = blended.reshape(2 * rows, half).astype(BF)
        return add_pair(x, dot(blended, wp), n), (x, normed, q, kv, lse, blended)

    def attend_backward(u, kept, gain, wqk, wv, wp, n):
        x, normed, q, kv, lse, blended = kept
        u_low = u.astype(BF)
        p_slope = t_dot(blended, u_low)
        b_slope = heads(dot_t(u_low, wp).astype(BF))
        keys, values = heads(kv[:, :half]), heads(kv[:, half:])
        s = jnp.einsum("qhd,khd->hqk", heads(q), keys, preferred_element_type=F32) * 0.125
        s = jnp.where(key_ok[None, None, :], s, -1e9)
        shares = jnp.exp(s - lse)
        ss = jnp.einsum("qhd,khd->hqk", b_slope, values, preferred_element_type=F32)
        ss = (shares * (ss - jnp.sum(shares * ss, -1, keepdims=True))).astype(BF)
        q_slope = jnp.einsum("hqk,khd->qhd", ss, keys, preferred_element_type=F32) * 0.125
        k_slope = jnp.einsum("hqk,qhd->khd", ss, heads(q), preferred_element_type=F32) * 0.125
        v_slope = jnp.einsum("hqk,qhd->khd", shares.astype(BF), b_slope, preferred_element_type=F32)
        kv_slope = jnp.concatenate([k_slope.reshape(-1, half), v_slope.reshape(-1, half)], 1)
        got = links.partner(kv_slope[2 * rows :].astype(BF)).astype(F32)
        kv_slope = (kv_slope[: 2 * rows] + got).astype(BF)
        qk_slope = jnp.concatenate([q_slope.reshape(-1, half).astype(BF), kv_slope[:, :half]], 1)
        v_slope = kv_slope[:, half:]
        n_slope = dot_t(qk_slope, wqk) + dot_t(v_slope, wv)
        dx, g_slope = norm_back(x, gain, n_slope, n)
        slopes = t_dot(normed, qk_slope), t_dot(normed, v_slope), p_slope
        return u[:n] + dx, g_slope, slopes

    def norm_back(x, gain, n_slope, n):
        n_slope = add_pair(jnp.zeros((2 * rows, 1), F32), n_slope, n)
        return layer_norm_back(x[:n], gain, n_slope, rows)

    x1, kept1 = attend_forward(x0, gains[0], wqk1, wv1, wp1, 2 * rows)
    normed2 = layer_norm(x1, gains[1])
    hidden = [dot(normed2, w) for w, _ in wff]
    active = [gelu_both(h)[0].astype(BF) for h in hidden]
    x2 = add_pair(x1, dot(active[0], wff[0][1]) + dot(active[1], wff[1][1]), 2 * rows)
    x3, kept3 = attend_forward(x2, gains[2], wqk3, wv3, wp3, rows)

    moe = layer_norm(x3, gains[3])
    gates_all = jax.nn.softmax(dot(moe, router_all), axis=-1)
    expert_ids = jnp.arange(experts, dtype=jnp.int32)
    match = (chosen[:, :, None] == expert_ids).astype(F32)
    gate = jnp.sum(gates_all[:, None, :] * match, -1)
    place = chosen ^ e if links.fast else chosen
    target = jnp.where(slot < cap, place * cap_rows + slot, experts * cap_rows)
    pick = (target[:, :, None] == jnp.arange(experts * cap_rows, dtype=jnp.int32)).astype(BF)
    pick0, pick1 = pick[:, 0], pick[:, 1]
    sent = t_dot(pick0 + pick1, moe).astype(BF)
    slope0 = (gate[:, 0:1] * up).astype(BF)
    slope1 = (gate[:, 1:2] * up).astype(BF)
    sent_slope = (t_dot(pick0, slope0) + t_dot(pick1, slope1)).astype(BF)

    def blocks(a, b):
        cut = lambda t, j: t[j * cap_rows : (j + 1) * cap_rows]
        return [jnp.concatenate([cut(a, j), cut(b, j)], 0) for j in range(experts)]

    def unblock(t):
        return jnp.concatenate([x[:cap_rows] for x in t]), jnp.concatenate([x[cap_rows:] for x in t])

    e_rows, e_slope = unblock(links.swap_blocks(blocks(sent, sent_slope)))

    def expert_half(w_in, w_out):
        h = dot(e_rows, w_in)
        act, dact = gelu_both(h)
        act = act.astype(BF)
        result = dot(act, w_out)
        hs = (dact * dot_t(e_slope, w_out)).astype(BF)
        return result, dot_t(hs, w_in), t_dot(e_rows, hs), t_dot(act, e_slope)

    half_a = expert_half(ein_own, eout_own)
    half_b = expert_half(ein_sib, eout_sib)
    back = blocks((half_a[0] + half_b[0]).astype(BF), (half_a[1] + half_b[1]).astype(BF))
    result, row_slope = unblock(links.swap_blocks(back))
    e_sums = []
    for k in (2, 3):
        mine = half_a[k] + links.sib(half_b[k].astype(BF)).astype(F32)
        e_sums.append(lax.psum(mine.astype(BF), "context").astype(F32))

    picked0, picked1 = dot(pick0, result), dot(pick1, result)
    acts = (x3 + gate[:, 0:1] * picked0 + gate[:, 1:2] * picked1) * present
    gate_slope = jnp.stack([jnp.sum(up * picked0, -1), jnp.sum(up * picked1, -1)], 1)
    all_slope = jnp.sum(gate_slope[:, :, None] * match, 1)
    logit_slope = gates_all * (all_slope - jnp.sum(gates_all * all_slope, -1, keepdims=True))
    logit_slope = logit_slope.astype(BF)
    router_slope = t_dot(moe, logit_slope)
    n_slope = dot(pick0 + pick1, row_slope) + dot_t(logit_slope, router_all)
    dx, g4_slope = layer_norm_back(x3, gains[3], n_slope, rows)
    u = up + dx
    u = jnp.concatenate([u, links.sib(u.astype(BF)).astype(F32)], 0)

    u, g3_slope, slopes3 = attend_backward(u, kept3, gains[2], wqk3, wv3, wp3, 2 * rows)
    w3_out, p3_out = wt.owner_attend(*slopes3)
    u_low = u.astype(BF)
    n_slope, slopes2 = 0.0, []
    for (wi, wo), h, a in zip(wff, hidden, active):
        h_slope = (gelu_both(h)[1] * dot_t(u_low, wo)).astype(BF)
        slopes2.append((t_dot(normed2, h_slope), t_dot(a, u_low)))
        n_slope = n_slope + dot_t(h_slope, wi)
    dx, g2_slope = norm_back(x1, gains[1], n_slope, 2 * rows)
    u = u + dx
    win_out, wout_out = wt.owner_widen(slopes2)
    u, g1_slope, slopes1 = attend_backward(u, kept1, gains[0], wqk1, wv1, wp1, rows)
    w1_out, p1_out = wt.owner_attend(*slopes1)

    small = jnp.concatenate([jnp.stack([g1_slope, g2_slope, g3_slope, g4_slope]), router_slope.T], 0)
    small = links.total(small)
    flat = (e * links.C + lax.axis_index("context")) * 2 + d
    small = small.reshape(-1, 2 * links.chips, rdev)
    small = lax.dynamic_index_in_dim(small, flat, 1, False)

    acts = links.move(acts[:blk_len])[None]
    token_slope = links.move(u[:blk_len])[None]
    return (
        acts, token_slope, small[0], w1_out, p1_out, small[1], win_out, wout_out,
        small[2], w3_out, p3_out, small[3], small[4:].T, e_sums[0][None], e_sums[1][None],
    )


def solution(mesh):
    links = Links(mesh)
    tok = P(("expert", "dp"), "context", None)
    vec, mat = P(ALL), P(ALL, None)
    ein, eout = P("expert", None, "dp"), P("expert", "dp", None)
    dense = (vec, mat, mat, vec, mat, mat, vec, mat, mat, vec, mat, ein, eout)
    return jax.shard_map(
        functools.partial(body, links),
        mesh=mesh,
        in_specs=(tok, tok) + dense + (tok, tok),
        out_specs=(tok, tok) + dense,
        check_vma=False,
    )
```

```python
import functools

import jax
import jax.numpy as jnp
from jax import lax
from jax.experimental import pallas as pl
from jax.experimental.pallas import tpu as pltpu
from jax.sharding import PartitionSpec as P

HEADS = 12
HEAD_DIM = 64
LEN = 577
TOP = 2
ALL = ("expert", "context", "dp")
CHIPS = ("expert", "context")
BF = jnp.bfloat16
F32 = jnp.float32
VM = pl.BlockSpec(memory_space=pltpu.VMEM)
HB = pl.BlockSpec(memory_space=pl.ANY)
SM = pl.BlockSpec(memory_space=pltpu.SMEM)


def up16(n):
    return (n + 15) // 16 * 16


def dot(a, b):
    return jnp.dot(a, b, preferred_element_type=F32)


def dot_t(a, b):
    return lax.dot_general(a, b, (((1,), (1,)), ((), ())), preferred_element_type=F32)


def t_dot(a, b):
    return lax.dot_general(a, b, (((0,), (0,)), ((), ())), preferred_element_type=F32)


def call(kernel, outs, ins, scratch=(), after=(), flops=0, bytes_accessed=0):
    n_in, n_after = len(ins), len(after)

    def run(*refs):
        kernel(*refs[:n_in], *refs[n_in + n_after :])

    return pl.pallas_call(
        run,
        out_shape=[jax.ShapeDtypeStruct(s, t) for s, t, _ in outs],
        in_specs=[s for _, s in ins] + [HB] * n_after,
        out_specs=[s for _, _, s in outs],
        scratch_shapes=list(scratch),
        compiler_params=pltpu.CompilerParams(vmem_limit_bytes=50 * 2**20),
        cost_estimate=pl.CostEstimate(
            flops=flops, bytes_accessed=bytes_accessed, transcendentals=0
        ),
    )(*[a for a, _ in ins], *after)


def norm_parts(x):
    mean = jnp.mean(x, -1, keepdims=True)
    centre = x - mean
    scale = lax.rsqrt(jnp.mean(centre * centre, -1, keepdims=True) + 1e-06)
    return centre * scale, scale


def layer_norm(x, gain):
    return (norm_parts(x)[0] * gain).astype(BF)


def norm_back(x, gain, slope, own):
    unit, scale = norm_parts(x)
    gain_slope = jnp.sum(slope[:own] * unit[:own], 0, keepdims=True)
    inner = slope * gain
    inner = inner - jnp.mean(inner, -1, keepdims=True) - unit * jnp.mean(inner * unit, -1, keepdims=True)
    return inner * scale, gain_slope


def gelu_both(h):
    k = 0.7978845608028654
    t = jnp.tanh(k * (h + 0.044715 * h * h * h))
    half = 0.5 * (1 + t)
    return h * half, half + 0.5 * h * (1 - t * t) * (k + (3 * 0.044715 * k) * h * h)


def add_both(mine, got, rows):
    return mine + jnp.concatenate([got[rows:], got[:rows]], 0).astype(F32)


def pair_masks():
    lane = lax.broadcasted_iota(jnp.int32, (1, 2 * HEAD_DIM), 1)
    return [(lane < HEAD_DIM).astype(BF), (lane >= HEAD_DIM).astype(BF)]


def key_mask(blk, rows, blk_len, longest):
    pos = lax.broadcasted_iota(jnp.int32, (rows, 1), 0)
    parts = []
    for j in range(4):
        last = jnp.where((blk ^ j) < longest, blk_len, blk_len - 1)
        parts.append(pos < last)
    return jnp.concatenate([jnp.where(p, 1.0, 0.0) for p in parts], 0) > 0.5


def attend_core(where, q, kv_own, kv_far, wp, rows, blk_len, longest, solo, after=()):
    half = q.shape[1]
    feat = wp.shape[1]
    pairs = half // (2 * HEAD_DIM)

    def kernel(where_ref, q_ref, ko_ref, kf_ref, wp_ref, part_ref, low_ref, blend_ref, lse_ref):
        ok = key_mask(where_ref[0], rows, blk_len, longest)
        masks = pair_masks()
        for p in range(pairs):
            at, vat = pl.ds(p * 128, 128), pl.ds(half + p * 128, 128)
            k = jnp.concatenate([ko_ref[:, at], kf_ref[:, at]], 0)
            v = jnp.concatenate([ko_ref[:, vat], kf_ref[:, vat]], 0)
            qp = q_ref[:, at]
            acc = None
            for h in range(2):
                s = dot_t(k, qp * masks[h]) * 0.125
                s = jnp.where(ok, s, -1e9)
                top = jnp.max(s, 0, keepdims=True)
                ex = jnp.exp(s - top)
                total = jnp.sum(ex, 0, keepdims=True)
                lse_ref[pl.ds(2 * p + h, 1), :] = top + jnp.log(total)
                shares = (ex * (1.0 / total)).astype(BF)
                out = t_dot(v * masks[h], shares)
                acc = out if acc is None else acc + out
            blend_ref[at, :] = acc.astype(BF)
        part = t_dot(blend_ref[...], wp_ref[...])
        part_ref[...] = part
        low_ref[...] = (part[rows:] if solo else part).astype(BF)

    r2 = 2 * rows
    return call(
        kernel,
        [((r2, feat), F32, VM), ((rows if solo else r2, feat), BF, VM), ((half, r2), BF, VM), ((8, r2), F32, VM)],
        [(where, SM), (q, VM), (kv_own, VM), (kv_far, VM), (wp, VM)],
        after=after,
        flops=2 * r2 * half * (8 * rows + feat),
        bytes_accessed=4 * 2**20,
    )


def attend_core_back(where, u_low, wp, blend, q, kv_own, kv_far, lse, rows, blk_len, longest, after=()):
    half = q.shape[1]
    feat = wp.shape[1]
    pairs = half // (2 * HEAD_DIM)
    r2 = 2 * rows

    def kernel(
        where_ref, u_ref, wp_ref, blend_ref, q_ref, ko_ref, kf_ref, lse_ref,
        dq_ref, own_ref, far_ref, wps_ref, bt_ref, dqt_ref,
    ):
        ok = key_mask(where_ref[0], rows, blk_len, longest)
        masks = pair_masks()
        sub = lax.broadcasted_iota(jnp.int32, (2 * HEAD_DIM, 1), 0)
        row_masks = [(sub < HEAD_DIM).astype(BF), (sub >= HEAD_DIM).astype(BF)]
        u = u_ref[...]
        bt_ref[...] = dot_t(wp_ref[...], u).astype(BF)
        for p in range(pairs):
            at, vat = pl.ds(p * 128, 128), pl.ds(half + p * 128, 128)
            k = jnp.concatenate([ko_ref[:, at], kf_ref[:, at]], 0)
            v = jnp.concatenate([ko_ref[:, vat], kf_ref[:, vat]], 0)
            qp = q_ref[:, at]
            bt = bt_ref[at, :]
            dqt = dk = dv = 0.0
            for h in range(2):
                qm = qp * masks[h]
                s = dot_t(k, qm) * 0.125
                shares = jnp.where(ok, jnp.exp(s - lse_ref[pl.ds(2 * p + h, 1), :]), 0.0)
                slope = dot(v * masks[h], bt)
                t = shares * slope
                ss = (t - shares * jnp.sum(t, 0, keepdims=True)).astype(BF)
                dqt += t_dot(k * masks[h], ss)
                dk += dot(ss, qm)
                dv += dot_t(shares.astype(BF), bt * row_masks[h])
            dqt_ref[at, :] = dqt * 0.125
            dk = dk * 0.125
            own_ref[:, at] = dk[:r2]
            own_ref[:, vat] = dv[:r2]
            far_ref[:, at] = dk[r2:].astype(BF)
            far_ref[:, vat] = dv[r2:].astype(BF)
        dq_ref[...] = dqt_ref[...].T.astype(BF)
        wps_ref[...] = dot(blend_ref[...], u).astype(BF)

    return call(
        kernel,
        [
            ((r2, half), BF, VM), ((r2, 2 * half), F32, VM), ((r2, 2 * half), BF, VM),
            ((half, feat), BF, VM),
        ],
        [
            (where, SM), (u_low, VM), (wp, VM), (blend, VM), (q, VM), (kv_own, VM), (kv_far, VM),
            (lse, VM),
        ],
        scratch=[pltpu.VMEM((half, r2), BF), pltpu.VMEM((half, r2), F32)],
        after=after,
        flops=2 * r2 * half * (20 * rows + 2 * feat),
        bytes_accessed=6 * 2**20,
    )


def block_refs(a0, a1, a23, first):
    second = 3 - first
    found = {0: a0, first: a1, second: a23.at[0], 3: a23.at[1]}
    return [found[j] for j in range(4)]


def start_all(copies):
    for c in copies:
        c.start()


def wait_all(copies):
    for c in copies:
        c.wait()


def attend_copies(e, a, b, w_ref, p_ref, small_ref, sems):
    copies = []

    def add(src, dst):
        copies.append(pltpu.make_async_copy(src, dst, sems.at[len(copies)]))

    n = w_ref.shape[0] // 4
    half = p_ref.shape[0]
    m = half // 4
    for j in range(4):
        to = e ^ j
        rows, prows = pl.ds(pl.multiple_of(to * n, 16), n), pl.ds(pl.multiple_of(to * m, 16), m)
        add(a[j], w_ref.at[rows, pl.ds(0, 2 * half)])
        add(b[j].at[pl.ds(0, n)], w_ref.at[rows, pl.ds(2 * half, half)])
        add(b[j].at[pl.ds(n, m)], p_ref.at[prows, pl.ds(0, half)])
        add(b[j].at[pl.ds(n + m, m)], p_ref.at[prows, pl.ds(half, half)])
        if small_ref is not None:
            for g in range(3):
                srows = pl.ds(pl.multiple_of(to * n + g * (n // 3), 16), n // 3)
                add(b[j].at[pl.ds(n + 2 * m, n // 3), pl.ds(128 * g, 128)], small_ref.at[srows])
    return copies


def attend_start(where, tokens, small_rows, gain_row, a, b, firsts, rows, after=()):
    opening = small_rows is not None
    feat = tokens[0].shape[1]
    half = feat // 2
    r2 = 2 * rows
    n_copy = 28 if opening else 16

    def kernel(where_ref, *refs):
        refs = list(refs)
        take = lambda n: [refs.pop(0) for _ in range(n)]
        tok = take(len(tokens))
        gain_ref = None if opening else take(1)[0]
        a_refs, b_refs = take(3), take(3)
        x_ref, normed_ref, q_ref, kv_ref, w_ref, p_ref = take(6)
        small_ref, rows_ref = take(2) if opening else (None, None)
        (sems,) = take(1)
        copies = attend_copies(
            where_ref[1], block_refs(*a_refs, firsts[0]), block_refs(*b_refs, firsts[1]),
            w_ref, p_ref, small_ref, sems,
        )
        start_all(copies)
        if opening:
            x_ref[...] = jnp.zeros_like(x_ref)
            n = tok[0].shape[0]
            x_ref[pl.ds(0, n), :] = tok[0][...].astype(F32)
            x_ref[pl.ds(rows, n), :] = tok[1][...].astype(F32)
            wait_all(copies)
            turned = small_ref[...].astype(F32).T
            rows_ref[...] = turned[: rows_ref.shape[0]]
            gain = turned[gain_row : gain_row + 1]
            x = x_ref[...]
            normed = layer_norm(x, gain)
        else:
            x = add_both(tok[0][...] + tok[1][...], tok[2][...], rows)
            x_ref[...] = x
            normed = layer_norm(x, gain_ref[pl.ds(gain_row, 1), :])
            wait_all(copies)
        normed_ref[...] = normed
        q_ref[...] = dot(normed, w_ref[:, :half]).astype(BF)
        kv_ref[...] = dot(normed, w_ref[:, half:]).astype(BF)

    outs = [
        ((r2, feat), F32, VM), ((r2, feat), BF, VM), ((r2, half), BF, VM), ((r2, feat), BF, VM),
        ((feat, 3 * half), BF, VM), ((half, feat), BF, VM),
    ]
    ins = [(where, SM)] + [(t, VM) for t in tokens]
    if opening:
        outs += [((feat, 128), BF, VM), ((small_rows, feat), F32, VM)]
    return ins, outs, kernel, n_copy


def attend_first(where, own, sib, small_rows, a, b, firsts, rows, after=()):
    ins, outs, kernel, n = attend_start(where, (own, sib), small_rows, 0, a, b, firsts, rows)
    ins += [(t, HB) for t in (*a, *b)]
    return call(
        kernel, outs, ins, scratch=[pltpu.SemaphoreType.DMA((n,))], after=after,
        flops=2 * 320 * 768 * 1152, bytes_accessed=6 * 2**20,
    )


def attend_next(where, x, part, got, gains, gain_row, a, b, firsts, rows, after=()):
    ins, outs, kernel, n = attend_start(where, (x, part, got), None, gain_row, a, b, firsts, rows)
    ins += [(gains, VM)] + [(t, HB) for t in (*a, *b)]
    return call(
        kernel, outs, ins, scratch=[pltpu.SemaphoreType.DMA((n,))], after=after,
        flops=2 * 320 * 768 * 1152, bytes_accessed=6 * 2**20,
    )


def widen_forward(where, x, part, got, gains, a, b, firsts, rows, after=()):
    r2, feat = x.shape
    wide = 2 * feat
    tile = 384

    def kernel(
        where_ref, x_ref, part_ref, got_ref, gains_ref, a0, a1, a23, b0, b1, b23,
        x1_ref, normed_ref, hidden_ref, out_ref, low_ref, wi_ref, wo_ref, sems,
    ):
        n = feat // 4
        copies = []
        for h, blocks in enumerate((block_refs(a0, a1, a23, firsts[0]), block_refs(b0, b1, b23, firsts[1]))):
            for j in range(4):
                at = (where_ref[1] ^ j) * n
                for src, dst in (
                    (blocks[j].at[0], wi_ref.at[pl.ds(pl.multiple_of(at, 16), n), pl.ds(h * feat, feat)]),
                    (blocks[j].at[1], wo_ref.at[pl.ds(pl.multiple_of(at + h * feat, 16), n)]),
                ):
                    copies.append(pltpu.make_async_copy(src, dst, sems.at[len(copies)]))
        start_all(copies)
        x1 = add_both(x_ref[...] + part_ref[...], got_ref[...], rows)
        x1_ref[...] = x1
        normed_ref[...] = layer_norm(x1, gains_ref[pl.ds(1, 1), :])
        wait_all(copies)
        out_ref[...] = jnp.zeros_like(out_ref)

        @pl.loop(0, wide // tile)
        def _(t):
            at = pl.ds(pl.multiple_of(t * tile, 128), tile)
            h = dot(normed_ref[...], wi_ref[:, at])
            hidden_ref[:, at] = h
            out_ref[...] += dot(gelu_both(h)[0].astype(BF), wo_ref[at, :])

        low_ref[...] = out_ref[...].astype(BF)

    return call(
        kernel,
        [
            ((r2, feat), F32, VM), ((r2, feat), BF, VM), ((r2, wide), F32, VM), ((r2, feat), F32, VM),
            ((r2, feat), BF, VM), ((feat, wide), BF, VM), ((wide, feat), BF, VM),
        ],
        [(where, SM), (x, VM), (part, VM), (got, VM), (gains, VM)] + [(t, HB) for t in (*a, *b)],
        scratch=[pltpu.SemaphoreType.DMA((16,))],
        after=after,
        flops=4 * r2 * feat * wide,
        bytes_accessed=16 * 2**20,
    )


def spread_out(e, firsts, pieces, sems):
    copies = []
    for src, n, h, place in pieces:
        first = firsts[h]
        for side, js in enumerate(((0, 3 - first), (first, 3))):
            for i, j in enumerate(js):
                at = pl.ds(pl.multiple_of((e ^ j) * n, 16), n)
                copies.append(
                    pltpu.make_async_copy(src(at), place(side, i), sems.at[len(copies)])
                )
    return copies


def widen_back(where, u, x, gains, part, got, normed, hidden, wi, wo, firsts, rows, after=()):
    r2, feat = u.shape
    wide = 2 * feat
    tile = 384
    n = feat // 4

    def kernel(
        where_ref, u_ref, x_ref, gains_ref, part_ref, got_ref, normed_ref, hidden_ref, wi_ref, wo_ref,
        u2_ref, gs_ref, out_ref, low_ref, keep_a, send_a, keep_b, send_b,
        ulow_ref, turned_ref, wis_ref, wos_ref, sems,
    ):
        slope = add_both(part_ref[...], got_ref[...], rows)
        dx, gain_slope = norm_back(x_ref[...], gains_ref[pl.ds(2, 1), :], slope, rows)
        gs_ref[...] = gain_slope
        u2 = u_ref[...] + dx
        u2_ref[...] = u2
        ulow_ref[...] = u2.astype(BF)
        turned_ref[...] = normed_ref[...].T
        out_ref[...] = jnp.zeros_like(out_ref)

        @pl.loop(0, wide // tile)
        def _(t):
            at = pl.ds(pl.multiple_of(t * tile, 128), tile)
            ulow = ulow_ref[...]
            act, dact = gelu_both(hidden_ref[:, at])
            hs = (dact * dot_t(ulow, wo_ref[at, :])).astype(BF)
            wos_ref[at, :] = t_dot(act.astype(BF), ulow).astype(BF)
            wis_ref[:, at] = dot(turned_ref[...], hs).astype(BF)
            out_ref[...] += dot_t(hs, wi_ref[:, at])

        outs = ((keep_a, send_a), (keep_b, send_b))
        pieces = []
        for h in range(2):
            pieces.append((
                lambda at, h=h: wis_ref.at[at, pl.ds(h * feat, feat)], n, h,
                lambda side, i, h=h: outs[h][side].at[i, 0],
            ))
            pieces.append((
                lambda at, h=h: wos_ref.at[pl.ds(h * feat, feat)].at[at], n, h,
                lambda side, i, h=h: outs[h][side].at[i, 1],
            ))
        copies = spread_out(where_ref[1], firsts, pieces, sems)
        start_all(copies)
        low_ref[...] = out_ref[...].astype(BF)
        wait_all(copies)

    block = ((2, 2, n, feat), BF, HB)
    return call(
        kernel,
        [((r2, feat), F32, VM), ((1, feat), F32, VM), ((r2, feat), F32, VM), ((r2, feat), BF, VM)]
        + [block] * 4,
        [
            (where, SM), (u, VM), (x, VM), (gains, VM), (part, VM), (got, VM), (normed, VM),
            (hidden, VM), (wi, VM), (wo, VM),
        ],
        scratch=[
            pltpu.VMEM((r2, feat), BF), pltpu.VMEM((feat, r2), BF), pltpu.VMEM((feat, wide), BF),
            pltpu.VMEM((wide, feat), BF), pltpu.SemaphoreType.DMA((16,)),
        ],
        after=after,
        flops=10 * r2 * feat * wide,
        bytes_accessed=24 * 2**20,
    )


def attend_proj_back(where, dq, own, got, normed, w, wps, firsts, rows, last, after=()):
    r2, feat = normed.shape
    half = feat // 2
    n, m = feat // 4, half // 4
    tile = 384

    def kernel(
        where_ref, dq_ref, own_ref, got_ref, normed_ref, w_ref, wps_ref,
        out_ref, low_ref, keep_a, send_a, keep_b, send_b, packed_ref, turned_ref, ws_ref, sems,
    ):
        packed_ref[:, :half] = dq_ref[...]
        packed_ref[:, half:] = (own_ref[...] + got_ref[...].astype(F32)).astype(BF)
        out = dot_t(packed_ref[...], w_ref[...])
        out_ref[...] = out[: out_ref.shape[0]]
        low_ref[...] = (out[rows:] if last else out).astype(BF)
        turned_ref[...] = normed_ref[...].T

        @pl.loop(0, 3 * half // tile)
        def _(t):
            at = pl.ds(pl.multiple_of(t * tile, 128), tile)
            ws_ref[:, at] = dot(turned_ref[...], packed_ref[:, at]).astype(BF)

        ab = ((keep_a, send_a), (keep_b, send_b))
        pieces = [
            (lambda at: ws_ref.at[at, pl.ds(0, feat)], n, 0, lambda side, i: ab[0][side].at[i]),
            (
                lambda at: ws_ref.at[at, pl.ds(feat, half)], n, 1,
                lambda side, i: ab[1][side].at[i, pl.ds(0, n)],
            ),
        ]
        for c in range(2):
            pieces.append((
                lambda at, c=c: wps_ref.at[at, pl.ds(c * half, half)], m, 1,
                lambda side, i, c=c: ab[1][side].at[i, pl.ds(n + c * m, m)],
            ))
        copies = spread_out(where_ref[1], firsts, pieces, sems)
        start_all(copies)
        wait_all(copies)

    n_out = rows if last else r2
    return call(
        kernel,
        [((n_out, feat), F32, VM), ((n_out, feat), BF, VM)]
        + [((2, n, feat), BF, HB)] * 2 + [((2, n + 2 * m, half), BF, HB)] * 2,
        [(where, SM), (dq, VM), (own, VM), (got, VM), (normed, VM), (w, VM), (wps, VM)],
        scratch=[
            pltpu.VMEM((r2, 3 * half), BF), pltpu.VMEM((feat, r2), BF), pltpu.VMEM((feat, 3 * half), BF),
            pltpu.SemaphoreType.DMA((16,)),
        ],
        after=after,
        flops=4 * r2 * feat * 3 * half,
        bytes_accessed=10 * 2**20,
    )


def join_upstream(u_own, u_sib, rows):
    feat = u_own.shape[1]

    def kernel(o_ref, s_ref, u_ref, low_ref):
        u_ref[pl.ds(0, rows), :] = o_ref[...]
        u_ref[pl.ds(rows, rows), :] = s_ref[...].astype(F32)
        low_ref[pl.ds(0, rows), :] = o_ref[...].astype(BF)
        low_ref[pl.ds(rows, rows), :] = s_ref[...]

    return call(
        kernel, [((2 * rows, feat), F32, VM), ((2 * rows, feat), BF, VM)], [(u_own, VM), (u_sib, VM)],
        bytes_accessed=2**21,
    )


def norm_step(u, x, gains, gain_row, part, got, rows, last, after=()):
    feat = x.shape[1]
    n = rows if last else 2 * rows

    def kernel(u_ref, x_ref, gains_ref, part_ref, got_ref, u2_ref, low_ref, gs_ref):
        if last:
            slope = part_ref[...] + got_ref[...].astype(F32)
        else:
            slope = add_both(part_ref[...], got_ref[...], rows)
        dx, gain_slope = norm_back(x_ref[:n], gains_ref[pl.ds(gain_row, 1), :], slope, rows)
        gs_ref[...] = gain_slope
        u2 = u_ref[:n] + dx
        u2_ref[...] = u2[: u2_ref.shape[0]]
        if not last:
            low_ref[...] = u2.astype(BF)

    n_out = last if last else n
    return call(
        kernel,
        [((n_out, feat), F32, VM), ((n if not last else 16, feat), BF, VM), ((1, feat), F32, VM)],
        [(u, VM), (x, VM), (gains, VM), (part, VM), (got, VM)],
        after=after,
        bytes_accessed=6 * 2**20,
    )


def picks(index, turn, cap, cap_rows, experts):
    at = lax.broadcasted_iota(jnp.int32, (1, experts * cap_rows), 1)
    out = []
    for k in range(TOP):
        chosen, slot = index[:, k : k + 1], index[:, TOP + k : TOP + k + 1]
        place = chosen if turn is None else chosen ^ turn
        target = jnp.where(slot < cap, place * cap_rows + slot, -1)
        out.append(jnp.where(at == target, 1.0, 0.0).astype(BF))
    return out


def lane_at(index, k):
    lane = lax.broadcasted_iota(jnp.int32, (1, 128), 1)
    return jnp.where(lane == index[:, k : k + 1] + 4, 1.0, 0.0)


def present_mask(blk, rows, blk_len, longest):
    pos = lax.broadcasted_iota(jnp.int32, (rows, 1), 0)
    last = jnp.where(blk < longest, blk_len, blk_len - 1)
    return jnp.where(pos < last, 1.0, 0.0)


def route(where, x, part, got, gains, small, cot, index, experts, cap, rows, blk_len, longest, fast, after=()):
    feat = x.shape[1]
    cap_rows = up16(cap)

    def kernel(where_ref, x_ref, part_ref, got_ref, gains_ref, small_ref, cot_ref, index_ref,
               x3_ref, moe_ref, gates_ref, up_ref, *blocks):
        x3 = x_ref[:rows] + part_ref[:rows] + got_ref[...].astype(F32)
        x3_ref[...] = x3
        moe = layer_norm(x3, gains_ref[pl.ds(3, 1), :])
        moe_ref[...] = moe
        lane = lax.broadcasted_iota(jnp.int32, (1, 128), 1)
        logits = dot(moe, small_ref[...])
        logits = jnp.where((lane >= 4) & (lane < 4 + experts), logits, -1e30)
        ex = jnp.exp(logits - jnp.max(logits, -1, keepdims=True))
        gates = ex / jnp.sum(ex, -1, keepdims=True)
        gates_ref[...] = gates
        up_ref[...] = jnp.zeros_like(up_ref)
        up_ref[pl.ds(0, blk_len), :] = cot_ref[...]
        up = up_ref[...] * present_mask(where_ref[0], rows, blk_len, longest)
        up_ref[...] = up
        index = index_ref[...]
        pick = picks(index, where_ref[1] if fast else None, cap, cap_rows, experts)
        sent = t_dot(pick[0] + pick[1], moe).astype(BF)
        slope = 0.0
        for k in range(TOP):
            gate = jnp.sum(gates * lane_at(index, k), -1, keepdims=True)
            slope += t_dot(pick[k], (gate * up).astype(BF))
        slope = slope.astype(BF)
        for j, ref in enumerate(blocks):
            ref[pl.ds(0, cap_rows), :] = sent[j * cap_rows : (j + 1) * cap_rows]
            ref[pl.ds(cap_rows, cap_rows), :] = slope[j * cap_rows : (j + 1) * cap_rows]

    return call(
        kernel,
        [((rows, feat), F32, VM), ((rows, feat), BF, VM), ((rows, 128), F32, VM), ((rows, feat), F32, VM)]
        + [((2 * cap_rows, feat), BF, VM)] * experts,
        [(where, SM), (x, VM), (part, VM), (got, VM), (gains, VM), (small, VM), (cot, VM), (index, VM)],
        after=after,
        flops=6 * rows * experts * cap_rows * feat,
        bytes_accessed=5 * 2**20,
    )


def expert_half(blocks, w_in, w_out, acc, cap_rows, after=()):
    feat = w_in.shape[0]
    wide = w_in.shape[1]
    tile = 512 if wide % 512 == 0 else wide
    n = len(blocks) * cap_rows
    steps = wide // tile
    final = acc is not None

    def kernel(*refs):
        refs = list(refs)
        take = lambda k: [refs.pop(0) for _ in range(k)]
        ins = take(len(blocks))
        wi_ref, wo_ref = take(2)
        before = take(2) if final else None
        take(len(after))
        outs = take(len(blocks)) if final else take(2)
        wis_ref, wos_ref = take(2)
        rows_ref, slope_ref, turned_ref, res_ref, back_ref = take(5)
        t = pl.program_id(0)

        @pl.when(t == 0)
        def _():
            for j, ref in enumerate(ins):
                at = pl.ds(j * cap_rows, cap_rows)
                rows_ref[at, :] = ref[pl.ds(0, cap_rows), :]
                slope_ref[at, :] = ref[pl.ds(cap_rows, cap_rows), :]
            turned_ref[...] = rows_ref[...].T
            if final:
                res_ref[...] = before[0][...]
                back_ref[...] = before[1][...]
            else:
                res_ref[...] = jnp.zeros_like(res_ref)
                back_ref[...] = jnp.zeros_like(back_ref)

        act, dact = gelu_both(dot(rows_ref[...], wi_ref[...]))
        act = act.astype(BF)
        hs = (dact * dot_t(slope_ref[...], wo_ref[...])).astype(BF)
        res_ref[...] += dot(act, wo_ref[...])
        back_ref[...] += dot_t(hs, wi_ref[...])
        wis_ref[...] = dot(turned_ref[...], hs).astype(BF)
        wos_ref[...] = t_dot(act, slope_ref[...]).astype(BF)

        @pl.when(t == steps - 1)
        def _():
            if final:
                for j, ref in enumerate(outs):
                    at = pl.ds(j * cap_rows, cap_rows)
                    ref[pl.ds(0, cap_rows), :] = res_ref[at, :].astype(BF)
                    ref[pl.ds(cap_rows, cap_rows), :] = back_ref[at, :].astype(BF)
            else:
                outs[0][...] = res_ref[...]
                outs[1][...] = back_ref[...]

    whole = lambda shape: pl.BlockSpec(shape, lambda t: (0,) * len(shape))
    wi_spec = pl.BlockSpec((feat, tile), lambda t: (0, t))
    wo_spec = pl.BlockSpec((tile, feat), lambda t: (t, 0))
    blk = (2 * cap_rows, feat)
    ins = [*blocks, w_in, w_out] + (list(acc) if final else []) + list(after)
    in_specs = [whole(blk)] * len(blocks) + [wi_spec, wo_spec] + [whole((n, feat))] * (2 if final else 0)
    in_specs += [HB] * len(after)
    if final:
        shapes, specs = [jax.ShapeDtypeStruct(blk, BF)] * len(blocks), [whole(blk)] * len(blocks)
    else:
        shapes, specs = [jax.ShapeDtypeStruct((n, feat), F32)] * 2, [whole((n, feat))] * 2
    shapes = shapes + [jax.ShapeDtypeStruct((feat, wide), BF), jax.ShapeDtypeStruct((wide, feat), BF)]
    return pl.pallas_call(
        kernel,
        grid=(steps,),
        out_shape=shapes,
        in_specs=in_specs,
        out_specs=specs + [wi_spec, wo_spec],
        scratch_shapes=[
            pltpu.VMEM((n, feat), BF), pltpu.VMEM((n, feat), BF), pltpu.VMEM((feat, n), BF),
            pltpu.VMEM((n, feat), F32), pltpu.VMEM((n, feat), F32),
        ],
        compiler_params=pltpu.CompilerParams(
            vmem_limit_bytes=50 * 2**20, dimension_semantics=("arbitrary",)
        ),
        cost_estimate=pl.CostEstimate(
            flops=12 * n * feat * wide, bytes_accessed=16 * 2**20, transcendentals=0
        ),
    )(*ins)


def combine(where, blocks, x3, moe, gates, up, index, small, gains, small_rows, experts, cap, rows, blk_len, longest, fast, after=()):
    feat = x3.shape[1]
    cap_rows = up16(cap)
    n = experts * cap_rows

    def kernel(where_ref, *refs):
        refs = list(refs)
        take = lambda k: [refs.pop(0) for _ in range(k)]
        ins = take(experts)
        x3_ref, moe_ref, gates_ref, up_ref, index_ref, small_ref, gains_ref = take(7)
        acts_ref, u_ref, low_ref, slopes_ref, result_ref, back_ref = take(6)
        for j, ref in enumerate(ins):
            at = pl.ds(j * cap_rows, cap_rows)
            result_ref[at, :] = ref[pl.ds(0, cap_rows), :]
            back_ref[at, :] = ref[pl.ds(cap_rows, cap_rows), :]
        index, gates, up, moe = index_ref[...], gates_ref[...], up_ref[...], moe_ref[...]
        pick = picks(index, where_ref[1] if fast else None, cap, cap_rows, experts)
        x3 = x3_ref[...]
        acts, all_slope = x3, 0.0
        for k in range(TOP):
            at_k = lane_at(index, k)
            gate = jnp.sum(gates * at_k, -1, keepdims=True)
            picked = dot(pick[k], result_ref[...])
            acts = acts + gate * picked
            all_slope += jnp.sum(up * picked, -1, keepdims=True) * at_k
        acts = acts * present_mask(where_ref[0], rows, blk_len, longest)
        acts_ref[...] = acts[:blk_len]
        logit = (gates * (all_slope - jnp.sum(gates * all_slope, -1, keepdims=True))).astype(BF)
        slope = dot(pick[0] + pick[1], back_ref[...]) + dot_t(logit, small_ref[...])
        dx, gain_slope = norm_back(x3, gains_ref[pl.ds(3, 1), :], slope, rows)
        u = up + dx
        u_ref[...] = u
        low_ref[...] = u.astype(BF)
        slopes_ref[...] = t_dot(logit, moe)[:small_rows]
        slopes_ref[pl.ds(3, 1), :] = gain_slope

    return call(
        kernel,
        [((blk_len, feat), F32, VM), ((rows, feat), F32, VM), ((rows, feat), BF, VM), ((small_rows, feat), F32, VM)],
        [(where, SM)] + [(b, VM) for b in blocks]
        + [(t, VM) for t in (x3, moe, gates, up, index, small, gains)],
        scratch=[pltpu.VMEM((n, feat), BF), pltpu.VMEM((n, feat), BF)],
        after=after,
        flops=6 * rows * n * feat,
        bytes_accessed=5 * 2**20,
    )


class Links:
    def __init__(self, mesh):
        self.E = mesh.shape["expert"]
        self.C = mesh.shape["context"]
        self.D = mesh.shape["dp"]
        assert self.C == 4 and self.D == 2 and self.E % 2 == 0
        self.fast = self.E == 4
        self.chips = self.E * self.C
        flat = lambda e, c, d: (e * self.C + c) * self.D + d
        self.team = [
            (flat(e, c, d), flat((e // 2) * 2 + c // 2, 2 * (e % 2) + d, c % 2))
            for e in range(self.E)
            for c in range(self.C)
            for d in range(self.D)
        ]
        self.to_lane = [(f, (f % self.chips) * 2 + f // self.chips) for f in range(2 * self.chips)]
        self.from_lane = [(b, a) for a, b in self.to_lane]

    def move(self, x):
        return lax.ppermute(x, ALL, self.team)

    def xor(self, x, axis, j):
        n = {"expert": self.E, "context": self.C, "dp": self.D}[axis]
        return lax.ppermute(x, axis, [(i, i ^ j) for i in range(n)])

    def sib(self, x):
        return self.xor(x, "dp", 1)

    def partner(self, x):
        return self.xor(x, "expert", 1)

    def column(self, x):
        c = lax.axis_index("context")
        got = self.xor(x, "context", 1)
        x = jnp.where(c & 1 == 1, jnp.stack([got, x]), jnp.stack([x, got]))
        got = self.xor(x, "context", 2)
        return jnp.where(c & 2 == 2, jnp.concatenate([got, x]), jnp.concatenate([x, got]))

    def plane(self, x, first):
        got = self.xor(x, "expert", first)
        return x, got, self.xor(jnp.stack([x, got]), "expert", 3 - first)

    def plane_sum(self, keep, send, first):
        got = self.xor(send, "expert", first).astype(F32)
        far = self.xor((keep[1].astype(F32) + got[1]).astype(BF), "expert", 3 - first)
        return keep[0].astype(F32) + got[0] + far.astype(F32)

    def column_sum(self, x):
        c = lax.axis_index("context")
        low, high = x[:2], x[2:]
        give = jnp.where(c & 2 == 2, low, high).astype(BF)
        x = jnp.where(c & 2 == 2, high, low) + self.xor(give, "context", 2).astype(F32)
        give = jnp.where(c & 1 == 1, x[0], x[1]).astype(BF)
        return jnp.where(c & 1 == 1, x[1], x[0]) + self.xor(give, "context", 1).astype(F32)

    def total(self, x):
        if not self.fast:
            return lax.psum(x, ALL)
        x = x + self.xor(x, "dp", 1)
        x = x + self.xor(x, "expert", 1)
        x = x + self.xor(x, "expert", 2)
        x = x + self.xor(x, "context", 1)
        return x + self.xor(x, "context", 2)

    def swap_blocks(self, x):
        if not self.fast:
            return list(lax.all_to_all(jnp.stack(x), "expert", 0, 0, tiled=True))
        return [x[0]] + [self.xor(x[j], "expert", j) for j in range(1, 4)]


def lane_rows(links, mine, d):
    keep = lax.dynamic_index_in_dim(mine, d, 0, False)
    got = links.sib(lax.dynamic_index_in_dim(mine, 1 - d, 0, False))
    return jnp.where(d == 0, jnp.concatenate([keep, got], 0), jnp.concatenate([got, keep], 0))


def in_order(d, own, other):
    return jnp.where(d == 0, jnp.stack([own, other]), jnp.stack([other, own]))


class Weights:
    def __init__(self, links, rdev, feat, ff):
        self.links, self.rdev, self.feat, self.ff = links, rdev, feat, ff
        self.d = lax.axis_index("dp")
        self.half = feat // 2
        self.firsts = (1, 2)

    def split_attend(self, w):
        w = w.reshape(self.rdev, 3, 2, self.half).transpose(2, 0, 1, 3)
        return w.reshape(2, self.rdev, 3 * self.half)

    def split_widen(self, w):
        w = w.reshape(self.rdev, self.links.chips, 2, 2, -1).transpose(2, 0, 3, 1, 4)
        return w.reshape(2, self.rdev, self.ff // 2)

    def pack_attend(self, w, p, small):
        parts = [w, jnp.concatenate([p[:, : self.half], p[:, self.half :]], 0)]
        if small is not None:
            parts.append(jnp.pad(small, ((0, 0), (0, 128 - small.shape[1]))))
        return jnp.concatenate(parts, 1)

    def pack_wide(self, wout):
        h = wout.shape[0] // 2
        return jnp.concatenate([wout[:h], wout[h:]], 1)

    def column(self, buf):
        if self.links.fast:
            return self.links.column(buf)
        return lax.all_gather(buf, CHIPS, axis=0, tiled=False)

    def plane(self, x, lane):
        first = self.firsts[lane]
        if self.links.fast:
            return self.links.plane(x, first)
        return x[0], x[first], jnp.stack([x[3 - first], x[3]])

    def cut(self, x):
        return x if self.links.fast else x.reshape(4, -1, x.shape[-1])

    def spread_attend(self, quad):
        f, h, r = self.feat, self.half, self.rdev
        n = quad.shape[0]
        p = quad[..., f + h : 2 * f].reshape(n, 2, r, h)
        v = quad[..., f : f + h]
        parts = [self.cut(t.reshape(-1, h)) for t in (v, p[:, 0], p[:, 1])]
        if quad.shape[2] > 2 * f:
            small = self.cut(quad[..., 2 * f :].reshape(-1, 128))
            small = small.reshape(small.shape[:-2] + (3, -1, 128))
            parts.append(jnp.concatenate([small[..., g, :, :] for g in range(3)], -1))
        a = self.plane(self.cut(quad[..., :f].reshape(-1, f)), 0)
        return a, self.plane(jnp.concatenate(parts, -2), 1)

    def spread_wide(self, quad_in, quad_out):
        out = []
        for i in range(2):
            pair = [self.cut(t[..., i * self.feat : (i + 1) * self.feat].reshape(-1, self.feat)) for t in (quad_in, quad_out)]
            out.append(self.plane(jnp.stack(pair, -3), i))
        return out

    def total(self, keep, send, lane):
        first = self.firsts[lane]
        if self.links.fast:
            return self.links.plane_sum(keep, send, first)
        blk = {0: keep[0], 3 - first: keep[1], first: send[0], 3: send[1]}
        return jnp.stack([blk[j] for j in range(4)])

    def column_sum(self, buf):
        if self.links.fast:
            return self.links.column_sum(buf)
        return lax.psum_scatter(buf.astype(BF), CHIPS, scatter_dimension=0, tiled=False).astype(F32)

    def exchange(self, w):
        w = w.reshape(2, self.rdev, -1)
        mine = lax.dynamic_index_in_dim(w, self.d, 0, False)
        got = self.links.sib(lax.dynamic_index_in_dim(w, 1 - self.d, 0, False))
        return in_order(self.d, mine, got)

    def owner_attend(self, keep_a, send_a, keep_b, send_b):
        f, h, r = self.feat, self.half, self.rdev
        a = self.total(keep_a, send_a, 0)
        b = self.total(keep_b, send_b, 1)
        n, m = f // 4, h // 4
        cut = lambda t, k: t.reshape(-1, k * r, t.shape[-1])
        p = [cut(b[..., n + i * m : n + (i + 1) * m, :], 1) for i in range(2)]
        buf = jnp.concatenate(
            [cut(a, 2), cut(b[..., :n, :], 2), jnp.concatenate(p, 1)], 2
        )
        buf = self.column_sum(buf)
        p = jnp.concatenate([buf[:r, f + h :], buf[r:, f + h :]], 1)
        p = lax.ppermute(p, ALL, self.links.from_lane)
        w = self.exchange(buf[:, : f + h])
        return w.reshape(2, r, 3, h).transpose(1, 2, 0, 3).reshape(r, 3 * f), p

    def owner_wide(self, keep_a, send_a, keep_b, send_b):
        f, r = self.feat, self.rdev
        a, b = self.total(keep_a, send_a, 0), self.total(keep_b, send_b, 1)
        hid = self.ff // (4 * self.links.chips)
        ins = [t[..., 0, :, :].reshape(-1, 2 * r, f) for t in (a, b)]
        outs = [t[..., 1, :, :].reshape(-1, hid, f) for t in (a, b)]
        if hid == 2 * r:
            buf = self.column_sum(jnp.concatenate(ins + outs, 2))
            ins, outs = buf[:, : 2 * f], buf[:, 2 * f :]
        else:
            ins, outs = [self.column_sum(jnp.concatenate(t, 2)) for t in (ins, outs)]
        w = self.exchange(ins).reshape(2, r, 2, self.links.chips, -1)
        w = w.transpose(1, 3, 0, 2, 4).reshape(r, self.ff)
        return w, jnp.concatenate([outs[:, :f], outs[:, f:]], 0)


def tie(x, *after):
    return lax.optimization_barrier((x, *after))[0]


def body(links, *args):
    (tokens, cotangent, g1, w1, p1, g2, win, wout, g3, w3, p3, g4, router, ein, eout, routes, slots) = args
    e = lax.axis_index("expert")
    d = lax.axis_index("dp")
    blk_len, feat = tokens.shape[1:]
    rows = up16(blk_len)
    half = feat // 2
    rdev = w1.shape[0]
    ff = win.shape[1]
    longest = LEN - (blk_len - 1) * links.C
    experts = router.shape[1]
    small_rows = (4 + experts + 7) // 8 * 8
    cap = max(2, (5 * TOP * blk_len + 4 * experts - 1) // (4 * experts))
    blk = 2 * (e % 2) + d
    where = jnp.stack([blk, e if links.fast else 0 * e]).astype(jnp.int32)
    wt = Weights(links, rdev, feat, ff)
    firsts = wt.firsts
    img = dict(rows=rows, blk_len=blk_len, longest=longest)

    small = jnp.concatenate([g1[:, None], g2[:, None], g3[:, None], g4[:, None], router], 1)
    gsm = small.shape[1]
    lane1 = jnp.concatenate(
        [wt.split_attend(w1), jnp.broadcast_to(small[None], (2, rdev, gsm))], 2
    )
    lane1 = lane_rows(links, lane1, d)
    ps = lax.ppermute(jnp.concatenate([p1, p3], 0), ALL, links.to_lane)
    tok = links.move(tokens[0])
    tok_sib = links.sib(tok)
    quad1 = wt.column(wt.pack_attend(lane1[:, : 3 * half], ps[:rdev], lane1[:, 3 * half :]))
    blocks1 = wt.spread_attend(quad1)

    later = jnp.concatenate([wt.split_widen(win), wt.split_attend(w3)], 2)
    later = lane_rows(links, later, d)
    w_in, w_out = later[:, : ff // 2], wt.pack_wide(wout)
    buf3 = wt.pack_attend(later[:, ff // 2 :], ps[rdev:], None)
    if w_in.shape == w_out.shape:
        quad = wt.column(tie(jnp.concatenate([w_in, w_out, buf3], 1), quad1))
        quad2, quad3 = (quad[..., : ff // 2], quad[..., ff // 2 : ff]), quad[..., ff:]
    else:
        quad2, quad3 = (wt.column(w_in), wt.column(w_out)), wt.column(buf3)
    blocks2 = wt.spread_wide(*quad2)
    blocks3 = wt.spread_attend(quad3)

    ein_own, eout_own = ein[0], eout[0]
    ein_sib, eout_sib = links.sib(ein_own), links.sib(eout_own)
    cot = links.move(cotangent[0])
    index = links.move(jnp.concatenate([routes[0], slots[0]], 1))
    index = jnp.pad(index, ((0, rows - blk_len), (0, 0)), constant_values=cap)

    x0, normed1, q1, kv1, wa1, wp1, small, gains = attend_first(
        where, tok, tok_sib, small_rows, *blocks1, firsts, rows
    )
    far1 = links.partner(kv1)
    part, low, blend1, lse1 = attend_core(where, q1, kv1, far1, wp1, solo=False, **img)
    x1, normed2, hidden, part2, low2, wi, wo = widen_forward(
        where, x0, part, links.sib(low), gains, *blocks2, firsts, rows
    )
    x2, normed3, q3, kv3, wa3, wp3 = attend_next(
        where, x1, part2, links.sib(low2), gains, 2, *blocks3, firsts, rows
    )
    far3 = links.partner(kv3)
    part3, low3, blend3, lse3 = attend_core(where, q3, kv3, far3, wp3, solo=True, **img)
    moe_args = dict(experts=experts, cap=cap, fast=links.fast, **img)
    x3, moe, gates, up, *sent = route(
        where, x2, part3, links.sib(low3), gains, small, cot, index, **moe_args
    )
    came = links.swap_blocks(sent)
    res, back, eis_sib, eos_sib = expert_half(came, ein_sib, eout_sib, None, up16(cap))
    *answer, eis, eos = expert_half(came, ein_own, eout_own, (res, back), up16(cap))
    answer = links.swap_blocks(answer)
    acts, u, u_low, small_slopes = combine(
        where, answer, x3, moe, gates, up, index, small, gains, small_rows, **moe_args
    )
    e_sums = [
        lax.psum((a.astype(F32) + links.sib(b).astype(F32)).astype(BF), "context").astype(F32)
        for a, b in ((eis, eis_sib), (eos, eos_sib))
    ]
    acts = links.move(acts)

    u, u_low = join_upstream(u, links.sib(u_low), rows)
    dq, own, far, wps = attend_core_back(where, u_low, wp3, blend3, q3, kv3, far3, lse3, **img)
    part, low, *slopes3 = attend_proj_back(
        where, dq, own, links.partner(far), normed3, wa3, wps, firsts, rows, False
    )
    u, g3_slope, part, low, *slopes2 = widen_back(
        where, u, x2, gains, part, links.sib(low), normed2, hidden, wi, wo, firsts, rows
    )
    w3_out, p3_out = wt.owner_attend(*slopes3)
    u, u_low, g2_slope = norm_step(u, x1, gains, 1, part, links.sib(low), rows, 0)
    win_out, wout_out = wt.owner_wide(*slopes2)
    dq, own, far, wps = attend_core_back(where, u_low, wp1, blend1, q1, kv1, far1, lse1, **img)
    part, low, *slopes1 = attend_proj_back(
        where, dq, own, links.partner(far), normed1, wa1, wps, firsts, rows, True
    )
    w1_out, p1_out = wt.owner_attend(*slopes1)
    u, _, g1_slope = norm_step(u, x0, gains, 0, part, links.sib(low), rows, blk_len)
    token_slope = links.move(u)

    small = jnp.concatenate([g1_slope, g2_slope, g3_slope, small_slopes[3:]], 0)
    small = links.total(small)
    flat = (e * links.C + lax.axis_index("context")) * 2 + d
    small = small.reshape(-1, 2 * links.chips, rdev)
    small = lax.dynamic_index_in_dim(small, flat, 1, False)
    return (
        acts[None], token_slope[None], small[0], w1_out, p1_out, small[1], win_out, wout_out,
        small[2], w3_out, p3_out, small[3], small[4 : 4 + experts].T, e_sums[0][None], e_sums[1][None],
    )


def solution(mesh):
    links = Links(mesh)
    tok = P(("expert", "dp"), "context", None)
    vec, mat = P(ALL), P(ALL, None)
    ein, eout = P("expert", None, "dp"), P("expert", "dp", None)
    dense = (vec, mat, mat, vec, mat, mat, vec, mat, mat, vec, mat, ein, eout)
    return jax.shard_map(
        functools.partial(body, links),
        mesh=mesh,
        in_specs=(tok, tok) + dense + (tok, tok),
        out_specs=(tok, tok) + dense,
        check_vma=False,
    )
```

```python
import functools

import jax
import jax.numpy as jnp
from jax import lax
from jax.experimental import pallas as pl
from jax.experimental.pallas import tpu as pltpu
from jax.sharding import PartitionSpec as P

HEADS = 12
HEAD_DIM = 64
LEN = 577
TOP = 2
ALL = ("expert", "context", "dp")
CHIPS = ("expert", "context")
BF = jnp.bfloat16
F32 = jnp.float32
VM = pl.BlockSpec(memory_space=pltpu.VMEM)
HB = pl.BlockSpec(memory_space=pl.ANY)
SM = pl.BlockSpec(memory_space=pltpu.SMEM)


def up16(n):
    return (n + 15) // 16 * 16


def dot(a, b):
    return jnp.dot(a, b, preferred_element_type=F32)


def dot_t(a, b):
    return lax.dot_general(a, b, (((1,), (1,)), ((), ())), preferred_element_type=F32)


def t_dot(a, b):
    return lax.dot_general(a, b, (((0,), (0,)), ((), ())), preferred_element_type=F32)


def call(kernel, outs, ins, scratch=(), after=(), flops=0, bytes_accessed=0):
    n_in, n_after = len(ins), len(after)

    def run(*refs):
        kernel(*refs[:n_in], *refs[n_in + n_after :])

    return pl.pallas_call(
        run,
        out_shape=[jax.ShapeDtypeStruct(s, t) for s, t, _ in outs],
        in_specs=[s for _, s in ins] + [HB] * n_after,
        out_specs=[s for _, _, s in outs],
        scratch_shapes=list(scratch),
        compiler_params=pltpu.CompilerParams(vmem_limit_bytes=50 * 2**20),
        cost_estimate=pl.CostEstimate(
            flops=flops, bytes_accessed=bytes_accessed, transcendentals=0
        ),
    )(*[a for a, _ in ins], *after)


def norm_parts(x):
    mean = jnp.mean(x, -1, keepdims=True)
    centre = x - mean
    scale = lax.rsqrt(jnp.mean(centre * centre, -1, keepdims=True) + 1e-06)
    return centre * scale, scale


def layer_norm(x, gain):
    return (norm_parts(x)[0] * gain).astype(BF)


def norm_back(x, gain, slope):
    unit, scale = norm_parts(x)
    terms = slope * unit
    inner = slope * gain
    inner = inner - jnp.mean(inner, -1, keepdims=True) - unit * jnp.mean(inner * unit, -1, keepdims=True)
    return inner * scale, terms


def gelu_both(h):
    k = 0.7978845608028654
    t = jnp.tanh(k * (h + 0.044715 * h * h * h))
    half = 0.5 * (1 + t)
    return h * half, half + 0.5 * h * (1 - t * t) * (k + (3 * 0.044715 * k) * h * h)


def add_both(mine, got, rows):
    return mine + jnp.concatenate([got[rows:], got[:rows]], 0).astype(F32)


def pair_masks():
    lane = lax.broadcasted_iota(jnp.int32, (1, 2 * HEAD_DIM), 1)
    return [(lane < HEAD_DIM).astype(BF), (lane >= HEAD_DIM).astype(BF)]


def key_mask(blk, rows, blk_len, longest):
    pos = lax.broadcasted_iota(jnp.int32, (rows, 1), 0)
    parts = []
    for j in range(4):
        last = jnp.where((blk ^ j) < longest, blk_len, blk_len - 1)
        parts.append(pos < last)
    return jnp.concatenate([jnp.where(p, 1.0, 0.0) for p in parts], 0) > 0.5


def attend_core(where, q, kv_own, kv_far, wp, rows, blk_len, longest, solo, far=None, after=()):
    half = q.shape[1]
    feat = wp.shape[1]
    pairs = half // (2 * HEAD_DIM)
    r2 = 2 * rows

    def kernel(where_ref, q_ref, ko_ref, *refs):
        refs = list(refs)
        take = lambda n: [refs.pop(0) for _ in range(n)]
        given = take(1 if far is None else 3)
        wp_ref, part_ref, low_ref, blend_ref, lse_ref = take(5)
        if far is None:
            kf_ref = given[0]
        else:
            (kf_ref,) = take(1)
            for j in range(2):
                kf_ref[pl.ds(j * rows, rows), :] = dot(given[j][...], given[2][:, half:]).astype(BF)
        ok = key_mask(where_ref[0], rows, blk_len, longest)
        masks = pair_masks()
        for p in range(pairs):
            at, vat = pl.ds(p * 128, 128), pl.ds(half + p * 128, 128)
            k = jnp.concatenate([ko_ref[:, at], kf_ref[:, at]], 0)
            v = jnp.concatenate([ko_ref[:, vat], kf_ref[:, vat]], 0)
            qp = q_ref[:, at]
            acc = None
            for h in range(2):
                s = dot_t(k, qp * masks[h]) * 0.125
                s = jnp.where(ok, s, -1e9)
                top = jnp.max(s, 0, keepdims=True)
                ex = jnp.exp(s - top)
                total = jnp.sum(ex, 0, keepdims=True)
                lse_ref[pl.ds(2 * p + h, 1), :] = top + jnp.log(total)
                shares = (ex * (1.0 / total)).astype(BF)
                out = t_dot(v * masks[h], shares)
                acc = out if acc is None else acc + out
            blend_ref[at, :] = acc.astype(BF)
        part = t_dot(blend_ref[...], wp_ref[...])
        part_ref[...] = part
        low_ref[...] = (part[rows:] if solo else part).astype(BF)

    outs = [
        ((r2, feat), F32, VM), ((rows if solo else r2, feat), BF, VM), ((half, r2), BF, VM), ((8, r2), F32, VM),
    ]
    ins = [(where, SM), (q, VM), (kv_own, VM)]
    if far is None:
        ins.append((kv_far, VM))
    else:
        ins += [(t, VM) for t in far]
        outs.append(((r2, feat), BF, VM))
    return call(
        kernel,
        outs,
        ins + [(wp, VM)],
        after=after,
        flops=2 * r2 * half * (8 * rows + feat),
        bytes_accessed=4 * 2**20,
    )


def attend_core_back(where, u_low, wp, blend, q, kv_own, kv_far, lse, rows, blk_len, longest, after=()):
    half = q.shape[1]
    feat = wp.shape[1]
    pairs = half // (2 * HEAD_DIM)
    r2 = 2 * rows

    def kernel(
        where_ref, u_ref, wp_ref, blend_ref, q_ref, ko_ref, kf_ref, lse_ref,
        dq_ref, own_ref, far_ref, wps_ref, bt_ref, dqt_ref,
    ):
        ok = key_mask(where_ref[0], rows, blk_len, longest)
        masks = pair_masks()
        sub = lax.broadcasted_iota(jnp.int32, (2 * HEAD_DIM, 1), 0)
        row_masks = [(sub < HEAD_DIM).astype(BF), (sub >= HEAD_DIM).astype(BF)]
        u = u_ref[...]
        bt_ref[...] = dot_t(wp_ref[...], u).astype(BF)
        for p in range(pairs):
            at, vat = pl.ds(p * 128, 128), pl.ds(half + p * 128, 128)
            k = jnp.concatenate([ko_ref[:, at], kf_ref[:, at]], 0)
            v = jnp.concatenate([ko_ref[:, vat], kf_ref[:, vat]], 0)
            qp = q_ref[:, at]
            bt = bt_ref[at, :]
            dqt = dk = dv = 0.0
            for h in range(2):
                qm = qp * masks[h]
                s = dot_t(k, qm) * 0.125
                shares = jnp.where(ok, jnp.exp(s - lse_ref[pl.ds(2 * p + h, 1), :]), 0.0)
                slope = dot(v * masks[h], bt)
                t = shares * slope
                ss = (t - shares * jnp.sum(t, 0, keepdims=True)).astype(BF)
                dqt += t_dot(k * masks[h], ss)
                dk += dot(ss, qm)
                dv += dot_t(shares.astype(BF), bt * row_masks[h])
            dqt_ref[at, :] = dqt * 0.125
            dk = dk * 0.125
            own_ref[:, at] = dk[:r2]
            own_ref[:, vat] = dv[:r2]
            far_ref[:, at] = dk[r2:].astype(BF)
            far_ref[:, vat] = dv[r2:].astype(BF)
        dq_ref[...] = dqt_ref[...].T.astype(BF)
        wps_ref[...] = dot(blend_ref[...], u).astype(BF)

    return call(
        kernel,
        [
            ((r2, half), BF, VM), ((r2, 2 * half), F32, VM), ((r2, 2 * half), BF, VM),
            ((half, feat), BF, VM),
        ],
        [
            (where, SM), (u_low, VM), (wp, VM), (blend, VM), (q, VM), (kv_own, VM), (kv_far, VM),
            (lse, VM),
        ],
        scratch=[pltpu.VMEM((half, r2), BF), pltpu.VMEM((half, r2), F32)],
        after=after,
        flops=2 * r2 * half * (20 * rows + 2 * feat),
        bytes_accessed=6 * 2**20,
    )


def start_all(copies):
    for c in copies:
        c.start()


def wait_all(copies):
    for c in copies:
        c.wait()


def attend_copies(e, refs, w_ref, p_ref, small_ref, sems):
    copies = []

    def add(src, dst):
        copies.append(pltpu.make_async_copy(src, dst, sems.at[len(copies)]))

    n = w_ref.shape[0] // 4
    half = p_ref.shape[0]
    m = half // 4
    for j in range(4):
        to = e ^ j
        rows, prows = pl.ds(pl.multiple_of(to * n, 16), n), pl.ds(pl.multiple_of(to * m, 16), m)
        a, b, at = (refs[j], refs[j], 2 * n) if j < 3 else (refs[3], refs[4], 0)
        for g in range(2):
            add(a.at[pl.ds(g * n, n)], w_ref.at[rows, pl.ds(g * half, half)])
        add(b.at[pl.ds(at, n)], w_ref.at[rows, pl.ds(2 * half, half)])
        add(b.at[pl.ds(at + n, m)], p_ref.at[prows, pl.ds(0, half)])
        add(b.at[pl.ds(at + n + m, m)], p_ref.at[prows, pl.ds(half, half)])
        if small_ref is not None:
            for g in range(3):
                srows = pl.ds(pl.multiple_of(to * n + g * (n // 3), 16), n // 3)
                add(b.at[pl.ds(at + n + 2 * m, n // 3), pl.ds(128 * g, 128)], small_ref.at[srows])
    return copies


def attend_first(where, tokens, small_rows, blocks, rows, after=()):
    blk_len, feat = tokens[0].shape
    half = feat // 2
    r2 = 2 * rows

    def kernel(where_ref, *refs):
        refs = list(refs)
        take = lambda n: [refs.pop(0) for _ in range(n)]
        tok, block_refs = take(4), take(5)
        x_ref, normed_ref, q_ref, kv_ref, far_ref, w_ref, p_ref, small_ref, rows_ref, all_ref, sems = take(11)
        copies = attend_copies(where_ref[1], block_refs, w_ref, p_ref, small_ref, sems)
        start_all(copies)
        all_ref[...] = jnp.zeros_like(all_ref)
        for j in range(4):
            all_ref[pl.ds(j * rows, blk_len), :] = tok[j][...].astype(F32)
        x = all_ref[...]
        x_ref[...] = x[:r2]
        unit = norm_parts(x)[0]
        wait_all(copies)
        turned = small_ref[...].astype(F32).T
        rows_ref[...] = turned[: rows_ref.shape[0]]
        normed = (unit * turned[0:1]).astype(BF)
        normed_ref[...] = normed[:r2]
        q_ref[...] = dot(normed[:r2], w_ref[:, :half]).astype(BF)
        kv = dot(normed, w_ref[:, half:]).astype(BF)
        kv_ref[...] = kv[:r2]
        far_ref[...] = kv[r2:]

    return call(
        kernel,
        [
            ((r2, feat), F32, VM), ((r2, feat), BF, VM), ((r2, half), BF, VM), ((r2, feat), BF, VM),
            ((r2, feat), BF, VM), ((feat, 3 * half), BF, VM), ((half, feat), BF, VM),
            ((feat, 128), BF, VM), ((small_rows, feat), F32, VM),
        ],
        [(where, SM)] + [(t, VM) for t in tokens] + [(t, HB) for t in blocks],
        scratch=[pltpu.VMEM((2 * r2, feat), F32), pltpu.SemaphoreType.DMA((32,))],
        after=after,
        flops=2 * r2 * feat * 5 * half,
        bytes_accessed=6 * 2**20,
    )


def norm_next(x, part, got, gains, gain_row, rows, after=()):
    r2, feat = x.shape

    def kernel(x_ref, part_ref, got_ref, gains_ref, x2_ref, normed_ref, own_ref):
        x2 = add_both(x_ref[...] + part_ref[...], got_ref[...], rows)
        x2_ref[...] = x2
        normed = layer_norm(x2, gains_ref[pl.ds(gain_row, 1), :])
        normed_ref[...] = normed
        own_ref[...] = normed[:rows]

    return call(
        kernel,
        [((r2, feat), F32, VM), ((r2, feat), BF, VM), ((rows, feat), BF, VM)],
        [(x, VM), (part, VM), (got, VM), (gains, VM)],
        after=after,
        bytes_accessed=5 * 2**20,
    )


def attend_next(where, normed, blocks, after=()):
    r2, feat = normed.shape
    half = feat // 2

    def kernel(where_ref, normed_ref, *refs):
        refs = list(refs)
        take = lambda n: [refs.pop(0) for _ in range(n)]
        block_refs = take(5)
        q_ref, kv_ref, w_ref, p_ref, sems = take(5)
        copies = attend_copies(where_ref[1], block_refs, w_ref, p_ref, None, sems)
        start_all(copies)
        wait_all(copies)
        normed = normed_ref[...]
        q_ref[...] = dot(normed, w_ref[:, :half]).astype(BF)
        kv_ref[...] = dot(normed, w_ref[:, half:]).astype(BF)

    return call(
        kernel,
        [
            ((r2, half), BF, VM), ((r2, feat), BF, VM), ((feat, 3 * half), BF, VM), ((half, feat), BF, VM),
        ],
        [(where, SM), (normed, VM)] + [(t, HB) for t in blocks],
        scratch=[pltpu.SemaphoreType.DMA((20,))],
        after=after,
        flops=2 * r2 * feat * 3 * half,
        bytes_accessed=5 * 2**20,
    )


def widen_forward(where, x, part, got, gains, blocks, rows, after=()):
    r2, feat = x.shape
    wide = 2 * feat
    tile = 384

    def kernel(
        where_ref, x_ref, part_ref, got_ref, gains_ref, z0, z1, z2, a3, b3,
        x1_ref, normed_ref, hidden_ref, out_ref, low_ref, wi_ref, wo_ref, sems,
    ):
        n = feat // 4
        copies = []
        for h, last in enumerate((a3, b3)):
            pairs = [z0.at[h], z1.at[h], z2.at[h], last]
            for j in range(4):
                at = (where_ref[1] ^ j) * n
                for src, dst in (
                    (pairs[j].at[0], wi_ref.at[pl.ds(pl.multiple_of(at, 16), n), pl.ds(h * feat, feat)]),
                    (pairs[j].at[1], wo_ref.at[pl.ds(pl.multiple_of(at + h * feat, 16), n)]),
                ):
                    copies.append(pltpu.make_async_copy(src, dst, sems.at[len(copies)]))
        start_all(copies)
        x1 = add_both(x_ref[...] + part_ref[...], got_ref[...], rows)
        x1_ref[...] = x1
        normed_ref[...] = layer_norm(x1, gains_ref[pl.ds(1, 1), :])
        wait_all(copies)
        out_ref[...] = jnp.zeros_like(out_ref)

        @pl.loop(0, wide // tile)
        def _(t):
            at = pl.ds(pl.multiple_of(t * tile, 128), tile)
            h = dot(normed_ref[...], wi_ref[:, at])
            hidden_ref[:, at] = h
            out_ref[...] += dot(gelu_both(h)[0].astype(BF), wo_ref[at, :])

        low_ref[...] = out_ref[...].astype(BF)

    return call(
        kernel,
        [
            ((r2, feat), F32, VM), ((r2, feat), BF, VM), ((r2, wide), F32, VM), ((r2, feat), F32, VM),
            ((r2, feat), BF, VM), ((feat, wide), BF, VM), ((wide, feat), BF, VM),
        ],
        [(where, SM), (x, VM), (part, VM), (got, VM), (gains, VM)] + [(t, HB) for t in blocks],
        scratch=[pltpu.SemaphoreType.DMA((16,))],
        after=after,
        flops=4 * r2 * feat * wide,
        bytes_accessed=16 * 2**20,
    )


def widen_back(where, u, x, gains, part, got, normed, hidden, wi, wo, first, rows, columns, after=()):
    r2, feat = u.shape
    wide = 2 * feat
    tile = 384
    n = feat // 4

    def kernel(
        where_ref, u_ref, x_ref, gains_ref, part_ref, got_ref, normed_ref, hidden_ref, wi_ref, wo_ref,
        u2_ref, out_ref, low_ref, *more,
    ):
        outs, (ulow_ref, turned_ref, wis_ref, wos_ref, sems) = more[:-5], more[-5:]
        slope = add_both(part_ref[...], got_ref[...], rows)
        u2 = u_ref[...] + norm_back(x_ref[...], gains_ref[pl.ds(2, 1), :], slope)[0]
        u2_ref[...] = u2
        ulow_ref[...] = u2.astype(BF)
        turned_ref[...] = normed_ref[...].T
        out_ref[...] = jnp.zeros_like(out_ref)

        @pl.loop(0, wide // tile)
        def _(t):
            at = pl.ds(pl.multiple_of(t * tile, 128), tile)
            ulow = ulow_ref[...]
            act, dact = gelu_both(hidden_ref[:, at])
            hs = (dact * dot_t(ulow, wo_ref[at, :])).astype(BF)
            wos_ref[at, :] = t_dot(act.astype(BF), ulow).astype(BF)
            wis_ref[:, at] = dot(turned_ref[...], hs).astype(BF)
            out_ref[...] += dot_t(hs, wi_ref[:, at])

        copies = []
        slots = (0, 3 - first, first, 3)

        def add(h, at, size, dst):
            wide_at = pl.ds(pl.multiple_of(at, 16), size)
            deep_at = pl.ds(pl.multiple_of(at + h * feat, 16), size)
            for i, src in enumerate((wis_ref.at[wide_at, pl.ds(h * feat, feat)], wos_ref.at[deep_at])):
                copies.append(pltpu.make_async_copy(src, dst.at[i], sems.at[len(copies)]))

        for i, j in enumerate(slots):
            to = (where_ref[1] ^ j) * n
            add(0, to, n, outs[i // 2].at[i % 2])
            if columns:
                for c in range(4):
                    add(1, to + c * (n // 4), n // 4, outs[2].at[c, i])
            else:
                add(1, to, n, outs[2 + i // 2].at[i % 2])
        start_all(copies)
        low_ref[...] = out_ref[...].astype(BF)
        wait_all(copies)

    block = ((2, 2, n, feat), BF, HB)
    more = [((4, 4, 2, n // 4, feat), BF, HB)] if columns else [block] * 2
    return call(
        kernel,
        [((r2, feat), F32, VM), ((r2, feat), F32, VM), ((r2, feat), BF, VM)] + [block] * 2 + more,
        [
            (where, SM), (u, VM), (x, VM), (gains, VM), (part, VM), (got, VM), (normed, VM),
            (hidden, VM), (wi, VM), (wo, VM),
        ],
        scratch=[
            pltpu.VMEM((r2, feat), BF), pltpu.VMEM((feat, r2), BF), pltpu.VMEM((feat, wide), BF),
            pltpu.VMEM((wide, feat), BF), pltpu.SemaphoreType.DMA((40,)),
        ],
        after=after,
        flops=10 * r2 * feat * wide,
        bytes_accessed=24 * 2**20,
    )


def attend_proj_back(where, dq, own, got, normed, w, wps, small, first, rows, last, after=()):
    r2, feat = normed.shape
    half = feat // 2
    n, m = feat // 4, half // 4
    tile = 384
    extra = 0 if small is None else n // 3

    def kernel(where_ref, dq_ref, own_ref, got_ref, normed_ref, w_ref, wps_ref, *refs):
        refs = list(refs)
        take = lambda k: [refs.pop(0) for _ in range(k)]
        small_ref = take(1)[0] if extra else None
        out_ref, low_ref, keep_ref, send_ref, packed_ref, turned_ref, ws_ref, sm_ref, sems = take(9)
        packed_ref[:, :half] = dq_ref[...]
        packed_ref[:, half:] = (own_ref[...] + got_ref[...].astype(F32)).astype(BF)
        out = dot_t(packed_ref[...], w_ref[...])
        out_ref[...] = out[: out_ref.shape[0]]
        low_ref[...] = (out[rows:] if last else out).astype(BF)
        turned_ref[...] = normed_ref[...].T

        @pl.loop(0, 3 * half // tile)
        def _(t):
            at = pl.ds(pl.multiple_of(t * tile, 128), tile)
            ws_ref[:, at] = dot(turned_ref[...], packed_ref[:, at]).astype(BF)

        if extra:
            wide = jnp.concatenate(
                [small_ref[...], jnp.zeros((128 - small_ref.shape[0], feat), F32)], 0
            )
            sm_ref[...] = wide.T.astype(BF)
        copies = []

        def add(src, dst):
            copies.append(pltpu.make_async_copy(src, dst, sems.at[len(copies)]))

        for ref, js in ((keep_ref, (0, 3 - first)), (send_ref, (first, 3))):
            for i, j in enumerate(js):
                to = where_ref[1] ^ j
                at, pat = pl.ds(pl.multiple_of(to * n, 16), n), pl.ds(pl.multiple_of(to * m, 16), m)
                for g in range(3):
                    add(ws_ref.at[at, pl.ds(g * half, half)], ref.at[i, pl.ds(g * n, n)])
                for g in range(2):
                    add(wps_ref.at[pat, pl.ds(g * half, half)], ref.at[i, pl.ds(3 * n + g * m, m)])
                if extra:
                    for g in range(3):
                        sat = pl.ds(pl.multiple_of(to * n + g * extra, 16), extra)
                        add(sm_ref.at[sat], ref.at[i, pl.ds(3 * n + 2 * m, extra), pl.ds(128 * g, 128)])
        start_all(copies)
        wait_all(copies)

    n_out = rows if last else r2
    block = ((2, 3 * n + 2 * m + extra, half), BF, HB)
    return call(
        kernel,
        [((n_out, feat), F32, VM), ((n_out, feat), BF, VM), block, block],
        [(where, SM), (dq, VM), (own, VM), (got, VM), (normed, VM), (w, VM), (wps, VM)]
        + ([(small, VM)] if extra else []),
        scratch=[
            pltpu.VMEM((r2, 3 * half), BF), pltpu.VMEM((feat, r2), BF), pltpu.VMEM((feat, 3 * half), BF),
            pltpu.VMEM((feat, 128), BF), pltpu.SemaphoreType.DMA((32,)),
        ],
        after=after,
        flops=4 * r2 * feat * 3 * half,
        bytes_accessed=10 * 2**20,
    )


def join_upstream(u_own, u_sib, rows):
    feat = u_own.shape[1]

    def kernel(o_ref, s_ref, u_ref, low_ref):
        u_ref[pl.ds(0, rows), :] = o_ref[...]
        u_ref[pl.ds(rows, rows), :] = s_ref[...].astype(F32)
        low_ref[pl.ds(0, rows), :] = o_ref[...].astype(BF)
        low_ref[pl.ds(rows, rows), :] = s_ref[...]

    return call(
        kernel, [((2 * rows, feat), F32, VM), ((2 * rows, feat), BF, VM)], [(u_own, VM), (u_sib, VM)],
        bytes_accessed=2**21,
    )


def norm_step(u, x, gains, gain_row, part, got, rows, last, after=()):
    feat = x.shape[1]
    n = rows if last else 2 * rows

    def kernel(u_ref, x_ref, gains_ref, part_ref, got_ref, *outs):
        if last:
            slope = part_ref[...] + got_ref[...].astype(F32)
        else:
            slope = add_both(part_ref[...], got_ref[...], rows)
        u2 = u_ref[:n] + norm_back(x_ref[:n], gains_ref[pl.ds(gain_row, 1), :], slope)[0]
        low = outs[-1]
        low[...] = u2[: low.shape[0]].astype(BF)
        if not last:
            outs[0][...] = u2

    outs = [((last if last else n, feat), BF, VM)]
    return call(
        kernel,
        outs if last else [((n, feat), F32, VM)] + outs,
        [(u, VM), (x, VM), (gains, VM), (part, VM), (got, VM)],
        after=after,
        bytes_accessed=6 * 2**20,
    )


def picks(index, turn, cap, cap_rows, experts):
    at = lax.broadcasted_iota(jnp.int32, (1, experts * cap_rows), 1)
    out = []
    for k in range(TOP):
        chosen, slot = index[:, k : k + 1], index[:, TOP + k : TOP + k + 1]
        place = chosen if turn is None else chosen ^ turn
        target = jnp.where(slot < cap, place * cap_rows + slot, -1)
        out.append(jnp.where(at == target, 1.0, 0.0).astype(BF))
    return out


def lane_at(index, k):
    lane = lax.broadcasted_iota(jnp.int32, (1, 128), 1)
    return jnp.where(lane == index[:, k : k + 1] + 4, 1.0, 0.0)


def present_mask(blk, rows, blk_len, longest):
    pos = lax.broadcasted_iota(jnp.int32, (rows, 1), 0)
    last = jnp.where(blk < longest, blk_len, blk_len - 1)
    return jnp.where(pos < last, 1.0, 0.0)


def route(where, x, part, got, gains, small, cot, index, experts, cap, rows, blk_len, longest, fast, after=()):
    feat = x.shape[1]
    cap_rows = up16(cap)

    def kernel(where_ref, x_ref, part_ref, got_ref, gains_ref, small_ref, cot_ref, index_ref,
               x3_ref, moe_ref, gates_ref, up_ref, *blocks):
        x3 = x_ref[:rows] + part_ref[:rows] + got_ref[...].astype(F32)
        x3_ref[...] = x3
        moe = layer_norm(x3, gains_ref[pl.ds(3, 1), :])
        moe_ref[...] = moe
        lane = lax.broadcasted_iota(jnp.int32, (1, 128), 1)
        logits = dot(moe, small_ref[...])
        logits = jnp.where((lane >= 4) & (lane < 4 + experts), logits, -1e30)
        ex = jnp.exp(logits - jnp.max(logits, -1, keepdims=True))
        gates = ex / jnp.sum(ex, -1, keepdims=True)
        gates_ref[...] = gates
        up_ref[...] = jnp.zeros_like(up_ref)
        up_ref[pl.ds(0, blk_len), :] = cot_ref[...].astype(F32)
        up = up_ref[...] * present_mask(where_ref[0], rows, blk_len, longest)
        up_ref[...] = up
        index = index_ref[...]
        pick = picks(index, where_ref[1] if fast else None, cap, cap_rows, experts)
        sent = t_dot(pick[0] + pick[1], moe).astype(BF)
        slope = 0.0
        for k in range(TOP):
            gate = jnp.sum(gates * lane_at(index, k), -1, keepdims=True)
            slope += t_dot(pick[k], (gate * up).astype(BF))
        slope = slope.astype(BF)
        for j, ref in enumerate(blocks):
            ref[pl.ds(0, cap_rows), :] = sent[j * cap_rows : (j + 1) * cap_rows]
            ref[pl.ds(cap_rows, cap_rows), :] = slope[j * cap_rows : (j + 1) * cap_rows]

    return call(
        kernel,
        [((rows, feat), F32, VM), ((rows, feat), BF, VM), ((rows, 128), F32, VM), ((rows, feat), F32, VM)]
        + [((2 * cap_rows, feat), BF, VM)] * experts,
        [(where, SM), (x, VM), (part, VM), (got, VM), (gains, VM), (small, VM), (cot, VM), (index, VM)],
        after=after,
        flops=6 * rows * experts * cap_rows * feat,
        bytes_accessed=5 * 2**20,
    )


def expert_half(blocks, w_in, w_out, acc, cap_rows, after=()):
    feat = w_in.shape[0]
    wide = w_in.shape[1]
    tile = 512 if wide % 512 == 0 else wide
    n = len(blocks) * cap_rows
    steps = wide // tile
    final = acc is not None

    def kernel(*refs):
        refs = list(refs)
        take = lambda k: [refs.pop(0) for _ in range(k)]
        ins = take(len(blocks))
        wi_ref, wo_ref = take(2)
        before = take(2) if final else None
        take(len(after))
        outs = take(len(blocks)) if final else take(2)
        rows_ref, slope_ref, res_ref, back_ref = take(4)
        t = pl.program_id(0)

        @pl.when(t == 0)
        def _():
            for j, ref in enumerate(ins):
                at = pl.ds(j * cap_rows, cap_rows)
                rows_ref[at, :] = ref[pl.ds(0, cap_rows), :]
                slope_ref[at, :] = ref[pl.ds(cap_rows, cap_rows), :]
            if final:
                res_ref[...] = before[0][...]
                back_ref[...] = before[1][...]
            else:
                res_ref[...] = jnp.zeros_like(res_ref)
                back_ref[...] = jnp.zeros_like(back_ref)

        act, dact = gelu_both(dot(rows_ref[...], wi_ref[...]))
        hs = (dact * dot_t(slope_ref[...], wo_ref[...])).astype(BF)
        res_ref[...] += dot(act.astype(BF), wo_ref[...])
        back_ref[...] += dot_t(hs, wi_ref[...])

        @pl.when(t == steps - 1)
        def _():
            if final:
                for j, ref in enumerate(outs):
                    at = pl.ds(j * cap_rows, cap_rows)
                    ref[pl.ds(0, cap_rows), :] = res_ref[at, :].astype(BF)
                    ref[pl.ds(cap_rows, cap_rows), :] = back_ref[at, :].astype(BF)
            else:
                outs[0][...] = res_ref[...]
                outs[1][...] = back_ref[...]

    whole = lambda shape: pl.BlockSpec(shape, lambda t: (0,) * len(shape))
    blk = (2 * cap_rows, feat)
    ins = [*blocks, w_in, w_out] + (list(acc) if final else []) + list(after)
    in_specs = [whole(blk)] * len(blocks) + [
        pl.BlockSpec((feat, tile), lambda t: (0, t)), pl.BlockSpec((tile, feat), lambda t: (t, 0))
    ]
    in_specs += [whole((n, feat))] * (2 if final else 0) + [HB] * len(after)
    if final:
        shapes, specs = [jax.ShapeDtypeStruct(blk, BF)] * len(blocks), [whole(blk)] * len(blocks)
    else:
        shapes, specs = [jax.ShapeDtypeStruct((n, feat), F32)] * 2, [whole((n, feat))] * 2
    return pl.pallas_call(
        kernel,
        grid=(steps,),
        out_shape=shapes,
        in_specs=in_specs,
        out_specs=specs,
        scratch_shapes=[
            pltpu.VMEM((n, feat), BF), pltpu.VMEM((n, feat), BF),
            pltpu.VMEM((n, feat), F32), pltpu.VMEM((n, feat), F32),
        ],
        compiler_params=pltpu.CompilerParams(
            vmem_limit_bytes=50 * 2**20, dimension_semantics=("arbitrary",)
        ),
        cost_estimate=pl.CostEstimate(
            flops=8 * n * feat * wide, bytes_accessed=10 * 2**20, transcendentals=0
        ),
    )(*ins)


def expert_slopes(every, w_in, w_out, got, after=()):
    feat, wide = w_in.shape
    tile = 256 if wide % 256 == 0 else wide
    steps = wide // tile
    groups, experts, cap_rows = every.shape[0], every.shape[1], every.shape[2] // 2
    total = groups * experts * cap_rows
    kind = BF if got is None else F32

    def kernel(*refs):
        refs = list(refs)
        take = lambda k: [refs.pop(0) for _ in range(k)]
        every_ref, wi_ref, wo_ref = take(3)
        got_refs = take(2) if got is not None else None
        take(len(after))
        wis_ref, wos_ref, rows_ref, slope_ref, turned_ref, sems = take(6)

        @pl.when(pl.program_id(0) == 0)
        def _():
            copies = []
            for k in range(groups):
                for j in range(experts):
                    at = pl.ds((k * experts + j) * cap_rows, cap_rows)
                    for i, ref in enumerate((rows_ref, slope_ref)):
                        copies.append(pltpu.make_async_copy(
                            every_ref.at[k, j, pl.ds(i * cap_rows, cap_rows)], ref.at[at],
                            sems.at[len(copies)],
                        ))
            start_all(copies)
            wait_all(copies)
            turned_ref[...] = rows_ref[...].T

        act, dact = gelu_both(dot(rows_ref[...], wi_ref[...]))
        hs = (dact * dot_t(slope_ref[...], wo_ref[...])).astype(BF)
        wis = dot(turned_ref[...], hs)
        wos = t_dot(act.astype(BF), slope_ref[...])
        if got is not None:
            wis, wos = wis + got_refs[0][...].astype(F32), wos + got_refs[1][...].astype(F32)
        wis_ref[...] = wis.astype(kind)
        wos_ref[...] = wos.astype(kind)

    wi_spec = pl.BlockSpec((feat, tile), lambda t: (0, t))
    wo_spec = pl.BlockSpec((tile, feat), lambda t: (t, 0))
    return pl.pallas_call(
        kernel,
        grid=(steps,),
        out_shape=[jax.ShapeDtypeStruct((feat, wide), kind), jax.ShapeDtypeStruct((wide, feat), kind)],
        in_specs=[HB] + [wi_spec, wo_spec] * (1 if got is None else 2) + [HB] * len(after),
        out_specs=[wi_spec, wo_spec],
        scratch_shapes=[
            pltpu.VMEM((total, feat), BF), pltpu.VMEM((total, feat), BF), pltpu.VMEM((feat, total), BF),
            pltpu.SemaphoreType.DMA((2 * groups * experts,)),
        ],
        compiler_params=pltpu.CompilerParams(
            vmem_limit_bytes=56 * 2**20, dimension_semantics=("arbitrary",)
        ),
        cost_estimate=pl.CostEstimate(
            flops=8 * total * feat * wide, bytes_accessed=20 * 2**20, transcendentals=0
        ),
    )(every, w_in, w_out, *(got or ()), *after)


def combine(where, blocks, x3, moe, gates, up, index, small, gains, small_rows, experts, cap, rows, blk_len, longest, fast, after=()):
    feat = x3.shape[1]
    cap_rows = up16(cap)
    n = experts * cap_rows

    def kernel(where_ref, *refs):
        refs = list(refs)
        take = lambda k: [refs.pop(0) for _ in range(k)]
        ins = take(experts)
        x3_ref, moe_ref, gates_ref, up_ref, index_ref, small_ref, gains_ref = take(7)
        acts_ref, u_ref, low_ref, slopes_ref, result_ref, back_ref = take(6)
        for j, ref in enumerate(ins):
            at = pl.ds(j * cap_rows, cap_rows)
            result_ref[at, :] = ref[pl.ds(0, cap_rows), :]
            back_ref[at, :] = ref[pl.ds(cap_rows, cap_rows), :]
        index, gates, up, moe = index_ref[...], gates_ref[...], up_ref[...], moe_ref[...]
        pick = picks(index, where_ref[1] if fast else None, cap, cap_rows, experts)
        x3 = x3_ref[...]
        acts, all_slope = x3, 0.0
        for k in range(TOP):
            at_k = lane_at(index, k)
            gate = jnp.sum(gates * at_k, -1, keepdims=True)
            picked = dot(pick[k], result_ref[...])
            acts = acts + gate * picked
            all_slope += jnp.sum(up * picked, -1, keepdims=True) * at_k
        acts = acts * present_mask(where_ref[0], rows, blk_len, longest)
        acts_ref[...] = acts[:blk_len].astype(BF)
        logit = (gates * (all_slope - jnp.sum(gates * all_slope, -1, keepdims=True))).astype(BF)
        slope = dot(pick[0] + pick[1], back_ref[...]) + dot_t(logit, small_ref[...])
        dx, terms = norm_back(x3, gains_ref[pl.ds(3, 1), :], slope)
        u = up + dx
        u_ref[...] = u
        low_ref[...] = u.astype(BF)
        slopes_ref[...] = t_dot(logit, moe)[:small_rows]
        slopes_ref[pl.ds(3, 1), :] = jnp.sum(terms, 0, keepdims=True)

    return call(
        kernel,
        [((blk_len, feat), BF, VM), ((rows, feat), F32, VM), ((rows, feat), BF, VM), ((small_rows, feat), F32, VM)],
        [(where, SM)] + [(b, VM) for b in blocks]
        + [(t, VM) for t in (x3, moe, gates, up, index, small, gains)],
        scratch=[pltpu.VMEM((n, feat), BF), pltpu.VMEM((n, feat), BF)],
        after=after,
        flops=6 * rows * n * feat,
        bytes_accessed=5 * 2**20,
    )


def tie(xs, *after):
    return list(lax.optimization_barrier((*xs, *after)))[: len(xs)]


class Links:
    def __init__(self, mesh):
        self.E = mesh.shape["expert"]
        self.C = mesh.shape["context"]
        self.D = mesh.shape["dp"]
        assert self.C == 4 and self.D == 2 and self.E % 2 == 0
        self.fast = self.E == 4
        self.chips = self.E * self.C
        flat = lambda e, c, d: (e * self.C + c) * self.D + d
        self.team = [
            (flat(e, c, d), flat((e // 2) * 2 + c // 2, 2 * (e % 2) + d, c % 2))
            for e in range(self.E)
            for c in range(self.C)
            for d in range(self.D)
        ]
        self.to_lane = [(f, (f % self.chips) * 2 + f // self.chips) for f in range(2 * self.chips)]
        self.from_lane = [(b, a) for a, b in self.to_lane]

    def move(self, x):
        return lax.ppermute(x, ALL, self.team)

    def xor(self, x, axis, j):
        n = {"expert": self.E, "context": self.C, "dp": self.D}[axis]
        return lax.ppermute(x, axis, [(i, i ^ j) for i in range(n)])

    def sib(self, x):
        return self.xor(x, "dp", 1)

    def partner(self, x):
        return self.xor(x, "expert", 1)

    def column(self, x, *hold):
        c = lax.axis_index("context")
        got = tie([x] + [self.xor(x, "context", j) for j in range(1, 4)], *hold)
        pick = lambda k: jnp.where(
            c & 2 == 0, jnp.where(c & 1 == 0, got[k], got[k ^ 1]), jnp.where(c & 1 == 0, got[k ^ 2], got[k ^ 3])
        )
        return jnp.stack([pick(k) for k in range(4)])

    def plane_sum(self, keep, send, first, hold):
        (got,) = tie([self.xor(send, "expert", first)], *hold[0])
        got = got.astype(F32)
        give = (keep[1].astype(F32) + got[1]).astype(BF)
        (far,) = tie([self.xor(give, "expert", 3 - first)], *hold[1])
        return keep[0].astype(F32) + got[0] + far.astype(F32), give

    def column_sum(self, x, *hold):
        c = lax.axis_index("context")
        low = x.astype(BF)
        got = [self.xor(lax.dynamic_index_in_dim(low, c ^ j, 0, False), "context", j) for j in range(1, 4)]
        got = tie(got, *hold)
        total = lax.dynamic_index_in_dim(x, c, 0, False)
        for t in got:
            total = total + t.astype(F32)
        return total

    def swap_blocks(self, x):
        if not self.fast:
            return list(lax.all_to_all(jnp.stack(x), "expert", 0, 0, tiled=True))
        return [x[0]] + [self.xor(x[j], "expert", j) for j in range(1, 4)]


def lane_rows(links, mine, d):
    keep = lax.dynamic_index_in_dim(mine, d, 0, False)
    got = links.sib(lax.dynamic_index_in_dim(mine, 1 - d, 0, False))
    return jnp.where(d == 0, jnp.concatenate([keep, got], 0), jnp.concatenate([got, keep], 0))


def in_order(d, own, other):
    return jnp.where(d == 0, jnp.stack([own, other]), jnp.stack([other, own]))


class Weights:
    def __init__(self, links, rdev, feat, ff):
        self.links, self.rdev, self.feat, self.ff = links, rdev, feat, ff
        self.d = lax.axis_index("dp")
        self.given = []
        self.half = feat // 2

    def split_attend(self, w):
        w = w.reshape(self.rdev, 3, 2, self.half).transpose(2, 0, 1, 3)
        return w.reshape(2, self.rdev, 3 * self.half)

    def split_widen(self, w):
        w = w.reshape(self.rdev, self.links.chips, 2, 2, -1).transpose(2, 0, 3, 1, 4)
        return w.reshape(2, self.rdev, self.ff // 2)

    def pack_attend(self, w, p, small):
        parts = [w, jnp.concatenate([p[:, : self.half], p[:, self.half :]], 0)]
        if small is not None:
            parts.append(jnp.pad(small, ((0, 0), (0, 128 - small.shape[1]))))
        return jnp.concatenate(parts, 1)

    def pack_wide(self, wout):
        h = wout.shape[0] // 2
        return jnp.concatenate([wout[:h], wout[h:]], 1)

    def column(self, buf, *hold):
        if self.links.fast:
            return self.links.column(buf, *hold)
        return lax.all_gather(buf, CHIPS, axis=0, tiled=False)

    def cut(self, x):
        return x if self.links.fast else x.reshape(4, -1, x.shape[-1])

    def pack_block(self, quad):
        f, h, r = self.feat, self.half, self.rdev
        n = quad.shape[0]
        p = quad[..., f + h : 2 * f].reshape(n, 2, r, h)
        parts = [quad[..., i * h : (i + 1) * h] for i in range(3)] + [p[:, 0], p[:, 1]]
        parts = [self.cut(t.reshape(-1, h)) for t in parts]
        if quad.shape[2] > 2 * f:
            small = self.cut(quad[..., 2 * f :].reshape(-1, 128))
            small = small.reshape(small.shape[:-2] + (3, -1, 128))
            parts.append(jnp.concatenate([small[..., g, :, :] for g in range(3)], -1))
        return jnp.concatenate(parts, -2)

    def pack_pair(self, quad_in, quad_out):
        f = self.feat
        halves = []
        for i in range(2):
            pair = [self.cut(t[..., i * f : (i + 1) * f].reshape(-1, f)) for t in (quad_in, quad_out)]
            halves.append(jnp.stack(pair, -3))
        return jnp.stack(halves, -4)

    def spread(self, x, cuts, *hold):
        if not self.links.fast:
            return [x[0], x[1], x[2], cuts[0](x[3]), cuts[1](x[3])]
        to = lambda t, j: self.links.xor(t, "expert", j)
        x1, x2 = tie([to(x, 1), to(x, 2)], *hold)
        return [x, x1, x2, to(cuts[0](x1), 2), to(cuts[1](x2), 1)]

    def spread_attend(self, x, *hold):
        n = self.feat // 2
        return self.spread(x, (lambda t: t[:n], lambda t: t[n:]), *hold)

    def spread_pair(self, x, *hold):
        return self.spread(x, (lambda t: t[0], lambda t: t[1]), *hold)

    def total(self, keep, send, first, hold):
        if self.links.fast:
            out, give = self.links.plane_sum(keep, send, first, hold)
            self.given.append(give)
            return out
        blk = {0: keep[0], 3 - first: keep[1], first: send[0], 3: send[1]}
        return jnp.stack([blk[j] for j in range(4)])

    def column_sum(self, buf, hold):
        if self.links.fast and hold is not None:
            return self.links.column_sum(buf, *hold)
        axes = "context" if self.links.fast else CHIPS
        return lax.psum_scatter(buf.astype(BF), axes, scatter_dimension=0, tiled=False).astype(F32)

    def exchange(self, w):
        w = w.reshape(2, self.rdev, -1)
        mine = lax.dynamic_index_in_dim(w, self.d, 0, False)
        got = self.links.sib(lax.dynamic_index_in_dim(w, 1 - self.d, 0, False))
        return in_order(self.d, mine, got)

    def owner_attend(self, keep, send, first, hold, after=()):
        f, h, r = self.feat, self.half, self.rdev
        t = self.total(keep, send, first, hold)
        n, m = f // 4, h // 4
        cut = lambda t, k: t.reshape(-1, k * r, t.shape[-1])
        parts = [cut(t[..., g * n : (g + 1) * n, :], 2) for g in range(3)]
        p = [cut(t[..., 3 * n + g * m : 3 * n + (g + 1) * m, :], 1) for g in range(2)]
        parts.append(jnp.concatenate(p, 1))
        small = t.shape[-2] > 3 * n + 2 * m
        if small:
            sm = t[..., 3 * n + 2 * m :, :]
            sm = jnp.stack([sm[..., 128 * g : 128 * (g + 1)] for g in range(3)], -3)
            parts.append(sm.reshape(-1, 2 * r, 128))
        (buf,) = tie([jnp.concatenate(parts, 2)], *after)
        buf = self.column_sum(buf, hold[2])
        p = jnp.concatenate([buf[:r, f + h : 2 * f], buf[r:, f + h : 2 * f]], 1)
        p = lax.ppermute(p, ALL, self.links.from_lane)
        w = buf[:, : f + h]
        if small:
            w = jnp.concatenate([w, buf[:, 2 * f :]], 1)
        w = self.exchange(w)
        extra = w[0, :, f + h :] + w[1, :, f + h :]
        w = w[..., : f + h].reshape(2, r, 3, h).transpose(1, 2, 0, 3).reshape(r, 3 * f)
        return w, p, extra

    def reduce_column(self, by_context):
        t = lax.psum_scatter(by_context, "context", scatter_dimension=0, tiled=False)
        return t[:2], t[2:]

    def owner_wide(self, slopes, first, hold):
        f, r = self.feat, self.rdev
        a = self.total(*slopes[:2], first, hold[0])
        if self.links.fast:
            a = jnp.moveaxis(a.reshape(2, 4, 2 * r, f), 1, 0)
            a = self.column_sum(a, hold[0][2])
            b = self.total(*slopes[2:], first, hold[1])
            w = jnp.concatenate([a[0], b[0]], 1)
            w_out = jnp.concatenate([a[1], b[1]], 0)
        else:
            b = self.total(*slopes[2:], first, hold[1])
            hid = self.ff // (4 * self.links.chips)
            w = [t[..., 0, :, :].reshape(-1, 2 * r, f) for t in (a, b)]
            w_out = [t[..., 1, :, :].reshape(-1, hid, f) for t in (a, b)]
            w, w_out = [self.column_sum(jnp.concatenate(t, 2), None) for t in (w, w_out)]
            w_out = jnp.concatenate([w_out[:, :f], w_out[:, f:]], 0)
        w = self.exchange(w).reshape(2, r, 2, self.links.chips, -1)
        return w.transpose(1, 3, 0, 2, 4).reshape(r, self.ff), w_out


def body(links, *args):
    (tokens, cotangent, g1, w1, p1, g2, win, wout, g3, w3, p3, g4, router, ein, eout, routes, slots) = args
    e = lax.axis_index("expert")
    d = lax.axis_index("dp")
    blk_len, feat = tokens.shape[1:]
    rows = up16(blk_len)
    half = feat // 2
    rdev = w1.shape[0]
    ff = win.shape[1]
    longest = LEN - (blk_len - 1) * links.C
    experts = router.shape[1]
    small_rows = (4 + experts + 7) // 8 * 8
    cap = max(2, (5 * TOP * blk_len + 4 * experts - 1) // (4 * experts))
    blk = 2 * (e % 2) + d
    where = jnp.stack([blk, e if links.fast else 0 * e]).astype(jnp.int32)
    wt = Weights(links, rdev, feat, ff)
    img = dict(rows=rows, blk_len=blk_len, longest=longest)

    tok = links.move(tokens[0])
    ps = lax.ppermute(jnp.concatenate([p1, p3], 0), ALL, links.to_lane)
    small = jnp.concatenate([g1[:, None], g2[:, None], g3[:, None], g4[:, None], router], 1)
    gsm = small.shape[1]
    lane1 = jnp.concatenate(
        [wt.split_attend(w1), jnp.broadcast_to(small[None], (2, rdev, gsm))], 2
    )
    lane1 = lane_rows(links, lane1, d)
    buf1 = wt.pack_attend(lane1[:, : 3 * half], ps[:rdev], lane1[:, 3 * half :])
    quad1 = wt.column(buf1)
    tok_pair = jnp.stack([tok, links.partner(tok)])
    tok_sib = links.sib(tok_pair)
    toks = [tok_pair[0], tok_sib[0], tok_pair[1], tok_sib[1]]
    blocks1 = wt.spread_attend(wt.pack_block(quad1))

    later = jnp.concatenate([wt.split_widen(win), wt.split_attend(w3)], 2)
    later = lane_rows(links, later, d)
    w_in, w_out = later[:, : ff // 2], wt.pack_wide(wout)
    buf3 = wt.pack_attend(later[:, ff // 2 :], ps[rdev:], None)

    x0, normed1, q1, kv1, far1, wa1, wp1, small, gains = attend_first(where, toks, small_rows, blocks1, rows)
    part, low, blend1, lse1 = attend_core(where, q1, kv1, far1, wp1, solo=False, **img)
    if links.fast:
        (buf2,) = tie([jnp.concatenate([w_in, w_out], 1)], quad1)
        quad2 = wt.column(buf2, part)
        quad2 = quad2[..., : ff // 2], quad2[..., ff // 2 :]
    else:
        quad2 = wt.column(w_in), wt.column(w_out)
    pair2 = wt.pack_pair(*quad2)
    blocks2 = wt.spread_pair(pair2)
    quad3 = wt.column(tie([buf3], pair2)[0], *blocks2[1:3])
    cot, raw = tie([cotangent[0].astype(BF), jnp.concatenate([routes[0], slots[0]], 1)], quad3)
    raw, cot = tie([links.move(raw), links.move(cot)], blocks2[3])
    index = jnp.pad(raw, ((0, rows - blk_len), (0, 0)), constant_values=cap)
    x1, normed2, hidden, part2, low2, wi, wo = widen_forward(
        where, x0, part, links.sib(low), gains, blocks2, rows
    )
    blocks3 = wt.spread_attend(tie([wt.pack_block(quad3)], *blocks2[3:])[0], x1)
    x2, normed3, own3 = norm_next(x1, part2, links.sib(low2), gains, 2, rows)
    far_own = links.partner(own3)
    q3, kv3, wa3, wp3 = attend_next(where, normed3, blocks3, after=(cot, index))
    (far_own,) = tie([far_own], q3)
    part3, low3, blend3, lse3, far3 = attend_core(
        where, q3, kv3, None, wp3, solo=True, far=(far_own, links.sib(far_own), wa3), **img
    )
    moe_args = dict(experts=experts, cap=cap, fast=links.fast, **img)
    x3, moe, gates, up, *sent = route(
        where, x2, part3, links.sib(low3), gains, small, cot, index, **moe_args
    )
    ein_own, eout_own = ein[0], eout[0]
    ein_sib, eout_sib = [links.sib(t) for t in tie([ein_own, eout_own], low3)]
    came = links.swap_blocks(sent)
    every = lax.all_gather(jnp.stack(came), "context", axis=0, tiled=False)
    sums = expert_half(came, ein_sib, eout_sib, None, up16(cap))
    answer = links.swap_blocks(expert_half(came, ein_own, eout_own, sums, up16(cap)))
    acts, u, u_low, small_slopes = combine(
        where, answer, x3, moe, gates, up, index, small, gains, small_rows, **moe_args
    )

    u, u_low = join_upstream(u, links.sib(u_low), rows)
    dq, own, far, wps = attend_core_back(where, u_low, wp3, blend3, q3, kv3, far3, lse3, **img)
    first3, first2, first1 = 2, 2, 1
    part, low, *slopes3 = attend_proj_back(
        where, dq, own, links.partner(far), normed3, wa3, wps, small_slopes, first3, rows, False
    )
    u, part, low, *slopes2 = widen_back(
        where, u, x2, gains, part, links.sib(low), normed2, hidden, wi, wo, first2, rows, links.fast
    )
    u1, u_low = norm_step(u, x1, gains, 1, part, links.sib(low), rows, 0)
    dq1, own, far, wps = attend_core_back(where, u_low, wp1, blend1, q1, kv1, far1, lse1, **img)
    part, low, *slopes1 = attend_proj_back(
        where, dq1, own, links.partner(far), normed1, wa1, wps, None, first1, rows, True
    )
    (u2,) = norm_step(u1, x0, gains, 0, part, links.sib(low), rows, blk_len)
    moved = links.move(jnp.stack([acts, u2]))
    acts, token_slope = moved[0], moved[1]
    if links.fast:
        (by_context,) = tie(slopes2[2:], every)
        slopes2 = slopes2[:2] + list(wt.reduce_column(by_context))
        after3 = slopes2[2:]
    else:
        after3 = ()
    e_sib = expert_slopes(every, ein_sib, eout_sib, None, after=(u2,))
    w3_out, p3_out, extra = wt.owner_attend(*slopes3, first3, ((u,), (dq1,), None), after=after3)
    wt.given = []
    win_out, wout_out = wt.owner_wide(slopes2, first2, (((dq1,), (e_sib[0],), ()), ((e_sib[0],), (), ())))
    w1_out, p1_out, _ = wt.owner_attend(*slopes1, first1, ((e_sib[0],), (), ()))
    e_slopes = expert_slopes(every, ein_own, eout_own, [links.sib(t) for t in e_sib], after=wt.given)

    def gain_slope(w, slope, gain):
        return jnp.sum(w.astype(F32) * slope, 1) / gain.astype(F32)

    return (
        acts.astype(F32)[None], token_slope.astype(F32)[None],
        gain_slope(w1, w1_out, g1), w1_out, p1_out, gain_slope(win, win_out, g2), win_out, wout_out,
        gain_slope(w3, w3_out, g3), w3_out, p3_out, extra[:, 3], extra[:, 4 : 4 + experts],
        e_slopes[0][None], e_slopes[1][None],
    )


def solution(mesh):
    links = Links(mesh)
    tok = P(("expert", "dp"), "context", None)
    vec, mat = P(ALL), P(ALL, None)
    ein, eout = P("expert", None, "dp"), P("expert", "dp", None)
    dense = (vec, mat, mat, vec, mat, mat, vec, mat, mat, vec, mat, ein, eout)
    return jax.shard_map(
        functools.partial(body, links),
        mesh=mesh,
        in_specs=(tok, tok) + dense + (tok, tok),
        out_specs=(tok, tok) + dense,
        check_vma=False,
    )
```

```python
import functools

import jax
import jax.numpy as jnp
from jax import lax
from jax.experimental import pallas as pl
from jax.experimental.pallas import tpu as pltpu
from jax.sharding import PartitionSpec as P

HEADS = 12
HEAD_DIM = 64
LEN = 577
TOP = 2
ALL = ("expert", "context", "dp")
CHIPS = ("expert", "context")
BF = jnp.bfloat16
F32 = jnp.float32
VM = pl.BlockSpec(memory_space=pltpu.VMEM)
HB = pl.BlockSpec(memory_space=pl.ANY)
SM = pl.BlockSpec(memory_space=pltpu.SMEM)


def up16(n):
    return (n + 15) // 16 * 16


def dot(a, b):
    return jnp.dot(a, b, preferred_element_type=F32)


def dot_t(a, b):
    return lax.dot_general(a, b, (((1,), (1,)), ((), ())), preferred_element_type=F32)


def t_dot(a, b):
    return lax.dot_general(a, b, (((0,), (0,)), ((), ())), preferred_element_type=F32)


def call(kernel, outs, ins, scratch=(), after=(), flops=0, bytes_accessed=0):
    n_in, n_after = len(ins), len(after)

    def run(*refs):
        kernel(*refs[:n_in], *refs[n_in + n_after :])

    return pl.pallas_call(
        run,
        out_shape=[jax.ShapeDtypeStruct(s, t) for s, t, _ in outs],
        in_specs=[s for _, s in ins] + [HB] * n_after,
        out_specs=[s for _, _, s in outs],
        scratch_shapes=list(scratch),
        compiler_params=pltpu.CompilerParams(vmem_limit_bytes=50 * 2**20),
        cost_estimate=pl.CostEstimate(
            flops=flops, bytes_accessed=bytes_accessed, transcendentals=0
        ),
    )(*[a for a, _ in ins], *after)


def norm_parts(x):
    mean = jnp.mean(x, -1, keepdims=True)
    centre = x - mean
    scale = lax.rsqrt(jnp.mean(centre * centre, -1, keepdims=True) + 1e-06)
    return centre * scale, scale


def layer_norm(x, gain):
    return (norm_parts(x)[0] * gain).astype(BF)


def norm_back(x, gain, slope):
    unit, scale = norm_parts(x)
    terms = slope * unit
    inner = slope * gain
    inner = inner - jnp.mean(inner, -1, keepdims=True) - unit * jnp.mean(inner * unit, -1, keepdims=True)
    return inner * scale, terms


def gelu_both(h):
    k = 0.7978845608028654
    t = jnp.tanh(k * (h + 0.044715 * h * h * h))
    half = 0.5 * (1 + t)
    return h * half, half + 0.5 * h * (1 - t * t) * (k + (3 * 0.044715 * k) * h * h)


def add_both(mine, got, rows):
    return mine + jnp.concatenate([got[rows:], got[:rows]], 0).astype(F32)


def pair_masks():
    lane = lax.broadcasted_iota(jnp.int32, (1, 2 * HEAD_DIM), 1)
    return [(lane < HEAD_DIM).astype(BF), (lane >= HEAD_DIM).astype(BF)]


def key_mask(blk, rows, blk_len, longest):
    pos = lax.broadcasted_iota(jnp.int32, (rows, 1), 0)
    parts = []
    for j in range(4):
        last = jnp.where((blk ^ j) < longest, blk_len, blk_len - 1)
        parts.append(pos < last)
    return jnp.concatenate([jnp.where(p, 1.0, 0.0) for p in parts], 0) > 0.5


def attend_core(where, q, kv_own, kv_far, wp, rows, blk_len, longest, solo, far=None, after=()):
    half = q.shape[1]
    feat = wp.shape[1]
    pairs = half // (2 * HEAD_DIM)
    r2 = 2 * rows

    def kernel(where_ref, q_ref, ko_ref, *refs):
        refs = list(refs)
        take = lambda n: [refs.pop(0) for _ in range(n)]
        given = take(1 if far is None else 3)
        wp_ref, part_ref, low_ref, blend_ref, lse_ref = take(5)
        if far is None:
            kf_ref = given[0]
        else:
            (kf_ref,) = take(1)
            for j in range(2):
                kf_ref[pl.ds(j * rows, rows), :] = dot(given[j][...], given[2][:, half:]).astype(BF)
        ok = key_mask(where_ref[0], rows, blk_len, longest)
        masks = pair_masks()
        for p in range(pairs):
            at, vat = pl.ds(p * 128, 128), pl.ds(half + p * 128, 128)
            k = jnp.concatenate([ko_ref[:, at], kf_ref[:, at]], 0)
            v = jnp.concatenate([ko_ref[:, vat], kf_ref[:, vat]], 0)
            qp = q_ref[:, at]
            acc = None
            for h in range(2):
                s = dot_t(k, qp * masks[h]) * 0.125
                s = jnp.where(ok, s, -1e9)
                top = jnp.max(s, 0, keepdims=True)
                ex = jnp.exp(s - top)
                total = jnp.sum(ex, 0, keepdims=True)
                lse_ref[pl.ds(2 * p + h, 1), :] = top + jnp.log(total)
                shares = (ex * (1.0 / total)).astype(BF)
                out = t_dot(v * masks[h], shares)
                acc = out if acc is None else acc + out
            blend_ref[at, :] = acc.astype(BF)
        part = t_dot(blend_ref[...], wp_ref[...])
        part_ref[...] = part
        low_ref[...] = (part[rows:] if solo else part).astype(BF)

    outs = [
        ((r2, feat), F32, VM), ((rows if solo else r2, feat), BF, VM), ((half, r2), BF, VM), ((8, r2), F32, VM),
    ]
    ins = [(where, SM), (q, VM), (kv_own, VM)]
    if far is None:
        ins.append((kv_far, VM))
    else:
        ins += [(t, VM) for t in far]
        outs.append(((r2, feat), BF, VM))
    return call(
        kernel,
        outs,
        ins + [(wp, VM)],
        after=after,
        flops=2 * r2 * half * (8 * rows + feat),
        bytes_accessed=4 * 2**20,
    )


def attend_core_back(where, u_low, wp, blend, q, kv_own, kv_far, lse, rows, blk_len, longest, after=()):
    half = q.shape[1]
    feat = wp.shape[1]
    pairs = half // (2 * HEAD_DIM)
    r2 = 2 * rows

    def kernel(
        where_ref, u_ref, wp_ref, blend_ref, q_ref, ko_ref, kf_ref, lse_ref,
        dq_ref, own_ref, far_ref, wps_ref, bt_ref, dqt_ref,
    ):
        ok = key_mask(where_ref[0], rows, blk_len, longest)
        masks = pair_masks()
        sub = lax.broadcasted_iota(jnp.int32, (2 * HEAD_DIM, 1), 0)
        row_masks = [(sub < HEAD_DIM).astype(BF), (sub >= HEAD_DIM).astype(BF)]
        u = u_ref[...]
        bt_ref[...] = dot_t(wp_ref[...], u).astype(BF)
        for p in range(pairs):
            at, vat = pl.ds(p * 128, 128), pl.ds(half + p * 128, 128)
            k = jnp.concatenate([ko_ref[:, at], kf_ref[:, at]], 0)
            v = jnp.concatenate([ko_ref[:, vat], kf_ref[:, vat]], 0)
            qp = q_ref[:, at]
            bt = bt_ref[at, :]
            dqt = dk = dv = 0.0
            for h in range(2):
                qm = qp * masks[h]
                s = dot_t(k, qm) * 0.125
                shares = jnp.where(ok, jnp.exp(s - lse_ref[pl.ds(2 * p + h, 1), :]), 0.0)
                slope = dot(v * masks[h], bt)
                t = shares * slope
                ss = (t - shares * jnp.sum(t, 0, keepdims=True)).astype(BF)
                dqt += t_dot(k * masks[h], ss)
                dk += dot(ss, qm)
                dv += dot_t(shares.astype(BF), bt * row_masks[h])
            dqt_ref[at, :] = dqt * 0.125
            dk = dk * 0.125
            own_ref[:, at] = dk[:r2]
            own_ref[:, vat] = dv[:r2]
            far_ref[:, at] = dk[r2:].astype(BF)
            far_ref[:, vat] = dv[r2:].astype(BF)
        dq_ref[...] = dqt_ref[...].T.astype(BF)
        wps_ref[...] = dot(blend_ref[...], u).astype(BF)

    return call(
        kernel,
        [
            ((r2, half), BF, VM), ((r2, 2 * half), F32, VM), ((r2, 2 * half), BF, VM),
            ((half, feat), BF, VM),
        ],
        [
            (where, SM), (u_low, VM), (wp, VM), (blend, VM), (q, VM), (kv_own, VM), (kv_far, VM),
            (lse, VM),
        ],
        scratch=[pltpu.VMEM((half, r2), BF), pltpu.VMEM((half, r2), F32)],
        after=after,
        flops=2 * r2 * half * (20 * rows + 2 * feat),
        bytes_accessed=6 * 2**20,
    )


def start_all(copies):
    for c in copies:
        c.start()


def wait_all(copies):
    for c in copies:
        c.wait()


def attend_copies(e, refs, w_ref, p_ref, small_ref, sems, skip):
    copies = []

    def add(src, dst):
        copies.append(pltpu.make_async_copy(src, dst, sems.at[len(copies)]))

    n = w_ref.shape[0] // 4
    half = p_ref.shape[0]
    m = half // 4
    for j in range(4):
        to = e ^ j
        rows, prows = pl.ds(pl.multiple_of(to * n, 16), n), pl.ds(pl.multiple_of(to * m, 16), m)
        a, b, at = (refs[j], refs[j], 2 * n + skip) if j < 3 else (refs[3], refs[4], 0)
        for g in range(2):
            add(a.at[pl.ds(g * n, n)], w_ref.at[rows, pl.ds(g * half, half)])
        add(b.at[pl.ds(at, n)], w_ref.at[rows, pl.ds(2 * half, half)])
        add(b.at[pl.ds(at + n, m)], p_ref.at[prows, pl.ds(0, half)])
        add(b.at[pl.ds(at + n + m, m)], p_ref.at[prows, pl.ds(half, half)])
        if small_ref is not None:
            for g in range(3):
                srows = pl.ds(pl.multiple_of(to * n + g * (n // 3), 16), n // 3)
                add(b.at[pl.ds(at + n + 2 * m, n // 3), pl.ds(128 * g, 128)], small_ref.at[srows])
    return copies


def attend_first(where, tokens, small_rows, blocks, rows, skip, after=()):
    blk_len, feat = tokens[0].shape
    half = feat // 2
    r2 = 2 * rows

    def kernel(where_ref, *refs):
        refs = list(refs)
        take = lambda n: [refs.pop(0) for _ in range(n)]
        tok, block_refs = take(4), take(5)
        x_ref, normed_ref, q_ref, kv_ref, far_ref, w_ref, p_ref, small_ref, rows_ref, all_ref, sems = take(11)
        copies = attend_copies(where_ref[1], block_refs, w_ref, p_ref, small_ref, sems, skip)
        start_all(copies)
        all_ref[...] = jnp.zeros_like(all_ref)
        for j in range(4):
            all_ref[pl.ds(j * rows, blk_len), :] = tok[j][...].astype(F32)
        x = all_ref[...]
        x_ref[...] = x[:r2]
        unit = norm_parts(x)[0]
        wait_all(copies)
        turned = small_ref[...].astype(F32).T
        rows_ref[...] = turned[: rows_ref.shape[0]]
        normed = (unit * turned[0:1]).astype(BF)
        normed_ref[...] = normed[:r2]
        q_ref[...] = dot(normed[:r2], w_ref[:, :half]).astype(BF)
        kv = dot(normed, w_ref[:, half:]).astype(BF)
        kv_ref[...] = kv[:r2]
        far_ref[...] = kv[r2:]

    return call(
        kernel,
        [
            ((r2, feat), F32, VM), ((r2, feat), BF, VM), ((r2, half), BF, VM), ((r2, feat), BF, VM),
            ((r2, feat), BF, VM), ((feat, 3 * half), BF, VM), ((half, feat), BF, VM),
            ((feat, 128), BF, VM), ((small_rows, feat), F32, VM),
        ],
        [(where, SM)] + [(t, VM) for t in tokens] + [(t, HB) for t in blocks],
        scratch=[pltpu.VMEM((2 * r2, feat), F32), pltpu.SemaphoreType.DMA((32,))],
        after=after,
        flops=2 * r2 * feat * 5 * half,
        bytes_accessed=6 * 2**20,
    )


def norm_next(x, part, got, gains, gain_row, rows, after=()):
    r2, feat = x.shape

    def kernel(x_ref, part_ref, got_ref, gains_ref, x2_ref, normed_ref, own_ref):
        x2 = add_both(x_ref[...] + part_ref[...], got_ref[...], rows)
        x2_ref[...] = x2
        normed = layer_norm(x2, gains_ref[pl.ds(gain_row, 1), :])
        normed_ref[...] = normed
        own_ref[...] = normed[:rows]

    return call(
        kernel,
        [((r2, feat), F32, VM), ((r2, feat), BF, VM), ((rows, feat), BF, VM)],
        [(x, VM), (part, VM), (got, VM), (gains, VM)],
        after=after,
        bytes_accessed=5 * 2**20,
    )


def attend_next(where, normed, source, after=()):
    r2, feat = normed.shape
    half = feat // 2
    packed = source.ndim == 4

    def kernel(where_ref, normed_ref, source_ref, q_ref, kv_ref, *more):
        if packed:
            w_ref, sems = more
            r = source_ref.shape[2] // 4
            copies = []
            for c in range(4):
                for j in range(4):
                    at = pl.multiple_of((where_ref[1] ^ j) * (feat // 4) + c * r, 16)
                    for g in range(3):
                        copies.append(pltpu.make_async_copy(
                            source_ref.at[c, j, pl.ds(g * r, r)],
                            w_ref.at[pl.ds(at, r), pl.ds(g * half, half)], sems.at[len(copies)],
                        ))
            start_all(copies)
            wait_all(copies)
        else:
            w_ref = source_ref
        normed = normed_ref[...]
        q_ref[...] = dot(normed, w_ref[:, :half]).astype(BF)
        kv_ref[...] = dot(normed, w_ref[:, half:]).astype(BF)

    out = call(
        kernel,
        [((r2, half), BF, VM), ((r2, feat), BF, VM)] + ([((feat, 3 * half), BF, VM)] if packed else []),
        [(where, SM), (normed, VM), (source, HB if packed else VM)],
        scratch=[pltpu.SemaphoreType.DMA((48,))] if packed else [],
        after=after,
        flops=2 * r2 * feat * 3 * half,
        bytes_accessed=4 * 2**20,
    )
    return out if packed else [*out, source]


def widen_forward(where, x, part, got, gains, blocks, rows, after=()):
    r2, feat = x.shape
    wide = 2 * feat
    tile = 384

    def kernel(
        where_ref, x_ref, part_ref, got_ref, gains_ref, z0, z1, z2, a3, b3,
        x1_ref, normed_ref, hidden_ref, out_ref, low_ref, wi_ref, wo_ref, sems,
    ):
        n = feat // 4
        copies = []
        for h, last in enumerate((a3, b3)):
            pairs = [z0.at[h], z1.at[h], z2.at[h], last]
            for j in range(4):
                at = (where_ref[1] ^ j) * n
                for src, dst in (
                    (pairs[j].at[0], wi_ref.at[pl.ds(pl.multiple_of(at, 16), n), pl.ds(h * feat, feat)]),
                    (pairs[j].at[1], wo_ref.at[pl.ds(pl.multiple_of(at + h * feat, 16), n)]),
                ):
                    copies.append(pltpu.make_async_copy(src, dst, sems.at[len(copies)]))
        start_all(copies)
        x1 = add_both(x_ref[...] + part_ref[...], got_ref[...], rows)
        x1_ref[...] = x1
        normed_ref[...] = layer_norm(x1, gains_ref[pl.ds(1, 1), :])
        wait_all(copies)
        out_ref[...] = jnp.zeros_like(out_ref)

        @pl.loop(0, wide // tile)
        def _(t):
            at = pl.ds(pl.multiple_of(t * tile, 128), tile)
            h = dot(normed_ref[...], wi_ref[:, at])
            hidden_ref[:, at] = h
            out_ref[...] += dot(gelu_both(h)[0].astype(BF), wo_ref[at, :])

        low_ref[...] = out_ref[...].astype(BF)

    return call(
        kernel,
        [
            ((r2, feat), F32, VM), ((r2, feat), BF, VM), ((r2, wide), F32, VM), ((r2, feat), F32, VM),
            ((r2, feat), BF, VM), ((feat, wide), BF, VM), ((wide, feat), BF, VM),
        ],
        [(where, SM), (x, VM), (part, VM), (got, VM), (gains, VM)] + [(t, HB) for t in blocks],
        scratch=[pltpu.SemaphoreType.DMA((16,))],
        after=after,
        flops=4 * r2 * feat * wide,
        bytes_accessed=16 * 2**20,
    )


def widen_back(where, u, x, gains, part, got, normed, hidden, wi, wo, first, rows, columns, after=()):
    r2, feat = u.shape
    wide = 2 * feat
    tile = 384
    n = feat // 4

    def kernel(
        where_ref, u_ref, x_ref, gains_ref, part_ref, got_ref, normed_ref, hidden_ref, wi_ref, wo_ref,
        u2_ref, out_ref, low_ref, *more,
    ):
        outs, (ulow_ref, turned_ref, wis_ref, wos_ref, sems) = more[:-5], more[-5:]
        slope = add_both(part_ref[...], got_ref[...], rows)
        u2 = u_ref[...] + norm_back(x_ref[...], gains_ref[pl.ds(2, 1), :], slope)[0]
        u2_ref[...] = u2
        ulow_ref[...] = u2.astype(BF)
        turned_ref[...] = normed_ref[...].T
        out_ref[...] = jnp.zeros_like(out_ref)

        @pl.loop(0, wide // tile)
        def _(t):
            at = pl.ds(pl.multiple_of(t * tile, 128), tile)
            ulow = ulow_ref[...]
            act, dact = gelu_both(hidden_ref[:, at])
            hs = (dact * dot_t(ulow, wo_ref[at, :])).astype(BF)
            wos_ref[at, :] = t_dot(act.astype(BF), ulow).astype(BF)
            wis_ref[:, at] = dot(turned_ref[...], hs).astype(BF)
            out_ref[...] += dot_t(hs, wi_ref[:, at])

        copies = []
        slots = (0, 3 - first, first, 3)

        def add(h, at, size, dst):
            wide_at = pl.ds(pl.multiple_of(at, 16), size)
            deep_at = pl.ds(pl.multiple_of(at + h * feat, 16), size)
            for i, src in enumerate((wis_ref.at[wide_at, pl.ds(h * feat, feat)], wos_ref.at[deep_at])):
                copies.append(pltpu.make_async_copy(src, dst.at[i], sems.at[len(copies)]))

        for i, j in enumerate(slots):
            to = (where_ref[1] ^ j) * n
            add(0, to, n, outs[i // 2].at[i % 2])
            if columns:
                for c in range(4):
                    add(1, to + c * (n // 4), n // 4, outs[2].at[c, i])
            else:
                add(1, to, n, outs[2 + i // 2].at[i % 2])
        start_all(copies)
        low_ref[...] = out_ref[...].astype(BF)
        wait_all(copies)

    block = ((2, 2, n, feat), BF, HB)
    more = [((4, 4, 2, n // 4, feat), BF, HB)] if columns else [block] * 2
    return call(
        kernel,
        [((r2, feat), F32, VM), ((r2, feat), F32, VM), ((r2, feat), BF, VM)] + [block] * 2 + more,
        [
            (where, SM), (u, VM), (x, VM), (gains, VM), (part, VM), (got, VM), (normed, VM),
            (hidden, VM), (wi, VM), (wo, VM),
        ],
        scratch=[
            pltpu.VMEM((r2, feat), BF), pltpu.VMEM((feat, r2), BF), pltpu.VMEM((feat, wide), BF),
            pltpu.VMEM((wide, feat), BF), pltpu.SemaphoreType.DMA((40,)),
        ],
        after=after,
        flops=10 * r2 * feat * wide,
        bytes_accessed=24 * 2**20,
    )


def attend_proj_back(where, dq, own, got, normed, w, wps, small, firsts, rows, last, after=()):
    r2, feat = normed.shape
    half = feat // 2
    n, m = feat // 4, half // 4
    tile = 384
    extra = 0 if small is None else n // 3

    def kernel(where_ref, dq_ref, own_ref, got_ref, normed_ref, w_ref, wps_ref, *refs):
        refs = list(refs)
        take = lambda k: [refs.pop(0) for _ in range(k)]
        small_ref = take(1)[0] if extra else None
        out_ref, low_ref = take(2)
        sides = [take(2) for _ in firsts]
        packed_ref, turned_ref, ws_ref, sm_ref, sems = take(5)
        packed_ref[:, :half] = dq_ref[...]
        packed_ref[:, half:] = (own_ref[...] + got_ref[...].astype(F32)).astype(BF)
        out = dot_t(packed_ref[...], w_ref[...])
        out_ref[...] = out[: out_ref.shape[0]]
        low_ref[...] = (out[rows:] if last else out).astype(BF)
        turned_ref[...] = normed_ref[...].T

        @pl.loop(0, 3 * half // tile)
        def _(t):
            at = pl.ds(pl.multiple_of(t * tile, 128), tile)
            ws_ref[:, at] = dot(turned_ref[...], packed_ref[:, at]).astype(BF)

        if extra:
            wide = jnp.concatenate(
                [small_ref[...], jnp.zeros((128 - small_ref.shape[0], feat), F32)], 0
            )
            sm_ref[...] = wide.T.astype(BF)
        copies = []

        def add(src, dst):
            copies.append(pltpu.make_async_copy(src, dst, sems.at[len(copies)]))

        for lane, first in enumerate(firsts):
            one = len(firsts) == 1
            skip = 2 * n if lane == 1 else 0
            for ref, js in zip(sides[lane], ((0, 3 - first), (first, 3))):
                for i, j in enumerate(js):
                    to = where_ref[1] ^ j
                    at, pat = pl.ds(pl.multiple_of(to * n, 16), n), pl.ds(pl.multiple_of(to * m, 16), m)
                    for g in range(3):
                        if one or (g == 2) == (lane == 1):
                            add(ws_ref.at[at, pl.ds(g * half, half)], ref.at[i, pl.ds(g * n - skip, n)])
                    for g in range(2):
                        if one or lane == 1:
                            add(
                                wps_ref.at[pat, pl.ds(g * half, half)],
                                ref.at[i, pl.ds(3 * n + g * m - skip, m)],
                            )
                    if extra:
                        for g in range(3):
                            sat = pl.ds(pl.multiple_of(to * n + g * extra, 16), extra)
                            add(sm_ref.at[sat], ref.at[i, pl.ds(3 * n + 2 * m, extra), pl.ds(128 * g, 128)])
        start_all(copies)
        wait_all(copies)

    n_out = rows if last else r2
    deep = 3 * n + 2 * m + extra
    deeps = [deep] * 2 if len(firsts) == 1 else [2 * n] * 2 + [n + 2 * m] * 2
    return call(
        kernel,
        [((n_out, feat), F32, VM), ((n_out, feat), BF, VM)] + [((2, k, half), BF, HB) for k in deeps],
        [(where, SM), (dq, VM), (own, VM), (got, VM), (normed, VM), (w, VM), (wps, VM)]
        + ([(small, VM)] if extra else []),
        scratch=[
            pltpu.VMEM((r2, 3 * half), BF), pltpu.VMEM((feat, r2), BF), pltpu.VMEM((feat, 3 * half), BF),
            pltpu.VMEM((feat, 128), BF), pltpu.SemaphoreType.DMA((32,)),
        ],
        after=after,
        flops=4 * r2 * feat * 3 * half,
        bytes_accessed=10 * 2**20,
    )


def join_upstream(u_own, u_sib, rows):
    feat = u_own.shape[1]

    def kernel(o_ref, s_ref, u_ref, low_ref):
        u_ref[pl.ds(0, rows), :] = o_ref[...]
        u_ref[pl.ds(rows, rows), :] = s_ref[...].astype(F32)
        low_ref[pl.ds(0, rows), :] = o_ref[...].astype(BF)
        low_ref[pl.ds(rows, rows), :] = s_ref[...]

    return call(
        kernel, [((2 * rows, feat), F32, VM), ((2 * rows, feat), BF, VM)], [(u_own, VM), (u_sib, VM)],
        bytes_accessed=2**21,
    )


def norm_step(u, x, gains, gain_row, part, got, rows, last, after=()):
    feat = x.shape[1]
    n = rows if last else 2 * rows

    def kernel(u_ref, x_ref, gains_ref, part_ref, got_ref, *outs):
        if last:
            slope = part_ref[...] + got_ref[...].astype(F32)
        else:
            slope = add_both(part_ref[...], got_ref[...], rows)
        u2 = u_ref[:n] + norm_back(x_ref[:n], gains_ref[pl.ds(gain_row, 1), :], slope)[0]
        low = outs[-1]
        low[...] = u2[: low.shape[0]].astype(BF)
        if not last:
            outs[0][...] = u2

    outs = [((last if last else n, feat), BF, VM)]
    return call(
        kernel,
        outs if last else [((n, feat), F32, VM)] + outs,
        [(u, VM), (x, VM), (gains, VM), (part, VM), (got, VM)],
        after=after,
        bytes_accessed=6 * 2**20,
    )


def picks(index, turn, cap, cap_rows, experts):
    at = lax.broadcasted_iota(jnp.int32, (1, experts * cap_rows), 1)
    out = []
    for k in range(TOP):
        chosen, slot = index[:, k : k + 1], index[:, TOP + k : TOP + k + 1]
        place = chosen if turn is None else chosen ^ turn
        target = jnp.where(slot < cap, place * cap_rows + slot, -1)
        out.append(jnp.where(at == target, 1.0, 0.0).astype(BF))
    return out


def lane_at(index, k):
    lane = lax.broadcasted_iota(jnp.int32, (1, 128), 1)
    return jnp.where(lane == index[:, k : k + 1] + 4, 1.0, 0.0)


def present_mask(blk, rows, blk_len, longest):
    pos = lax.broadcasted_iota(jnp.int32, (rows, 1), 0)
    last = jnp.where(blk < longest, blk_len, blk_len - 1)
    return jnp.where(pos < last, 1.0, 0.0)


def route(where, x, part, got, gains, small, cot, index, experts, cap, rows, blk_len, longest, fast, after=()):
    feat = x.shape[1]
    cap_rows = up16(cap)

    def kernel(where_ref, x_ref, part_ref, got_ref, gains_ref, small_ref, cot_ref, index_ref,
               x3_ref, moe_ref, gates_ref, up_ref, *blocks):
        x3 = x_ref[:rows] + part_ref[:rows] + got_ref[...].astype(F32)
        x3_ref[...] = x3
        moe = layer_norm(x3, gains_ref[pl.ds(3, 1), :])
        moe_ref[...] = moe
        lane = lax.broadcasted_iota(jnp.int32, (1, 128), 1)
        logits = dot(moe, small_ref[...])
        logits = jnp.where((lane >= 4) & (lane < 4 + experts), logits, -1e30)
        ex = jnp.exp(logits - jnp.max(logits, -1, keepdims=True))
        gates = ex / jnp.sum(ex, -1, keepdims=True)
        gates_ref[...] = gates
        up_ref[...] = jnp.zeros_like(up_ref)
        up_ref[pl.ds(0, blk_len), :] = cot_ref[...].astype(F32)
        up = up_ref[...] * present_mask(where_ref[0], rows, blk_len, longest)
        up_ref[...] = up
        index = index_ref[...]
        pick = picks(index, where_ref[1] if fast else None, cap, cap_rows, experts)
        sent = t_dot(pick[0] + pick[1], moe).astype(BF)
        slope = 0.0
        for k in range(TOP):
            gate = jnp.sum(gates * lane_at(index, k), -1, keepdims=True)
            slope += t_dot(pick[k], (gate * up).astype(BF))
        slope = slope.astype(BF)
        for j, ref in enumerate(blocks):
            ref[pl.ds(0, cap_rows), :] = sent[j * cap_rows : (j + 1) * cap_rows]
            ref[pl.ds(cap_rows, cap_rows), :] = slope[j * cap_rows : (j + 1) * cap_rows]

    return call(
        kernel,
        [((rows, feat), F32, VM), ((rows, feat), BF, VM), ((rows, 128), F32, VM), ((rows, feat), F32, VM)]
        + [((2 * cap_rows, feat), BF, VM)] * experts,
        [(where, SM), (x, VM), (part, VM), (got, VM), (gains, VM), (small, VM), (cot, VM), (index, VM)],
        after=after,
        flops=6 * rows * experts * cap_rows * feat,
        bytes_accessed=5 * 2**20,
    )


def experts_forward(blocks, own, sib, cap_rows, after=()):
    feat, wide = own[0].shape
    tile = 512 if wide % 512 == 0 else wide
    n = len(blocks) * cap_rows
    steps = wide // tile

    def kernel(*refs):
        refs = list(refs)
        take = lambda k: [refs.pop(0) for _ in range(k)]
        ins, weights = take(len(blocks)), take(4)
        take(len(after))
        outs = take(len(blocks))
        rows_ref, slope_ref, res_ref, back_ref = take(4)
        t = pl.program_id(0)

        @pl.when(t == 0)
        def _():
            for j, ref in enumerate(ins):
                at = pl.ds(j * cap_rows, cap_rows)
                rows_ref[at, :] = ref[pl.ds(0, cap_rows), :]
                slope_ref[at, :] = ref[pl.ds(cap_rows, cap_rows), :]
            res_ref[...] = jnp.zeros_like(res_ref)
            back_ref[...] = jnp.zeros_like(back_ref)

        def step(wi_ref, wo_ref):
            act, dact = gelu_both(dot(rows_ref[...], wi_ref[...]))
            hs = (dact * dot_t(slope_ref[...], wo_ref[...])).astype(BF)
            res_ref[...] += dot(act.astype(BF), wo_ref[...])
            back_ref[...] += dot_t(hs, wi_ref[...])

        @pl.when(t < steps)
        def _():
            step(*weights[:2])

        @pl.when(t >= steps)
        def _():
            step(*weights[2:])

        @pl.when(t == 2 * steps - 1)
        def _():
            for j, ref in enumerate(outs):
                at = pl.ds(j * cap_rows, cap_rows)
                ref[pl.ds(0, cap_rows), :] = res_ref[at, :].astype(BF)
                ref[pl.ds(cap_rows, cap_rows), :] = back_ref[at, :].astype(BF)

    blk = (2 * cap_rows, feat)
    whole = pl.BlockSpec(blk, lambda t: (0, 0))
    first = lambda t: jnp.minimum(t, steps - 1)
    later = lambda t: jnp.maximum(t - steps, 0)
    specs = []
    for place in (first, later):
        specs.append(pl.BlockSpec((feat, tile), lambda t, place=place: (0, place(t))))
        specs.append(pl.BlockSpec((tile, feat), lambda t, place=place: (place(t), 0)))
    return pl.pallas_call(
        kernel,
        grid=(2 * steps,),
        out_shape=[jax.ShapeDtypeStruct(blk, BF)] * len(blocks),
        in_specs=[whole] * len(blocks) + specs + [HB] * len(after),
        out_specs=[whole] * len(blocks),
        scratch_shapes=[
            pltpu.VMEM((n, feat), BF), pltpu.VMEM((n, feat), BF),
            pltpu.VMEM((n, feat), F32), pltpu.VMEM((n, feat), F32),
        ],
        compiler_params=pltpu.CompilerParams(
            vmem_limit_bytes=50 * 2**20, dimension_semantics=("arbitrary",)
        ),
        cost_estimate=pl.CostEstimate(
            flops=16 * n * feat * wide, bytes_accessed=20 * 2**20, transcendentals=0
        ),
    )(*blocks, *own, *sib, *after)


def expert_slopes(every, w_in, w_out, got, after=()):
    feat, wide = w_in.shape
    tile = 512 if wide % 512 == 0 else wide
    steps = wide // tile
    groups, experts, cap_rows = every.shape[0], every.shape[1], every.shape[2] // 2
    total = groups * experts * cap_rows
    kind = BF if got is None else F32

    def kernel(*refs):
        refs = list(refs)
        take = lambda k: [refs.pop(0) for _ in range(k)]
        every_ref, wi_ref, wo_ref = take(3)
        got_refs = take(2) if got is not None else None
        take(len(after))
        wis_ref, wos_ref, rows_ref, slope_ref, turned_ref, sems = take(6)

        @pl.when(pl.program_id(0) == 0)
        def _():
            copies = []
            for k in range(groups):
                for j in range(experts):
                    at = pl.ds((k * experts + j) * cap_rows, cap_rows)
                    for i, ref in enumerate((rows_ref, slope_ref)):
                        copies.append(pltpu.make_async_copy(
                            every_ref.at[k, j, pl.ds(i * cap_rows, cap_rows)], ref.at[at],
                            sems.at[len(copies)],
                        ))
            start_all(copies)
            per = total // groups
            for k in range(groups):
                wait_all(copies[k * 2 * experts : (k + 1) * 2 * experts])
                at = pl.ds(k * per, per)
                turned_ref[:, at] = rows_ref[at, :].T

        act, dact = gelu_both(dot(rows_ref[...], wi_ref[...]))
        hs = (dact * dot_t(slope_ref[...], wo_ref[...])).astype(BF)
        wis = dot(turned_ref[...], hs)
        wos = t_dot(act.astype(BF), slope_ref[...])
        if got is not None:
            wis, wos = wis + got_refs[0][...].astype(F32), wos + got_refs[1][...].astype(F32)
        wis_ref[...] = wis.astype(kind)
        wos_ref[...] = wos.astype(kind)

    wi_spec = pl.BlockSpec((feat, tile), lambda t: (0, t))
    wo_spec = pl.BlockSpec((tile, feat), lambda t: (t, 0))
    return pl.pallas_call(
        kernel,
        grid=(steps,),
        out_shape=[jax.ShapeDtypeStruct((feat, wide), kind), jax.ShapeDtypeStruct((wide, feat), kind)],
        in_specs=[HB] + [wi_spec, wo_spec] * (1 if got is None else 2) + [HB] * len(after),
        out_specs=[wi_spec, wo_spec],
        scratch_shapes=[
            pltpu.VMEM((total, feat), BF), pltpu.VMEM((total, feat), BF), pltpu.VMEM((feat, total), BF),
            pltpu.SemaphoreType.DMA((2 * groups * experts,)),
        ],
        compiler_params=pltpu.CompilerParams(
            vmem_limit_bytes=56 * 2**20, dimension_semantics=("arbitrary",)
        ),
        cost_estimate=pl.CostEstimate(
            flops=8 * total * feat * wide, bytes_accessed=20 * 2**20, transcendentals=0
        ),
    )(every, w_in, w_out, *(got or ()), *after)


def combine(where, blocks, x3, moe, gates, up, index, small, gains, small_rows, experts, cap, rows, blk_len, longest, fast, after=()):
    feat = x3.shape[1]
    cap_rows = up16(cap)
    n = experts * cap_rows

    def kernel(where_ref, *refs):
        refs = list(refs)
        take = lambda k: [refs.pop(0) for _ in range(k)]
        ins = take(experts)
        x3_ref, moe_ref, gates_ref, up_ref, index_ref, small_ref, gains_ref = take(7)
        acts_ref, u_ref, low_ref, slopes_ref, result_ref, back_ref = take(6)
        for j, ref in enumerate(ins):
            at = pl.ds(j * cap_rows, cap_rows)
            result_ref[at, :] = ref[pl.ds(0, cap_rows), :]
            back_ref[at, :] = ref[pl.ds(cap_rows, cap_rows), :]
        index, gates, up, moe = index_ref[...], gates_ref[...], up_ref[...], moe_ref[...]
        pick = picks(index, where_ref[1] if fast else None, cap, cap_rows, experts)
        x3 = x3_ref[...]
        acts, all_slope = x3, 0.0
        for k in range(TOP):
            at_k = lane_at(index, k)
            gate = jnp.sum(gates * at_k, -1, keepdims=True)
            picked = dot(pick[k], result_ref[...])
            acts = acts + gate * picked
            all_slope += jnp.sum(up * picked, -1, keepdims=True) * at_k
        acts = acts * present_mask(where_ref[0], rows, blk_len, longest)
        acts_ref[...] = acts[:blk_len].astype(BF)
        logit = (gates * (all_slope - jnp.sum(gates * all_slope, -1, keepdims=True))).astype(BF)
        slope = dot(pick[0] + pick[1], back_ref[...]) + dot_t(logit, small_ref[...])
        dx, terms = norm_back(x3, gains_ref[pl.ds(3, 1), :], slope)
        u = up + dx
        u_ref[...] = u
        low_ref[...] = u.astype(BF)
        slopes_ref[...] = t_dot(logit, moe)[:small_rows]
        slopes_ref[pl.ds(3, 1), :] = jnp.sum(terms, 0, keepdims=True)

    return call(
        kernel,
        [((blk_len, feat), BF, VM), ((rows, feat), F32, VM), ((rows, feat), BF, VM), ((small_rows, feat), F32, VM)],
        [(where, SM)] + [(b, VM) for b in blocks]
        + [(t, VM) for t in (x3, moe, gates, up, index, small, gains)],
        scratch=[pltpu.VMEM((n, feat), BF), pltpu.VMEM((n, feat), BF)],
        after=after,
        flops=6 * rows * n * feat,
        bytes_accessed=5 * 2**20,
    )


def tie(xs, *after):
    return list(lax.optimization_barrier((*xs, *after)))[: len(xs)]


class Links:
    def __init__(self, mesh):
        self.E = mesh.shape["expert"]
        self.C = mesh.shape["context"]
        self.D = mesh.shape["dp"]
        assert self.C == 4 and self.D == 2 and self.E % 2 == 0
        self.fast = self.E == 4
        self.chips = self.E * self.C
        flat = lambda e, c, d: (e * self.C + c) * self.D + d
        self.team = [
            (flat(e, c, d), flat((e // 2) * 2 + c // 2, 2 * (e % 2) + d, c % 2))
            for e in range(self.E)
            for c in range(self.C)
            for d in range(self.D)
        ]
        self.to_lane = [(f, (f % self.chips) * 2 + f // self.chips) for f in range(2 * self.chips)]
        self.from_lane = [(b, a) for a, b in self.to_lane]

    def move(self, x):
        return lax.ppermute(x, ALL, self.team)

    def xor(self, x, axis, j):
        n = {"expert": self.E, "context": self.C, "dp": self.D}[axis]
        return lax.ppermute(x, axis, [(i, i ^ j) for i in range(n)])

    def sib(self, x):
        return self.xor(x, "dp", 1)

    def partner(self, x):
        return self.xor(x, "expert", 1)

    def column(self, x, *hold):
        c = lax.axis_index("context")
        got = tie([x] + [self.xor(x, "context", j) for j in range(1, 4)], *hold)
        pick = lambda k: jnp.where(
            c & 2 == 0, jnp.where(c & 1 == 0, got[k], got[k ^ 1]), jnp.where(c & 1 == 0, got[k ^ 2], got[k ^ 3])
        )
        return jnp.stack([pick(k) for k in range(4)])

    def plane_sum(self, keep, send, first, hold):
        (got,) = tie([self.xor(send, "expert", first)], *hold[0])
        got = got.astype(F32)
        give = (keep[1].astype(F32) + got[1]).astype(BF)
        (far,) = tie([self.xor(give, "expert", 3 - first)], *hold[1])
        return keep[0].astype(F32) + got[0] + far.astype(F32), give

    def column_sum(self, x, *hold):
        c = lax.axis_index("context")
        low = x.astype(BF)
        got = [self.xor(lax.dynamic_index_in_dim(low, c ^ j, 0, False), "context", j) for j in range(1, 4)]
        got = tie(got, *hold)
        total = lax.dynamic_index_in_dim(x, c, 0, False)
        for t in got:
            total = total + t.astype(F32)
        return total

    def swap_blocks(self, x):
        if not self.fast:
            return list(lax.all_to_all(jnp.stack(x), "expert", 0, 0, tiled=True))
        return [x[0]] + [self.xor(x[j], "expert", j) for j in range(1, 4)]


def lane_rows(links, mine, d):
    keep = lax.dynamic_index_in_dim(mine, d, 0, False)
    got = links.sib(lax.dynamic_index_in_dim(mine, 1 - d, 0, False))
    return jnp.where(d == 0, jnp.concatenate([keep, got], 0), jnp.concatenate([got, keep], 0))


def in_order(d, own, other):
    return jnp.where(d == 0, jnp.stack([own, other]), jnp.stack([other, own]))


class Weights:
    def __init__(self, links, rdev, feat, ff):
        self.links, self.rdev, self.feat, self.ff = links, rdev, feat, ff
        self.d = lax.axis_index("dp")
        self.half = feat // 2

    def split_attend(self, w):
        w = w.reshape(self.rdev, 3, 2, self.half).transpose(2, 0, 1, 3)
        return w.reshape(2, self.rdev, 3 * self.half)

    def split_widen(self, w):
        w = w.reshape(self.rdev, self.links.chips, 2, 2, -1).transpose(2, 0, 3, 1, 4)
        return w.reshape(2, self.rdev, self.ff // 2)

    def pack_attend(self, w, p, small):
        parts = [w, jnp.concatenate([p[:, : self.half], p[:, self.half :]], 0)]
        if small is not None:
            parts.append(jnp.pad(small, ((0, 0), (0, 128 - small.shape[1]))))
        return jnp.concatenate(parts, 1)

    def pack_wide(self, wout):
        h = wout.shape[0] // 2
        return jnp.concatenate([wout[:h], wout[h:]], 1)

    def column(self, buf, *hold):
        if self.links.fast:
            return self.links.column(buf, *hold)
        return lax.all_gather(buf, CHIPS, axis=0, tiled=False)

    def cut(self, x):
        return x if self.links.fast else x.reshape(4, -1, x.shape[-1])

    def pack_block(self, quad, between):
        f, h, r = self.feat, self.half, self.rdev
        n = quad.shape[0]
        p = quad[..., f + h : 2 * f].reshape(n, 2, r, h)
        parts = [quad[..., i * h : (i + 1) * h] for i in range(3)] + [p[:, 0], p[:, 1]]
        parts = [self.cut(t.reshape(-1, h)) for t in parts]
        if self.links.fast:
            parts.insert(2, between)
        if quad.shape[2] > 2 * f:
            small = self.cut(quad[..., 2 * f :].reshape(-1, 128))
            small = small.reshape(small.shape[:-2] + (3, -1, 128))
            parts.append(jnp.concatenate([small[..., g, :, :] for g in range(3)], -1))
        return jnp.concatenate(parts, -2)

    def pack_pair(self, quad_in, quad_out):
        f = self.feat
        halves = []
        for i in range(2):
            pair = [self.cut(t[..., i * f : (i + 1) * f].reshape(-1, f)) for t in (quad_in, quad_out)]
            halves.append(jnp.stack(pair, -3))
        return jnp.stack(halves, -4)

    def spread(self, x, cuts, *hold):
        if not self.links.fast:
            return [x[0], x[1], x[2], cuts[0](x[3]), cuts[1](x[3])]
        to = lambda t, j: self.links.xor(t, "expert", j)
        x1, x2 = tie([to(x, 1), to(x, 2)], *hold)
        return [x, x1, x2, to(cuts[0](x1), 2), to(cuts[1](x2), 1)]

    def spread_attend(self, x, skip, *hold):
        n = self.feat // 2 + skip
        return self.spread(x, (lambda t: t[:n], lambda t: t[n:]), *hold)

    def spread_pair(self, x, *hold):
        return self.spread(x, (lambda t: t[0], lambda t: t[1]), *hold)

    def total(self, keep, send, first, hold):
        if self.links.fast:
            out, _ = self.links.plane_sum(keep, send, first, hold)
            return out
        blk = {0: keep[0], 3 - first: keep[1], first: send[0], 3: send[1]}
        return jnp.stack([blk[j] for j in range(4)])

    def all_sum(self, buf):
        return lax.psum_scatter(buf.astype(BF), CHIPS, scatter_dimension=0, tiled=False).astype(F32)

    def exchange(self, w):
        w = w.reshape(2, self.rdev, -1)
        mine = lax.dynamic_index_in_dim(w, self.d, 0, False)
        got = self.links.sib(lax.dynamic_index_in_dim(w, 1 - self.d, 0, False))
        return in_order(self.d, mine, got)

    def to_columns(self, t):
        n, m = self.feat // 4, self.half // 4
        r = self.rdev
        cut = lambda t, k: t.reshape(-1, k * r, t.shape[-1])
        parts = [cut(t[..., g * n : (g + 1) * n, :], 2) for g in range(3)]
        p = [cut(t[..., 3 * n + g * m : 3 * n + (g + 1) * m, :], 1) for g in range(2)]
        parts.append(jnp.concatenate(p, 1))
        if t.shape[-2] > 3 * n + 2 * m:
            sm = t[..., 3 * n + 2 * m :, :]
            sm = jnp.stack([sm[..., 128 * g : 128 * (g + 1)] for g in range(3)], -3)
            parts.append(sm.reshape(-1, 2 * r, 128))
        return jnp.concatenate(parts, 2)

    def owner_attend(self, buf):
        f, h, r = self.feat, self.half, self.rdev
        p = jnp.concatenate([buf[:r, f + h : 2 * f], buf[r:, f + h : 2 * f]], 1)
        p = lax.ppermute(p, ALL, self.links.from_lane)
        w = buf[:, : f + h]
        if buf.shape[1] > 2 * f:
            w = jnp.concatenate([w, buf[:, 2 * f :]], 1)
        w = self.exchange(w)
        extra = w[0, :, f + h :] + w[1, :, f + h :]
        w = w[..., : f + h].reshape(2, r, 3, h).transpose(1, 2, 0, 3).reshape(r, 3 * f)
        return w, p, extra

    def pair_columns(self, t):
        t = t.reshape(2, 4, 2 * self.rdev, self.feat)
        return jnp.concatenate([t[0], t[1]], 2)

    def owner_wide(self, w, w_out):
        r = self.rdev
        w = self.exchange(w).reshape(2, r, 2, self.links.chips, -1)
        return w.transpose(1, 3, 0, 2, 4).reshape(r, self.ff), w_out


def body(links, *args):
    (tokens, cotangent, g1, w1, p1, g2, win, wout, g3, w3, p3, g4, router, ein, eout, routes, slots) = args
    e = lax.axis_index("expert")
    d = lax.axis_index("dp")
    blk_len, feat = tokens.shape[1:]
    rows = up16(blk_len)
    half = feat // 2
    rdev = w1.shape[0]
    ff = win.shape[1]
    longest = LEN - (blk_len - 1) * links.C
    experts = router.shape[1]
    small_rows = (4 + experts + 7) // 8 * 8
    cap = max(2, (5 * TOP * blk_len + 4 * experts - 1) // (4 * experts))
    blk = 2 * (e % 2) + d
    where = jnp.stack([blk, e if links.fast else 0 * e]).astype(jnp.int32)
    wt = Weights(links, rdev, feat, ff)
    img = dict(rows=rows, blk_len=blk_len, longest=longest)

    tok = links.move(tokens[0])
    ps = lax.ppermute(jnp.concatenate([p1, p3], 0), ALL, links.to_lane)
    small = jnp.concatenate([g1[:, None], g2[:, None], g3[:, None], g4[:, None], router], 1)
    gsm = small.shape[1]
    lane1 = jnp.concatenate(
        [wt.split_attend(w1), jnp.broadcast_to(small[None], (2, rdev, gsm))], 2
    )
    lane1 = lane_rows(links, lane1, d)
    buf1 = wt.pack_attend(lane1[:, : 3 * half], ps[:rdev], lane1[:, 3 * half :])
    quad1 = wt.column(buf1)
    later = jnp.concatenate([wt.split_widen(win), wt.split_attend(w3)], 2)
    later = lane_rows(links, later, d)
    w_in, w_out = later[:, : ff // 2], wt.pack_wide(wout)
    w3_lane, p3_lane = later[:, ff // 2 :], ps[rdev:]
    block3 = jnp.concatenate(
        [w3_lane[:, g * half : (g + 1) * half] for g in range(3)] + [p3_lane[:, :half], p3_lane[:, half:]], 0
    )
    skip = block3.shape[0] if links.fast else 0
    tok_pair = jnp.stack([tok, links.partner(tok)])
    block1 = wt.pack_block(tie([quad1], tok_pair)[0], block3)
    if links.fast:
        (buf2,) = tie([jnp.concatenate([w_in, w_out], 1)], quad1)
        quad2 = wt.column(buf2)
        blocks1 = wt.spread_attend(block1, skip, quad2)
        (tok_pair,) = tie([tok_pair], *blocks1[1:3])
    else:
        quad2 = None
        blocks1 = wt.spread_attend(block1, skip)
    tok_sib = links.sib(tok_pair)
    toks = [tok_pair[0], tok_sib[0], tok_pair[1], tok_sib[1]]
    cot, raw = tie([cotangent[0].astype(BF), jnp.concatenate([routes[0], slots[0]], 1)], *blocks1[1:3])
    raw, cot = links.move(raw), links.move(cot)
    index = jnp.pad(raw, ((0, rows - blk_len), (0, 0)), constant_values=cap)
    if links.fast:
        (quad2,) = tie([quad2], *blocks1[3:], *toks, cot, index)
        pair2 = wt.pack_pair(quad2[..., : ff // 2], quad2[..., ff // 2 :])
        q, n = feat // 2, block3.shape[0]
        place3 = jnp.stack([t[q : q + n] for t in blocks1[:4]])
        source3 = lax.all_gather(place3, "context", axis=0, tiled=False)
        p3 = source3[:, :, 6 * rdev :].reshape(4, 4, 2, rdev, half)
        p3 = jnp.stack([lax.dynamic_index_in_dim(p3, e ^ k, 1, False) for k in range(4)])
        wp3 = p3.transpose(0, 1, 3, 2, 4).reshape(half, feat)
    else:
        pair2 = wt.pack_pair(wt.column(w_in), wt.column(w_out))
        all3 = lax.all_gather(block3, CHIPS, axis=0, tiled=False)
        source3 = all3[:, : 6 * rdev].reshape(links.chips, 3, 2 * rdev, half)
        source3 = source3.transpose(0, 2, 1, 3).reshape(feat, 3 * half)
        wp3 = all3[:, 6 * rdev :].reshape(links.chips, 2, rdev, half)
        wp3 = wp3.transpose(0, 2, 1, 3).reshape(half, feat)

    x0, normed1, q1, kv1, far1, wa1, wp1, small, gains = attend_first(
        where, toks, small_rows, blocks1, rows, skip
    )
    part, low, blend1, lse1 = attend_core(
        where, q1, kv1, far1, wp1, solo=False, **img
    )
    blocks2 = wt.spread_pair(pair2, part)
    x1, normed2, hidden, part2, low2, wi, wo = widen_forward(
        where, x0, part, links.sib(low), gains, blocks2, rows
    )
    x2, normed3, own3 = norm_next(x1, part2, links.sib(low2), gains, 2, rows)
    ein_own, eout_own = ein[0], eout[0]
    ein_sib, eout_sib = [links.sib(t) for t in tie([ein_own, eout_own], x1)]
    far_own = links.partner(own3)
    q3, kv3, wa3 = attend_next(where, normed3, source3)
    (far_own,) = tie([far_own], q3)
    part3, low3, blend3, lse3, far3 = attend_core(
        where, q3, kv3, None, wp3, solo=True, far=(far_own, links.sib(far_own), wa3),
        after=(ein_sib, eout_sib), **img
    )
    moe_args = dict(experts=experts, cap=cap, fast=links.fast, **img)
    x3, moe, gates, up, *sent = route(
        where, x2, part3, links.sib(low3), gains, small, cot, index, **moe_args
    )
    came = links.swap_blocks(sent)
    every = lax.all_gather(jnp.stack(came), "context", axis=0, tiled=False)
    answer = experts_forward(came, (ein_own, eout_own), (ein_sib, eout_sib), up16(cap))
    answer = links.swap_blocks(answer)
    acts, u, u_low, small_slopes = combine(
        where, answer, x3, moe, gates, up, index, small, gains, small_rows, **moe_args
    )

    u, u_low = join_upstream(u, links.sib(u_low), rows)
    dq, own, far, wps = attend_core_back(where, u_low, wp3, blend3, q3, kv3, far3, lse3, **img)
    first3, first2, first1 = (1,), 2, (1, 2)
    part, low, *slopes3 = attend_proj_back(
        where, dq, own, links.partner(far), normed3, wa3, wps, small_slopes, first3, rows, False
    )
    u, part, low, *slopes2 = widen_back(
        where, u, x2, gains, part, links.sib(low), normed2, hidden, wi, wo, first2, rows, False
    )
    u1, u_low = norm_step(u, x1, gains, 1, part, links.sib(low), rows, 0)
    dq1, own, far, wps = attend_core_back(where, u_low, wp1, blend1, q1, kv1, far1, lse1, **img)
    part, low, *slopes1 = attend_proj_back(
        where, dq1, own, links.partner(far), normed1, wa1, wps, None, first1, rows, True, after=(every,)
    )
    (u2,) = norm_step(u1, x0, gains, 0, part, links.sib(low), rows, blk_len)
    moved = links.move(jnp.stack([acts, u2]))
    acts, token_slope = moved[0], moved[1]
    e_sib = expert_slopes(every, ein_sib, eout_sib, None, after=(u2,))
    sum3 = wt.total(*slopes3, first3[0], ((low,), (e_sib[0],)))
    sum2a = wt.total(*slopes2[:2], first2, ((low,), (e_sib[0],)))
    sum2b = wt.total(*slopes2[2:], first2, ((e_sib[0],), ()))
    sum1 = [wt.total(*slopes1[2 * i : 2 * i + 2], first1[i], ((e_sib[0],), ())) for i in range(2)]
    col3, col1 = wt.to_columns(sum3), wt.to_columns(jnp.concatenate(sum1, -2))
    if links.fast:
        col2a, col2b = wt.pair_columns(sum2a), wt.pair_columns(sum2b)
        early = jnp.concatenate([col3, col2a], 2).astype(BF)
        early = lax.psum_scatter(tie([early], every)[0], "context", scatter_dimension=0, tiled=False)
        early = early.astype(F32)
        col3, col2a = early[:, : col3.shape[2]], early[:, col3.shape[2] :]
        late = jnp.concatenate([col2b, col1], 2)
        e_slopes = expert_slopes(every, ein_own, eout_own, [links.sib(t) for t in e_sib], after=(late,))
        late = links.column_sum(late, e_slopes[0])
        col2b, col1 = late[:, : 2 * feat], late[:, 2 * feat :]
        w2 = jnp.concatenate([col2a[:, :feat], col2b[:, :feat]], 1)
        w2_out = jnp.concatenate([col2a[:, feat:], col2b[:, feat:]], 0)
    else:
        e_slopes = expert_slopes(every, ein_own, eout_own, [links.sib(t) for t in e_sib])
        col3, col1 = wt.all_sum(col3), wt.all_sum(col1)
        hid = ff // (4 * links.chips)
        w2 = [t[..., 0, :, :].reshape(-1, 2 * rdev, feat) for t in (sum2a, sum2b)]
        w2_out = [t[..., 1, :, :].reshape(-1, hid, feat) for t in (sum2a, sum2b)]
        w2, w2_out = [wt.all_sum(jnp.concatenate(t, 2)) for t in (w2, w2_out)]
        w2_out = jnp.concatenate([w2_out[:, :feat], w2_out[:, feat:]], 0)
    w3_out, p3_out, extra = wt.owner_attend(col3)
    win_out, wout_out = wt.owner_wide(w2, w2_out)
    w1_out, p1_out, _ = wt.owner_attend(col1)

    def gain_slope(w, slope, gain):
        return jnp.sum(w.astype(F32) * slope, 1) / gain.astype(F32)

    return (
        acts.astype(F32)[None], token_slope.astype(F32)[None],
        gain_slope(w1, w1_out, g1), w1_out, p1_out, gain_slope(win, win_out, g2), win_out, wout_out,
        gain_slope(w3, w3_out, g3), w3_out, p3_out, extra[:, 3], extra[:, 4 : 4 + experts],
        e_slopes[0][None], e_slopes[1][None],
    )


def solution(mesh):
    links = Links(mesh)
    tok = P(("expert", "dp"), "context", None)
    vec, mat = P(ALL), P(ALL, None)
    ein, eout = P("expert", None, "dp"), P("expert", "dp", None)
    dense = (vec, mat, mat, vec, mat, mat, vec, mat, mat, vec, mat, ein, eout)
    return jax.shard_map(
        functools.partial(body, links),
        mesh=mesh,
        in_specs=(tok, tok) + dense + (tok, tok),
        out_specs=(tok, tok) + dense,
        check_vma=False,
    )
```

```python
import functools

import jax
import jax.numpy as jnp
from jax import lax
from jax.experimental import pallas as pl
from jax.experimental.pallas import tpu as pltpu
from jax.sharding import PartitionSpec as P

HEADS = 12
HEAD_DIM = 64
LEN = 577
TOP = 2
ALL = ("expert", "context", "dp")
CHIPS = ("expert", "context")
BF = jnp.bfloat16
F32 = jnp.float32
VM = pl.BlockSpec(memory_space=pltpu.VMEM)
HB = pl.BlockSpec(memory_space=pl.ANY)
SM = pl.BlockSpec(memory_space=pltpu.SMEM)


def up16(n):
    return (n + 15) // 16 * 16


def dot(a, b):
    return jnp.dot(a, b, preferred_element_type=F32)


def dot_t(a, b):
    return lax.dot_general(a, b, (((1,), (1,)), ((), ())), preferred_element_type=F32)


def t_dot(a, b):
    return lax.dot_general(a, b, (((0,), (0,)), ((), ())), preferred_element_type=F32)


def call(kernel, outs, ins, scratch=(), after=(), flops=0, bytes_accessed=0, grid=()):
    n_in, n_after = len(ins), len(after)

    def run(*refs):
        kernel(*refs[:n_in], *refs[n_in + n_after :])

    return pl.pallas_call(
        run,
        grid=grid,
        out_shape=[jax.ShapeDtypeStruct(s, t) for s, t, _ in outs],
        in_specs=[s for _, s in ins] + [HB] * n_after,
        out_specs=[s for _, _, s in outs],
        scratch_shapes=list(scratch),
        compiler_params=pltpu.CompilerParams(vmem_limit_bytes=50 * 2**20),
        cost_estimate=pl.CostEstimate(
            flops=flops, bytes_accessed=bytes_accessed, transcendentals=0
        ),
    )(*[a for a, _ in ins], *after)


def norm_parts(x):
    mean = jnp.mean(x, -1, keepdims=True)
    centre = x - mean
    scale = lax.rsqrt(jnp.mean(centre * centre, -1, keepdims=True) + 1e-06)
    return centre * scale, scale


def layer_norm(x, gain):
    return (norm_parts(x)[0] * gain).astype(BF)


def norm_back(x, gain, slope):
    unit, scale = norm_parts(x)
    terms = slope * unit
    inner = slope * gain
    inner = inner - jnp.mean(inner, -1, keepdims=True) - unit * jnp.mean(inner * unit, -1, keepdims=True)
    return inner * scale, terms


def gelu_both(h):
    k = 0.7978845608028654
    t = jnp.tanh(k * (h + 0.044715 * h * h * h))
    half = 0.5 * (1 + t)
    return h * half, half + 0.5 * h * (1 - t * t) * (k + (3 * 0.044715 * k) * h * h)


def add_both(mine, got, rows):
    return mine + jnp.concatenate([got[rows:], got[:rows]], 0).astype(F32)


def pair_masks():
    lane = lax.broadcasted_iota(jnp.int32, (1, 2 * HEAD_DIM), 1)
    return [(lane < HEAD_DIM).astype(BF), (lane >= HEAD_DIM).astype(BF)]


def key_mask(blk, rows, blk_len, longest):
    pos = lax.broadcasted_iota(jnp.int32, (rows, 1), 0)
    parts = []
    for j in range(4):
        last = jnp.where((blk ^ j) < longest, blk_len, blk_len - 1)
        parts.append(pos < last)
    return jnp.concatenate([jnp.where(p, 1.0, 0.0) for p in parts], 0) > 0.5


def attend_core(where, q, kv_own, kv_far, wp, rows, blk_len, longest, solo, far=None, after=()):
    half = q.shape[1]
    feat = wp.shape[1]
    pairs = half // (2 * HEAD_DIM)
    r2 = 2 * rows

    def kernel(where_ref, q_ref, ko_ref, *refs):
        refs = list(refs)
        take = lambda n: [refs.pop(0) for _ in range(n)]
        given = take(1 if far is None else 3)
        wp_ref, part_ref, low_ref, blend_ref, lse_ref = take(5)
        if far is None:
            kf_ref = given[0]
        else:
            (kf_ref,) = take(1)
            for j in range(2):
                kf_ref[pl.ds(j * rows, rows), :] = dot(given[j][...], given[2][:, half:]).astype(BF)
        ok = key_mask(where_ref[0], rows, blk_len, longest)
        masks = pair_masks()
        for p in range(pairs):
            at, vat = pl.ds(p * 128, 128), pl.ds(half + p * 128, 128)
            k = jnp.concatenate([ko_ref[:, at], kf_ref[:, at]], 0)
            v = jnp.concatenate([ko_ref[:, vat], kf_ref[:, vat]], 0)
            qp = q_ref[:, at]
            acc = None
            for h in range(2):
                s = dot_t(k, qp * masks[h]) * 0.125
                s = jnp.where(ok, s, -1e9)
                top = jnp.max(s, 0, keepdims=True)
                ex = jnp.exp(s - top)
                total = jnp.sum(ex, 0, keepdims=True)
                lse_ref[pl.ds(2 * p + h, 1), :] = top + jnp.log(total)
                shares = (ex * (1.0 / total)).astype(BF)
                out = t_dot(v * masks[h], shares)
                acc = out if acc is None else acc + out
            blend_ref[at, :] = acc.astype(BF)
        part = t_dot(blend_ref[...], wp_ref[...])
        part_ref[...] = part
        low_ref[...] = (part[rows:] if solo else part).astype(BF)

    outs = [
        ((r2, feat), F32, VM), ((rows if solo else r2, feat), BF, VM), ((half, r2), BF, VM), ((8, r2), F32, VM),
    ]
    ins = [(where, SM), (q, VM), (kv_own, VM)]
    if far is None:
        ins.append((kv_far, VM))
    else:
        ins += [(t, VM) for t in far]
        outs.append(((r2, feat), BF, VM))
    return call(
        kernel,
        outs,
        ins + [(wp, VM)],
        after=after,
        flops=2 * r2 * half * (8 * rows + feat),
        bytes_accessed=4 * 2**20,
    )


def attend_core_back(where, u_low, wp, blend, q, kv_own, kv_far, lse, rows, blk_len, longest, after=()):
    half = q.shape[1]
    feat = wp.shape[1]
    pairs = half // (2 * HEAD_DIM)
    r2 = 2 * rows

    def kernel(
        where_ref, u_ref, wp_ref, blend_ref, q_ref, ko_ref, kf_ref, lse_ref,
        dq_ref, own_ref, far_ref, wps_ref, bt_ref, dqt_ref,
    ):
        ok = key_mask(where_ref[0], rows, blk_len, longest)
        masks = pair_masks()
        sub = lax.broadcasted_iota(jnp.int32, (2 * HEAD_DIM, 1), 0)
        row_masks = [(sub < HEAD_DIM).astype(BF), (sub >= HEAD_DIM).astype(BF)]
        u = u_ref[...]
        bt_ref[...] = dot_t(wp_ref[...], u).astype(BF)
        for p in range(pairs):
            at, vat = pl.ds(p * 128, 128), pl.ds(half + p * 128, 128)
            k = jnp.concatenate([ko_ref[:, at], kf_ref[:, at]], 0)
            v = jnp.concatenate([ko_ref[:, vat], kf_ref[:, vat]], 0)
            qp = q_ref[:, at]
            bt = bt_ref[at, :]
            dqt = dk = dv = 0.0
            for h in range(2):
                qm = qp * masks[h]
                s = dot_t(k, qm) * 0.125
                shares = jnp.where(ok, jnp.exp(s - lse_ref[pl.ds(2 * p + h, 1), :]), 0.0)
                slope = dot(v * masks[h], bt)
                t = shares * slope
                ss = (t - shares * jnp.sum(t, 0, keepdims=True)).astype(BF)
                dqt += t_dot(k * masks[h], ss)
                dk += dot(ss, qm)
                dv += dot_t(shares.astype(BF), bt * row_masks[h])
            dqt_ref[at, :] = dqt * 0.125
            dk = dk * 0.125
            own_ref[:, at] = dk[:r2]
            own_ref[:, vat] = dv[:r2]
            far_ref[:, at] = dk[r2:].astype(BF)
            far_ref[:, vat] = dv[r2:].astype(BF)
        dq_ref[...] = dqt_ref[...].T.astype(BF)
        wps_ref[...] = dot(blend_ref[...], u).astype(BF)

    return call(
        kernel,
        [
            ((r2, half), BF, VM), ((r2, 2 * half), F32, VM), ((r2, 2 * half), BF, VM),
            ((half, feat), BF, VM),
        ],
        [
            (where, SM), (u_low, VM), (wp, VM), (blend, VM), (q, VM), (kv_own, VM), (kv_far, VM),
            (lse, VM),
        ],
        scratch=[pltpu.VMEM((half, r2), BF), pltpu.VMEM((half, r2), F32)],
        after=after,
        flops=2 * r2 * half * (20 * rows + 2 * feat),
        bytes_accessed=6 * 2**20,
    )


def start_all(copies):
    for c in copies:
        c.start()


def wait_all(copies):
    for c in copies:
        c.wait()


def attend_copies(e, refs, w_ref, p_ref, small_ref, sems, skip):
    copies = []

    def add(src, dst):
        copies.append(pltpu.make_async_copy(src, dst, sems.at[len(copies)]))

    n = w_ref.shape[0] // 4
    half = p_ref.shape[0]
    m = half // 4
    for j in range(4):
        to = e ^ j
        rows, prows = pl.ds(pl.multiple_of(to * n, 16), n), pl.ds(pl.multiple_of(to * m, 16), m)
        a, b, at = (refs[j], refs[j], 2 * n + skip) if j < 3 else (refs[3], refs[4], 0)
        for g in range(2):
            add(a.at[pl.ds(g * n, n)], w_ref.at[rows, pl.ds(g * half, half)])
        add(b.at[pl.ds(at, n)], w_ref.at[rows, pl.ds(2 * half, half)])
        add(b.at[pl.ds(at + n, m)], p_ref.at[prows, pl.ds(0, half)])
        add(b.at[pl.ds(at + n + m, m)], p_ref.at[prows, pl.ds(half, half)])
        if small_ref is not None:
            for g in range(3):
                srows = pl.ds(pl.multiple_of(to * n + g * (n // 3), 16), n // 3)
                add(b.at[pl.ds(at + n + 2 * m, n // 3), pl.ds(128 * g, 128)], small_ref.at[srows])
    return copies


def attend_first(where, tokens, small_rows, blocks, rows, skip, after=()):
    blk_len, feat = tokens[0].shape
    half = feat // 2
    r2 = 2 * rows

    def kernel(where_ref, *refs):
        refs = list(refs)
        take = lambda n: [refs.pop(0) for _ in range(n)]
        tok, block_refs = take(4), take(5)
        x_ref, normed_ref, q_ref, kv_ref, far_ref, w_ref, p_ref, small_ref, rows_ref, all_ref, sems = take(11)
        copies = attend_copies(where_ref[1], block_refs, w_ref, p_ref, small_ref, sems, skip)
        start_all(copies)
        all_ref[...] = jnp.zeros_like(all_ref)
        for j in range(4):
            all_ref[pl.ds(j * rows, blk_len), :] = tok[j][...].astype(F32)
        x = all_ref[...]
        x_ref[...] = x[:r2]
        unit = norm_parts(x)[0]
        wait_all(copies)
        turned = small_ref[...].astype(F32).T
        rows_ref[...] = turned[: rows_ref.shape[0]]
        normed = (unit * turned[0:1]).astype(BF)
        normed_ref[...] = normed[:r2]
        q_ref[...] = dot(normed[:r2], w_ref[:, :half]).astype(BF)
        kv = dot(normed, w_ref[:, half:]).astype(BF)
        kv_ref[...] = kv[:r2]
        far_ref[...] = kv[r2:]

    return call(
        kernel,
        [
            ((r2, feat), F32, VM), ((r2, feat), BF, VM), ((r2, half), BF, VM), ((r2, feat), BF, VM),
            ((r2, feat), BF, VM), ((feat, 3 * half), BF, VM), ((half, feat), BF, VM),
            ((feat, 128), BF, VM), ((small_rows, feat), F32, VM),
        ],
        [(where, SM)] + [(t, VM) for t in tokens] + [(t, HB) for t in blocks],
        scratch=[pltpu.VMEM((2 * r2, feat), F32), pltpu.SemaphoreType.DMA((32,))],
        after=after,
        flops=2 * r2 * feat * 5 * half,
        bytes_accessed=6 * 2**20,
    )


def norm_next(x, part, got, gains, gain_row, rows, after=()):
    r2, feat = x.shape

    def kernel(x_ref, part_ref, got_ref, gains_ref, x2_ref, normed_ref, own_ref):
        x2 = add_both(x_ref[...] + part_ref[...], got_ref[...], rows)
        x2_ref[...] = x2
        normed = layer_norm(x2, gains_ref[pl.ds(gain_row, 1), :])
        normed_ref[...] = normed
        own_ref[...] = normed[:rows]

    return call(
        kernel,
        [((r2, feat), F32, VM), ((r2, feat), BF, VM), ((rows, feat), BF, VM)],
        [(x, VM), (part, VM), (got, VM), (gains, VM)],
        after=after,
        bytes_accessed=5 * 2**20,
    )


def attend_next(where, normed, source, after=()):
    r2, feat = normed.shape
    half = feat // 2
    packed = source.ndim == 4

    def kernel(where_ref, normed_ref, source_ref, q_ref, kv_ref, *more):
        if packed:
            w_ref, sems = more
            r = source_ref.shape[2] // 4
            copies = []
            for c in range(4):
                for j in range(4):
                    at = pl.multiple_of((where_ref[1] ^ j) * (feat // 4) + c * r, 16)
                    for g in range(3):
                        copies.append(pltpu.make_async_copy(
                            source_ref.at[c, j, pl.ds(g * r, r)],
                            w_ref.at[pl.ds(at, r), pl.ds(g * half, half)], sems.at[len(copies)],
                        ))
            start_all(copies)
            wait_all(copies)
        else:
            w_ref = source_ref
        normed = normed_ref[...]
        q_ref[...] = dot(normed, w_ref[:, :half]).astype(BF)
        kv_ref[...] = dot(normed, w_ref[:, half:]).astype(BF)

    out = call(
        kernel,
        [((r2, half), BF, VM), ((r2, feat), BF, VM)] + ([((feat, 3 * half), BF, VM)] if packed else []),
        [(where, SM), (normed, VM), (source, HB if packed else VM)],
        scratch=[pltpu.SemaphoreType.DMA((48,))] if packed else [],
        after=after,
        flops=2 * r2 * feat * 3 * half,
        bytes_accessed=4 * 2**20,
    )
    return out if packed else [*out, source]


def widen_forward(where, x, part, got, gains, blocks, rows, after=()):
    r2, feat = x.shape
    wide = 2 * feat
    tile = 384

    def kernel(
        where_ref, x_ref, part_ref, got_ref, gains_ref, z0, z1, z2, a3, b3,
        x1_ref, normed_ref, hidden_ref, out_ref, low_ref, wi_ref, wo_ref, sems,
    ):
        n = feat // 4
        copies = []
        for h, last in enumerate((a3, b3)):
            pairs = [z0.at[h], z1.at[h], z2.at[h], last]
            for j in range(4):
                at = (where_ref[1] ^ j) * n
                for src, dst in (
                    (pairs[j].at[0], wi_ref.at[pl.ds(pl.multiple_of(at, 16), n), pl.ds(h * feat, feat)]),
                    (pairs[j].at[1], wo_ref.at[pl.ds(pl.multiple_of(at + h * feat, 16), n)]),
                ):
                    copies.append(pltpu.make_async_copy(src, dst, sems.at[len(copies)]))
        start_all(copies)
        x1 = add_both(x_ref[...] + part_ref[...], got_ref[...], rows)
        x1_ref[...] = x1
        normed_ref[...] = layer_norm(x1, gains_ref[pl.ds(1, 1), :])
        wait_all(copies)
        out_ref[...] = jnp.zeros_like(out_ref)

        @pl.loop(0, wide // tile)
        def _(t):
            at = pl.ds(pl.multiple_of(t * tile, 128), tile)
            h = dot(normed_ref[...], wi_ref[:, at])
            hidden_ref[:, at] = h
            out_ref[...] += dot(gelu_both(h)[0].astype(BF), wo_ref[at, :])

        low_ref[...] = out_ref[...].astype(BF)

    return call(
        kernel,
        [
            ((r2, feat), F32, VM), ((r2, feat), BF, VM), ((r2, wide), F32, VM), ((r2, feat), F32, VM),
            ((r2, feat), BF, VM), ((feat, wide), BF, VM), ((wide, feat), BF, VM),
        ],
        [(where, SM), (x, VM), (part, VM), (got, VM), (gains, VM)] + [(t, HB) for t in blocks],
        scratch=[pltpu.SemaphoreType.DMA((16,))],
        after=after,
        flops=4 * r2 * feat * wide,
        bytes_accessed=16 * 2**20,
    )


def widen_back(where, u, x, gains, part, got, normed, hidden, wi, wo, first, rows, columns, after=()):
    r2, feat = u.shape
    wide = 2 * feat
    tile = 384
    n = feat // 4

    def kernel(
        where_ref, u_ref, x_ref, gains_ref, part_ref, got_ref, normed_ref, hidden_ref, wi_ref, wo_ref,
        u2_ref, out_ref, low_ref, *more,
    ):
        outs, (ulow_ref, turned_ref, wis_ref, wos_ref, sems) = more[:-5], more[-5:]
        slope = add_both(part_ref[...], got_ref[...], rows)
        u2 = u_ref[...] + norm_back(x_ref[...], gains_ref[pl.ds(2, 1), :], slope)[0]
        u2_ref[...] = u2
        ulow_ref[...] = u2.astype(BF)
        turned_ref[...] = normed_ref[...].T
        out_ref[...] = jnp.zeros_like(out_ref)

        @pl.loop(0, wide // tile)
        def _(t):
            at = pl.ds(pl.multiple_of(t * tile, 128), tile)
            ulow = ulow_ref[...]
            act, dact = gelu_both(hidden_ref[:, at])
            hs = (dact * dot_t(ulow, wo_ref[at, :])).astype(BF)
            wos_ref[at, :] = t_dot(act.astype(BF), ulow).astype(BF)
            wis_ref[:, at] = dot(turned_ref[...], hs).astype(BF)
            out_ref[...] += dot_t(hs, wi_ref[:, at])

        copies = []
        slots = (0, 3 - first, first, 3)

        def add(h, at, size, dst):
            wide_at = pl.ds(pl.multiple_of(at, 16), size)
            deep_at = pl.ds(pl.multiple_of(at + h * feat, 16), size)
            for i, src in enumerate((wis_ref.at[wide_at, pl.ds(h * feat, feat)], wos_ref.at[deep_at])):
                copies.append(pltpu.make_async_copy(src, dst.at[i], sems.at[len(copies)]))

        for i, j in enumerate(slots):
            to = (where_ref[1] ^ j) * n
            add(0, to, n, outs[i // 2].at[i % 2])
            if columns:
                for c in range(4):
                    add(1, to + c * (n // 4), n // 4, outs[2].at[c, i])
            else:
                add(1, to, n, outs[2 + i // 2].at[i % 2])
        start_all(copies)
        low_ref[...] = out_ref[...].astype(BF)
        wait_all(copies)

    block = ((2, 2, n, feat), BF, HB)
    more = [((4, 4, 2, n // 4, feat), BF, HB)] if columns else [block] * 2
    return call(
        kernel,
        [((r2, feat), F32, VM), ((r2, feat), F32, VM), ((r2, feat), BF, VM)] + [block] * 2 + more,
        [
            (where, SM), (u, VM), (x, VM), (gains, VM), (part, VM), (got, VM), (normed, VM),
            (hidden, VM), (wi, VM), (wo, VM),
        ],
        scratch=[
            pltpu.VMEM((r2, feat), BF), pltpu.VMEM((feat, r2), BF), pltpu.VMEM((feat, wide), BF),
            pltpu.VMEM((wide, feat), BF), pltpu.SemaphoreType.DMA((40,)),
        ],
        after=after,
        flops=10 * r2 * feat * wide,
        bytes_accessed=24 * 2**20,
    )


def attend_proj_back(where, dq, own, got, normed, w, wps, small, firsts, rows, last, after=()):
    r2, feat = normed.shape
    half = feat // 2
    n, m = feat // 4, half // 4
    tile = 384
    extra = 0 if small is None else n // 3

    def kernel(where_ref, dq_ref, own_ref, got_ref, normed_ref, w_ref, wps_ref, *refs):
        refs = list(refs)
        take = lambda k: [refs.pop(0) for _ in range(k)]
        small_ref = take(1)[0] if extra else None
        out_ref, low_ref = take(2)
        sides = [take(2) for _ in firsts]
        packed_ref, turned_ref, ws_ref, sm_ref, sems = take(5)
        packed_ref[:, :half] = dq_ref[...]
        packed_ref[:, half:] = (own_ref[...] + got_ref[...].astype(F32)).astype(BF)
        out = dot_t(packed_ref[...], w_ref[...])
        out_ref[...] = out[: out_ref.shape[0]]
        low_ref[...] = (out[rows:] if last else out).astype(BF)
        turned_ref[...] = normed_ref[...].T

        @pl.loop(0, 3 * half // tile)
        def _(t):
            at = pl.ds(pl.multiple_of(t * tile, 128), tile)
            ws_ref[:, at] = dot(turned_ref[...], packed_ref[:, at]).astype(BF)

        if extra:
            wide = jnp.concatenate(
                [small_ref[...], jnp.zeros((128 - small_ref.shape[0], feat), F32)], 0
            )
            sm_ref[...] = wide.T.astype(BF)
        copies = []

        def add(src, dst):
            copies.append(pltpu.make_async_copy(src, dst, sems.at[len(copies)]))

        for lane, first in enumerate(firsts):
            one = len(firsts) == 1
            skip = 2 * n if lane == 1 else 0
            for ref, js in zip(sides[lane], ((0, 3 - first), (first, 3))):
                for i, j in enumerate(js):
                    to = where_ref[1] ^ j
                    at, pat = pl.ds(pl.multiple_of(to * n, 16), n), pl.ds(pl.multiple_of(to * m, 16), m)
                    for g in range(3):
                        if one or (g == 2) == (lane == 1):
                            add(ws_ref.at[at, pl.ds(g * half, half)], ref.at[i, pl.ds(g * n - skip, n)])
                    for g in range(2):
                        if one or lane == 1:
                            add(
                                wps_ref.at[pat, pl.ds(g * half, half)],
                                ref.at[i, pl.ds(3 * n + g * m - skip, m)],
                            )
                    if extra:
                        for g in range(3):
                            sat = pl.ds(pl.multiple_of(to * n + g * extra, 16), extra)
                            add(sm_ref.at[sat], ref.at[i, pl.ds(3 * n + 2 * m, extra), pl.ds(128 * g, 128)])
        start_all(copies)
        wait_all(copies)

    n_out = rows if last else r2
    deep = 3 * n + 2 * m + extra
    deeps = [deep] * 2 if len(firsts) == 1 else [2 * n] * 2 + [n + 2 * m] * 2
    return call(
        kernel,
        [((n_out, feat), F32, VM), ((n_out, feat), BF, VM)] + [((2, k, half), BF, HB) for k in deeps],
        [(where, SM), (dq, VM), (own, VM), (got, VM), (normed, VM), (w, VM), (wps, VM)]
        + ([(small, VM)] if extra else []),
        scratch=[
            pltpu.VMEM((r2, 3 * half), BF), pltpu.VMEM((feat, r2), BF), pltpu.VMEM((feat, 3 * half), BF),
            pltpu.VMEM((feat, 128), BF), pltpu.SemaphoreType.DMA((32,)),
        ],
        after=after,
        flops=4 * r2 * feat * 3 * half,
        bytes_accessed=10 * 2**20,
    )


def spread_attend_rows(t, store):
    half = t.shape[1]
    n, m = half // 2, half // 4
    r = n // 4
    for z in range(4):
        for g in range(3):
            store(z, g * half, t[g * n + z * r : g * n + (z + 1) * r])
        at = 3 * n + z * (m // 4)
        p = [t[at + g * m : at + g * m + m // 4] for g in range(2)]
        store(z, 3 * half, jnp.concatenate(p, 0))
    if t.shape[0] > 3 * n + 2 * m:
        sm = t[3 * n + 2 * m :]
        sm = jnp.concatenate([sm[:, 128 * g : 128 * (g + 1)] for g in range(3)], 0)
        for z in range(4):
            store(z, 4 * half, sm[z * r : (z + 1) * r])


def spread_pair_rows(t, first, store):
    r = t.shape[1] // 4
    for i in range(2):
        for z in range(4):
            store(z, first + i * t.shape[2], t[i, z * r : (z + 1) * r])


def columns_of(groups, after=()):
    wide = 0
    for t in groups:
        wide += 2 * t.shape[2] if t.ndim == 3 else 4 * t.shape[1] + (128 if t.shape[0] > 2 * t.shape[1] else 0)
    r = groups[0].shape[1] // 4 if groups[0].ndim == 3 else groups[0].shape[1] // 8

    def kernel(*refs):
        out = refs[len(groups)]

        def store(z, lane, value):
            out[z, :, pl.ds(lane, value.shape[1])] = value.astype(BF)

        at = 0
        for ref in refs[: len(groups)]:
            t = ref[...]
            if t.ndim == 3:
                spread_pair_rows(t, at, store)
                at += 2 * t.shape[2]
            else:
                spread_attend_rows(t, lambda z, lane, value, at=at: store(z, at + lane, value))
                at += 4 * t.shape[1] + (128 if t.shape[0] > 2 * t.shape[1] else 0)

    return call(
        kernel, [((4, r, wide), BF, VM)], [(t, VM) for t in groups], after=after,
        bytes_accessed=3 * 2**20,
    )[0]


def last_columns(where, upper, lower, pair, after=()):
    half = upper.shape[1]
    r = half // 8
    wide = 4 * half + 2 * pair.shape[2]

    def kernel(where_ref, upper_ref, lower_ref, pair_ref, *refs):
        outs, scratch = refs[:4], refs[4]

        def store(z, lane, value):
            scratch[z, :, pl.ds(lane, value.shape[1])] = value

        spread_attend_rows(jnp.concatenate([upper_ref[...], lower_ref[...]], 0), store)
        spread_pair_rows(pair_ref[...], 4 * half, store)
        c = where_ref[2]
        outs[0][...] = scratch[c]
        for j in range(1, 4):
            outs[j][...] = scratch[c ^ j].astype(BF)

    return call(
        kernel,
        [((r, wide), F32, VM)] + [((r, wide), BF, VM)] * 3,
        [(where, SM), (upper, VM), (lower, VM), (pair, VM)],
        scratch=[pltpu.VMEM((4, r, wide), F32)],
        after=after,
        bytes_accessed=6 * 2**20,
    )


def join_upstream(u_own, u_sib, rows):
    feat = u_own.shape[1]

    def kernel(o_ref, s_ref, u_ref, low_ref):
        u_ref[pl.ds(0, rows), :] = o_ref[...]
        u_ref[pl.ds(rows, rows), :] = s_ref[...].astype(F32)
        low_ref[pl.ds(0, rows), :] = o_ref[...].astype(BF)
        low_ref[pl.ds(rows, rows), :] = s_ref[...]

    return call(
        kernel, [((2 * rows, feat), F32, VM), ((2 * rows, feat), BF, VM)], [(u_own, VM), (u_sib, VM)],
        bytes_accessed=2**21,
    )


def norm_step(u, x, gains, gain_row, part, got, rows, last, after=()):
    feat = x.shape[1]
    n = rows if last else 2 * rows

    def kernel(u_ref, x_ref, gains_ref, part_ref, got_ref, *outs):
        if last:
            slope = part_ref[...] + got_ref[...].astype(F32)
        else:
            slope = add_both(part_ref[...], got_ref[...], rows)
        u2 = u_ref[:n] + norm_back(x_ref[:n], gains_ref[pl.ds(gain_row, 1), :], slope)[0]
        low = outs[-1]
        low[...] = u2[: low.shape[0]].astype(BF)
        if not last:
            outs[0][...] = u2

    outs = [((last if last else n, feat), BF, VM)]
    return call(
        kernel,
        outs if last else [((n, feat), F32, VM)] + outs,
        [(u, VM), (x, VM), (gains, VM), (part, VM), (got, VM)],
        after=after,
        bytes_accessed=6 * 2**20,
    )


def picks(index, turn, cap, cap_rows, experts):
    at = lax.broadcasted_iota(jnp.int32, (1, experts * cap_rows), 1)
    out = []
    for k in range(TOP):
        chosen, slot = index[:, k : k + 1], index[:, TOP + k : TOP + k + 1]
        place = chosen if turn is None else chosen ^ turn
        target = jnp.where(slot < cap, place * cap_rows + slot, -1)
        out.append(jnp.where(at == target, 1.0, 0.0).astype(BF))
    return out


def lane_at(index, k):
    lane = lax.broadcasted_iota(jnp.int32, (1, 128), 1)
    return jnp.where(lane == index[:, k : k + 1] + 4, 1.0, 0.0)


def present_mask(blk, rows, blk_len, longest):
    pos = lax.broadcasted_iota(jnp.int32, (rows, 1), 0)
    last = jnp.where(blk < longest, blk_len, blk_len - 1)
    return jnp.where(pos < last, 1.0, 0.0)


def route(where, x, part, got, gains, small, cot, index, experts, cap, rows, blk_len, longest, fast, after=()):
    feat = x.shape[1]
    cap_rows = up16(cap)

    def kernel(where_ref, x_ref, part_ref, got_ref, gains_ref, small_ref, cot_ref, index_ref,
               x3_ref, moe_ref, gates_ref, up_ref, *blocks):
        x3 = x_ref[:rows] + part_ref[:rows] + got_ref[...].astype(F32)
        x3_ref[...] = x3
        moe = layer_norm(x3, gains_ref[pl.ds(3, 1), :])
        moe_ref[...] = moe
        lane = lax.broadcasted_iota(jnp.int32, (1, 128), 1)
        logits = dot(moe, small_ref[...])
        logits = jnp.where((lane >= 4) & (lane < 4 + experts), logits, -1e30)
        ex = jnp.exp(logits - jnp.max(logits, -1, keepdims=True))
        gates = ex / jnp.sum(ex, -1, keepdims=True)
        gates_ref[...] = gates
        up_ref[...] = jnp.zeros_like(up_ref)
        up_ref[pl.ds(0, blk_len), :] = cot_ref[...].astype(F32)
        up = up_ref[...] * present_mask(where_ref[0], rows, blk_len, longest)
        up_ref[...] = up
        index = index_ref[...]
        pick = picks(index, where_ref[1] if fast else None, cap, cap_rows, experts)
        sent = t_dot(pick[0] + pick[1], moe).astype(BF)
        slope = 0.0
        for k in range(TOP):
            gate = jnp.sum(gates * lane_at(index, k), -1, keepdims=True)
            slope += t_dot(pick[k], (gate * up).astype(BF))
        slope = slope.astype(BF)
        for j, ref in enumerate(blocks):
            ref[pl.ds(0, cap_rows), :] = sent[j * cap_rows : (j + 1) * cap_rows]
            ref[pl.ds(cap_rows, cap_rows), :] = slope[j * cap_rows : (j + 1) * cap_rows]

    return call(
        kernel,
        [((rows, feat), F32, VM), ((rows, feat), BF, VM), ((rows, 128), F32, VM), ((rows, feat), F32, VM)]
        + [((2 * cap_rows, feat), BF, VM)] * experts,
        [(where, SM), (x, VM), (part, VM), (got, VM), (gains, VM), (small, VM), (cot, VM), (index, VM)],
        after=after,
        flops=6 * rows * experts * cap_rows * feat,
        bytes_accessed=5 * 2**20,
    )


def experts_forward(blocks, own, sib, cap_rows, after=()):
    feat, wide = own[0].shape
    tile = 512 if wide % 512 == 0 else wide
    n = len(blocks) * cap_rows
    steps = wide // tile

    def kernel(*refs):
        refs = list(refs)
        take = lambda k: [refs.pop(0) for _ in range(k)]
        ins, weights = take(len(blocks)), take(4)
        take(len(after))
        outs = take(len(blocks))
        rows_ref, slope_ref, res_ref, back_ref = take(4)
        t = pl.program_id(0)

        @pl.when(t == 0)
        def _():
            for j, ref in enumerate(ins):
                at = pl.ds(j * cap_rows, cap_rows)
                rows_ref[at, :] = ref[pl.ds(0, cap_rows), :]
                slope_ref[at, :] = ref[pl.ds(cap_rows, cap_rows), :]
            res_ref[...] = jnp.zeros_like(res_ref)
            back_ref[...] = jnp.zeros_like(back_ref)

        def step(wi_ref, wo_ref):
            act, dact = gelu_both(dot(rows_ref[...], wi_ref[...]))
            hs = (dact * dot_t(slope_ref[...], wo_ref[...])).astype(BF)
            res_ref[...] += dot(act.astype(BF), wo_ref[...])
            back_ref[...] += dot_t(hs, wi_ref[...])

        @pl.when(t < steps)
        def _():
            step(*weights[:2])

        @pl.when(t >= steps)
        def _():
            step(*weights[2:])

        @pl.when(t == 2 * steps - 1)
        def _():
            for j, ref in enumerate(outs):
                at = pl.ds(j * cap_rows, cap_rows)
                ref[pl.ds(0, cap_rows), :] = res_ref[at, :].astype(BF)
                ref[pl.ds(cap_rows, cap_rows), :] = back_ref[at, :].astype(BF)

    blk = (2 * cap_rows, feat)
    whole = pl.BlockSpec(blk, lambda t: (0, 0))
    first = lambda t: jnp.minimum(t, steps - 1)
    later = lambda t: jnp.maximum(t - steps, 0)
    specs = []
    for place in (first, later):
        specs.append(pl.BlockSpec((feat, tile), lambda t, place=place: (0, place(t))))
        specs.append(pl.BlockSpec((tile, feat), lambda t, place=place: (place(t), 0)))
    return pl.pallas_call(
        kernel,
        grid=(2 * steps,),
        out_shape=[jax.ShapeDtypeStruct(blk, BF)] * len(blocks),
        in_specs=[whole] * len(blocks) + specs + [HB] * len(after),
        out_specs=[whole] * len(blocks),
        scratch_shapes=[
            pltpu.VMEM((n, feat), BF), pltpu.VMEM((n, feat), BF),
            pltpu.VMEM((n, feat), F32), pltpu.VMEM((n, feat), F32),
        ],
        compiler_params=pltpu.CompilerParams(
            vmem_limit_bytes=62 * 2**20, dimension_semantics=("arbitrary",)
        ),
        cost_estimate=pl.CostEstimate(
            flops=16 * n * feat * wide, bytes_accessed=20 * 2**20, transcendentals=0
        ),
    )(*blocks, *own, *sib, *after)


def expert_slopes(every, w_in, w_out, got, after=()):
    feat, wide = w_in.shape
    tile = 512 if wide % 512 == 0 else wide
    steps = wide // tile
    groups, experts, cap_rows = every.shape[0], every.shape[1], every.shape[2] // 2
    total = groups * experts * cap_rows
    kind = BF if got is None else F32

    def kernel(*refs):
        refs = list(refs)
        take = lambda k: [refs.pop(0) for _ in range(k)]
        every_ref, wi_ref, wo_ref = take(3)
        got_refs = take(2) if got is not None else None
        take(len(after))
        wis_ref, wos_ref, rows_ref, slope_ref, turned_ref, sems = take(6)

        @pl.when(pl.program_id(0) == 0)
        def _():
            copies = []
            for k in range(groups):
                for j in range(experts):
                    at = pl.ds((k * experts + j) * cap_rows, cap_rows)
                    for i, ref in enumerate((rows_ref, slope_ref)):
                        copies.append(pltpu.make_async_copy(
                            every_ref.at[k, j, pl.ds(i * cap_rows, cap_rows)], ref.at[at],
                            sems.at[len(copies)],
                        ))
            start_all(copies)
            per = total // groups
            for k in range(groups):
                wait_all(copies[k * 2 * experts : (k + 1) * 2 * experts])
                at = pl.ds(k * per, per)
                turned_ref[:, at] = rows_ref[at, :].T

        act, dact = gelu_both(dot(rows_ref[...], wi_ref[...]))
        hs = (dact * dot_t(slope_ref[...], wo_ref[...])).astype(BF)
        wis = dot(turned_ref[...], hs)
        wos = t_dot(act.astype(BF), slope_ref[...])
        if got is not None:
            wis, wos = wis + got_refs[0][...].astype(F32), wos + got_refs[1][...].astype(F32)
        wis_ref[...] = wis.astype(kind)
        wos_ref[...] = wos.astype(kind)

    wi_spec = pl.BlockSpec((feat, tile), lambda t: (0, t))
    wo_spec = pl.BlockSpec((tile, feat), lambda t: (t, 0))
    return pl.pallas_call(
        kernel,
        grid=(steps,),
        out_shape=[jax.ShapeDtypeStruct((feat, wide), kind), jax.ShapeDtypeStruct((wide, feat), kind)],
        in_specs=[HB] + [wi_spec, wo_spec] * (1 if got is None else 2) + [HB] * len(after),
        out_specs=[wi_spec, wo_spec],
        scratch_shapes=[
            pltpu.VMEM((total, feat), BF), pltpu.VMEM((total, feat), BF), pltpu.VMEM((feat, total), BF),
            pltpu.SemaphoreType.DMA((2 * groups * experts,)),
        ],
        compiler_params=pltpu.CompilerParams(
            vmem_limit_bytes=56 * 2**20, dimension_semantics=("arbitrary",)
        ),
        cost_estimate=pl.CostEstimate(
            flops=8 * total * feat * wide, bytes_accessed=20 * 2**20, transcendentals=0
        ),
    )(every, w_in, w_out, *(got or ()), *after)


def combine(where, blocks, x3, moe, gates, up, index, small, gains, small_rows, experts, cap, rows, blk_len, longest, fast, after=()):
    feat = x3.shape[1]
    cap_rows = up16(cap)
    n = experts * cap_rows

    def kernel(where_ref, *refs):
        refs = list(refs)
        take = lambda k: [refs.pop(0) for _ in range(k)]
        ins = take(experts)
        x3_ref, moe_ref, gates_ref, up_ref, index_ref, small_ref, gains_ref = take(7)
        acts_ref, u_ref, low_ref, slopes_ref, result_ref, back_ref = take(6)
        for j, ref in enumerate(ins):
            at = pl.ds(j * cap_rows, cap_rows)
            result_ref[at, :] = ref[pl.ds(0, cap_rows), :]
            back_ref[at, :] = ref[pl.ds(cap_rows, cap_rows), :]
        index, gates, up, moe = index_ref[...], gates_ref[...], up_ref[...], moe_ref[...]
        pick = picks(index, where_ref[1] if fast else None, cap, cap_rows, experts)
        x3 = x3_ref[...]
        acts, all_slope = x3, 0.0
        for k in range(TOP):
            at_k = lane_at(index, k)
            gate = jnp.sum(gates * at_k, -1, keepdims=True)
            picked = dot(pick[k], result_ref[...])
            acts = acts + gate * picked
            all_slope += jnp.sum(up * picked, -1, keepdims=True) * at_k
        acts = acts * present_mask(where_ref[0], rows, blk_len, longest)
        acts_ref[...] = acts[:blk_len].astype(BF)
        logit = (gates * (all_slope - jnp.sum(gates * all_slope, -1, keepdims=True))).astype(BF)
        slope = dot(pick[0] + pick[1], back_ref[...]) + dot_t(logit, small_ref[...])
        dx, terms = norm_back(x3, gains_ref[pl.ds(3, 1), :], slope)
        u = up + dx
        u_ref[...] = u
        low_ref[...] = u.astype(BF)
        slopes_ref[...] = t_dot(logit, moe)[:small_rows]
        slopes_ref[pl.ds(3, 1), :] = jnp.sum(terms, 0, keepdims=True)

    return call(
        kernel,
        [((blk_len, feat), BF, VM), ((rows, feat), F32, VM), ((rows, feat), BF, VM), ((small_rows, feat), F32, VM)],
        [(where, SM)] + [(b, VM) for b in blocks]
        + [(t, VM) for t in (x3, moe, gates, up, index, small, gains)],
        scratch=[pltpu.VMEM((n, feat), BF), pltpu.VMEM((n, feat), BF)],
        after=after,
        flops=6 * rows * n * feat,
        bytes_accessed=5 * 2**20,
    )


def tie(xs, *after):
    return list(lax.optimization_barrier((*xs, *after)))[: len(xs)]


class Links:
    def __init__(self, mesh):
        self.E = mesh.shape["expert"]
        self.C = mesh.shape["context"]
        self.D = mesh.shape["dp"]
        assert self.C == 4 and self.D == 2 and self.E % 2 == 0
        self.fast = self.E == 4
        self.chips = self.E * self.C
        flat = lambda e, c, d: (e * self.C + c) * self.D + d
        self.team = [
            (flat(e, c, d), flat((e // 2) * 2 + c // 2, 2 * (e % 2) + d, c % 2))
            for e in range(self.E)
            for c in range(self.C)
            for d in range(self.D)
        ]
        self.to_lane = [(f, (f % self.chips) * 2 + f // self.chips) for f in range(2 * self.chips)]
        self.from_lane = [(b, a) for a, b in self.to_lane]

    def move(self, x):
        return lax.ppermute(x, ALL, self.team)

    def xor(self, x, axis, j):
        n = {"expert": self.E, "context": self.C, "dp": self.D}[axis]
        return lax.ppermute(x, axis, [(i, i ^ j) for i in range(n)])

    def sib(self, x):
        return self.xor(x, "dp", 1)

    def partner(self, x):
        return self.xor(x, "expert", 1)

    def column(self, x, *hold):
        c = lax.axis_index("context")
        got = tie([x] + [self.xor(x, "context", j) for j in range(1, 4)], *hold)
        pick = lambda k: jnp.where(
            c & 2 == 0, jnp.where(c & 1 == 0, got[k], got[k ^ 1]), jnp.where(c & 1 == 0, got[k ^ 2], got[k ^ 3])
        )
        return jnp.stack([pick(k) for k in range(4)])

    def plane_sum(self, keep, send, first, hold):
        (got,) = tie([self.xor(send, "expert", first)], *hold[0])
        got = got.astype(F32)
        give = (keep[1].astype(F32) + got[1]).astype(BF)
        (far,) = tie([self.xor(give, "expert", 3 - first)], *hold[1])
        return keep[0].astype(F32) + got[0] + far.astype(F32), give

    def column_sum(self, x, *hold):
        c = lax.axis_index("context")
        low = x.astype(BF)
        got = [self.xor(lax.dynamic_index_in_dim(low, c ^ j, 0, False), "context", j) for j in range(1, 4)]
        got = tie(got, *hold)
        total = lax.dynamic_index_in_dim(x, c, 0, False)
        for t in got:
            total = total + t.astype(F32)
        return total

    def swap_blocks(self, x):
        if not self.fast:
            return list(lax.all_to_all(jnp.stack(x), "expert", 0, 0, tiled=True))
        return [x[0]] + [self.xor(x[j], "expert", j) for j in range(1, 4)]


def lane_rows(links, mine, d):
    keep = lax.dynamic_index_in_dim(mine, d, 0, False)
    got = links.sib(lax.dynamic_index_in_dim(mine, 1 - d, 0, False))
    return jnp.where(d == 0, jnp.concatenate([keep, got], 0), jnp.concatenate([got, keep], 0))


def in_order(d, own, other):
    return jnp.where(d == 0, jnp.stack([own, other]), jnp.stack([other, own]))


class Weights:
    def __init__(self, links, rdev, feat, ff):
        self.links, self.rdev, self.feat, self.ff = links, rdev, feat, ff
        self.d = lax.axis_index("dp")
        self.half = feat // 2

    def split_attend(self, w):
        w = w.reshape(self.rdev, 3, 2, self.half).transpose(2, 0, 1, 3)
        return w.reshape(2, self.rdev, 3 * self.half)

    def split_widen(self, w):
        w = w.reshape(self.rdev, self.links.chips, 2, 2, -1).transpose(2, 0, 3, 1, 4)
        return w.reshape(2, self.rdev, self.ff // 2)

    def pack_attend(self, w, p, small):
        parts = [w, jnp.concatenate([p[:, : self.half], p[:, self.half :]], 0)]
        if small is not None:
            parts.append(jnp.pad(small, ((0, 0), (0, 128 - small.shape[1]))))
        return jnp.concatenate(parts, 1)

    def pack_wide(self, wout):
        h = wout.shape[0] // 2
        return jnp.concatenate([wout[:h], wout[h:]], 1)

    def column(self, buf, *hold):
        if self.links.fast:
            return self.links.column(buf, *hold)
        return lax.all_gather(buf, CHIPS, axis=0, tiled=False)

    def cut(self, x):
        return x if self.links.fast else x.reshape(4, -1, x.shape[-1])

    def pack_block(self, quad, between):
        f, h, r = self.feat, self.half, self.rdev
        n = quad.shape[0]
        p = quad[..., f + h : 2 * f].reshape(n, 2, r, h)
        parts = [quad[..., i * h : (i + 1) * h] for i in range(3)] + [p[:, 0], p[:, 1]]
        parts = [self.cut(t.reshape(-1, h)) for t in parts]
        if self.links.fast:
            parts.insert(2, between)
        if quad.shape[2] > 2 * f:
            small = self.cut(quad[..., 2 * f :].reshape(-1, 128))
            small = small.reshape(small.shape[:-2] + (3, -1, 128))
            parts.append(jnp.concatenate([small[..., g, :, :] for g in range(3)], -1))
        return jnp.concatenate(parts, -2)

    def pack_pair(self, quad_in, quad_out):
        f = self.feat
        halves = []
        for i in range(2):
            pair = [self.cut(t[..., i * f : (i + 1) * f].reshape(-1, f)) for t in (quad_in, quad_out)]
            halves.append(jnp.stack(pair, -3))
        return jnp.stack(halves, -4)

    def spread(self, x, cuts, *hold):
        if not self.links.fast:
            return [x[0], x[1], x[2], cuts[0](x[3]), cuts[1](x[3])]
        to = lambda t, j: self.links.xor(t, "expert", j)
        x1, x2 = tie([to(x, 1), to(x, 2)], *hold)
        return [x, x1, x2, to(cuts[0](x1), 2), to(cuts[1](x2), 1)]

    def spread_attend(self, x, skip, *hold):
        n = self.feat // 2 + skip
        return self.spread(x, (lambda t: t[:n], lambda t: t[n:]), *hold)

    def spread_pair(self, x, *hold):
        return self.spread(x, (lambda t: t[0], lambda t: t[1]), *hold)

    def total(self, keep, send, first, hold):
        if self.links.fast:
            out, _ = self.links.plane_sum(keep, send, first, hold)
            return out
        blk = {0: keep[0], 3 - first: keep[1], first: send[0], 3: send[1]}
        return jnp.stack([blk[j] for j in range(4)])

    def all_sum(self, buf):
        return lax.psum_scatter(buf.astype(BF), CHIPS, scatter_dimension=0, tiled=False).astype(F32)

    def exchange(self, w):
        w = w.reshape(2, self.rdev, -1)
        mine = lax.dynamic_index_in_dim(w, self.d, 0, False)
        got = self.links.sib(lax.dynamic_index_in_dim(w, 1 - self.d, 0, False))
        return in_order(self.d, mine, got)

    def to_columns(self, t):
        n, m = self.feat // 4, self.half // 4
        r = self.rdev
        cut = lambda t, k: t.reshape(-1, k * r, t.shape[-1])
        parts = [cut(t[..., g * n : (g + 1) * n, :], 2) for g in range(3)]
        p = [cut(t[..., 3 * n + g * m : 3 * n + (g + 1) * m, :], 1) for g in range(2)]
        parts.append(jnp.concatenate(p, 1))
        if t.shape[-2] > 3 * n + 2 * m:
            sm = t[..., 3 * n + 2 * m :, :]
            sm = jnp.stack([sm[..., 128 * g : 128 * (g + 1)] for g in range(3)], -3)
            parts.append(sm.reshape(-1, 2 * r, 128))
        return jnp.concatenate(parts, 2)

    def owners(self, col1, col3, w2):
        f, h, r = self.feat, self.half, self.rdev
        w = f + h
        p = [jnp.concatenate([c[:r, w : 2 * f], c[r:, w : 2 * f]], 1) for c in (col1, col3)]
        p = lax.ppermute(jnp.concatenate(p, 0), ALL, self.links.from_lane)
        t = self.exchange(jnp.concatenate([col1[:, :w], col3[:, :w], col3[:, 2 * f :], w2], 1))

        def attend(t):
            return t.reshape(2, r, 3, h).transpose(1, 2, 0, 3).reshape(r, 3 * f)

        small = t[..., 2 * w : 2 * w + 128]
        win = t[..., 2 * w + 128 :].reshape(2, r, 2, self.links.chips, -1)
        win = win.transpose(1, 3, 0, 2, 4).reshape(r, self.ff)
        return attend(t[..., :w]), p[:r], attend(t[..., w : 2 * w]), p[r:], small[0] + small[1], win


def body(links, *args):
    (tokens, cotangent, g1, w1, p1, g2, win, wout, g3, w3, p3, g4, router, ein, eout, routes, slots) = args
    e = lax.axis_index("expert")
    d = lax.axis_index("dp")
    blk_len, feat = tokens.shape[1:]
    rows = up16(blk_len)
    half = feat // 2
    rdev = w1.shape[0]
    ff = win.shape[1]
    longest = LEN - (blk_len - 1) * links.C
    experts = router.shape[1]
    assert experts <= 128
    small_rows = (4 + experts + 7) // 8 * 8
    cap = max(2, (5 * TOP * blk_len + 4 * experts - 1) // (4 * experts))
    blk = 2 * (e % 2) + d
    where = jnp.stack([blk, e if links.fast else 0 * e, lax.axis_index("context")]).astype(jnp.int32)
    wt = Weights(links, rdev, feat, ff)
    img = dict(rows=rows, blk_len=blk_len, longest=longest)

    tok = links.move(tokens[0])
    ps = lax.ppermute(jnp.concatenate([p1, p3], 0), ALL, links.to_lane)
    small = jnp.concatenate([g1[:, None], g2[:, None], g3[:, None], g4[:, None], router], 1)
    gsm = small.shape[1]
    lane1 = jnp.concatenate(
        [wt.split_attend(w1), jnp.broadcast_to(small[None], (2, rdev, gsm))], 2
    )
    lane1 = lane_rows(links, lane1, d)
    buf1 = wt.pack_attend(lane1[:, : 3 * half], ps[:rdev], lane1[:, 3 * half :])
    quad1 = wt.column(buf1)
    later = jnp.concatenate([wt.split_widen(win), wt.split_attend(w3)], 2)
    later = lane_rows(links, later, d)
    w_in, w_out = later[:, : ff // 2], wt.pack_wide(wout)
    w3_lane, p3_lane = later[:, ff // 2 :], ps[rdev:]
    block3 = jnp.concatenate(
        [w3_lane[:, g * half : (g + 1) * half] for g in range(3)] + [p3_lane[:, :half], p3_lane[:, half:]], 0
    )
    skip = block3.shape[0] if links.fast else 0
    tok_pair = jnp.stack([tok, links.partner(tok)])
    block1 = wt.pack_block(tie([quad1], tok_pair)[0], block3)
    if links.fast:
        (buf2,) = tie([jnp.concatenate([w_in, w_out], 1)], quad1)
        quad2 = wt.column(buf2)
        blocks1 = wt.spread_attend(block1, skip, quad2)
        (tok_pair,) = tie([tok_pair], *blocks1[1:3])
    else:
        quad2 = None
        blocks1 = wt.spread_attend(block1, skip)
    tok_sib = links.sib(tok_pair)
    toks = [tok_pair[0], tok_sib[0], tok_pair[1], tok_sib[1]]
    raw = jnp.concatenate([routes[0], slots[0]], 1).astype(BF)
    cot = jnp.concatenate([cotangent[0].astype(BF), jnp.pad(raw, ((0, 0), (0, 128 - 2 * TOP)))], 1)
    cot = links.move(tie([cot], *blocks1[1:3])[0])
    if links.fast:
        (quad2,) = tie([quad2], *blocks1[3:], *toks, cot)
        pair2 = wt.pack_pair(quad2[..., : ff // 2], quad2[..., ff // 2 :])
        q, n = feat // 2, block3.shape[0]
        place3 = jnp.stack([t[q : q + n] for t in blocks1[:4]])
        source3 = lax.all_gather(place3, "context", axis=0, tiled=False)
        p3 = source3[:, :, 6 * rdev :].reshape(4, 4, 2, rdev, half)
        p3 = jnp.stack([lax.dynamic_index_in_dim(p3, e ^ k, 1, False) for k in range(4)])
        wp3 = p3.transpose(0, 1, 3, 2, 4).reshape(half, feat)
    else:
        pair2 = wt.pack_pair(wt.column(w_in), wt.column(w_out))
        all3 = lax.all_gather(block3, CHIPS, axis=0, tiled=False)
        source3 = all3[:, : 6 * rdev].reshape(links.chips, 3, 2 * rdev, half)
        source3 = source3.transpose(0, 2, 1, 3).reshape(feat, 3 * half)
        wp3 = all3[:, 6 * rdev :].reshape(links.chips, 2, rdev, half)
        wp3 = wp3.transpose(0, 2, 1, 3).reshape(half, feat)

    x0, normed1, q1, kv1, far1, wa1, wp1, small, gains = attend_first(
        where, toks, small_rows, blocks1, rows, skip
    )
    part, low, blend1, lse1 = attend_core(
        where, q1, kv1, far1, wp1, solo=False, **img
    )
    blocks2 = wt.spread_pair(pair2, part)
    x1, normed2, hidden, part2, low2, wi, wo = widen_forward(
        where, x0, part, links.sib(low), gains, blocks2, rows
    )
    x2, normed3, own3 = norm_next(x1, part2, links.sib(low2), gains, 2, rows)
    ein_own, eout_own = ein[0], eout[0]
    ein_sib, eout_sib = [links.sib(t) for t in tie([ein_own, eout_own], own3)]
    far_own = links.partner(own3)
    q3, kv3, wa3 = attend_next(where, normed3, source3)
    (far_own,) = tie([far_own], q3)
    part3, low3, blend3, lse3, far3 = attend_core(
        where, q3, kv3, None, wp3, solo=True, far=(far_own, links.sib(far_own), wa3), **img
    )
    moe_args = dict(experts=experts, cap=cap, fast=links.fast, **img)
    index = cot[:, feat : feat + 2 * TOP].astype(jnp.int32)
    index = jnp.pad(index, ((0, rows - blk_len), (0, 0)), constant_values=cap)
    x3, moe, gates, up, *sent = route(
        where, x2, part3, links.sib(low3), gains, small, cot[:, :feat], index,
        after=(ein_sib, eout_sib), **moe_args
    )
    came = links.swap_blocks(sent)
    every = lax.all_gather(jnp.stack(came), "context", axis=0, tiled=False)
    answer = experts_forward(came, (ein_own, eout_own), (ein_sib, eout_sib), up16(cap))
    answer = links.swap_blocks(answer)
    acts, u, u_low, small_slopes = combine(
        where, answer, x3, moe, gates, up, index, small, gains, small_rows, **moe_args
    )

    u, u_low = join_upstream(u, links.sib(u_low), rows)
    dq, own, far, wps = attend_core_back(where, u_low, wp3, blend3, q3, kv3, far3, lse3, **img)
    first3, first2, first1 = (1,), 2, (1, 2)
    part, low, *slopes3 = attend_proj_back(
        where, dq, own, links.partner(far), normed3, wa3, wps, small_slopes, first3, rows, False
    )
    u, part, low, *slopes2 = widen_back(
        where, u, x2, gains, part, links.sib(low), normed2, hidden, wi, wo, first2, rows, False
    )
    u1, u_low = norm_step(u, x1, gains, 1, part, links.sib(low), rows, 0)
    dq1, own, far, wps = attend_core_back(where, u_low, wp1, blend1, q1, kv1, far1, lse1, **img)
    part, low, *slopes1 = attend_proj_back(
        where, dq1, own, links.partner(far), normed1, wa1, wps, None, first1, rows, True, after=(every,)
    )
    (u2,) = norm_step(u1, x0, gains, 0, part, links.sib(low), rows, blk_len)
    moved = links.move(jnp.stack([acts, u2]))
    acts, token_slope = moved[0], moved[1]
    e_sib = expert_slopes(every, ein_sib, eout_sib, None, after=(u2,))
    sum3 = wt.total(*slopes3, first3[0], ((low,), (e_sib[0],)))
    sum2a = wt.total(*slopes2[:2], first2, ((low,), (e_sib[0],)))
    sum2b = wt.total(*slopes2[2:], first2, ((e_sib[0],), ()))
    sum1 = [wt.total(*slopes1[2 * i : 2 * i + 2], first1[i], ((e_sib[0],), ())) for i in range(2)]
    if links.fast:
        early = columns_of([sum3, sum2a])
        early = lax.psum_scatter(tie([early], every)[0], "context", scatter_dimension=0, tiled=False)
        own, *away = last_columns(where, *sum1, sum2b, after=(moved,))
        e_slopes = expert_slopes(every, ein_own, eout_own, [links.sib(t) for t in e_sib], after=(own,))
        for t in tie([links.xor(t, "context", j + 1) for j, t in enumerate(away)], e_slopes[0]):
            own = own + t.astype(F32)
        early = tie([early], e_slopes[0])[0].astype(F32)
        col1, col2b = own[:, : 2 * feat], own[:, 2 * feat :]
        col3, col2a = early[:, : early.shape[1] - 2 * feat], early[:, early.shape[1] - 2 * feat :]
        w2 = jnp.concatenate([col2a[:, :feat], col2b[:, :feat]], 1)
        wout_out = jnp.concatenate([col2a[:, feat:], col2b[:, feat:]], 0)
    else:
        e_slopes = expert_slopes(every, ein_own, eout_own, [links.sib(t) for t in e_sib])
        col3, col1 = wt.to_columns(sum3), wt.to_columns(jnp.concatenate(sum1, -2))
        col3, col1 = wt.all_sum(col3), wt.all_sum(col1)
        hid = ff // (4 * links.chips)
        w2 = [t[..., 0, :, :].reshape(-1, 2 * rdev, feat) for t in (sum2a, sum2b)]
        w2_out = [t[..., 1, :, :].reshape(-1, hid, feat) for t in (sum2a, sum2b)]
        w2, w2_out = [wt.all_sum(jnp.concatenate(t, 2)) for t in (w2, w2_out)]
        wout_out = jnp.concatenate([w2_out[:, :feat], w2_out[:, feat:]], 0)
    w1_out, p1_out, w3_out, p3_out, extra, win_out = wt.owners(col1, col3, w2)

    def gain_slope(w, slope, gain):
        return jnp.sum(w.astype(F32) * slope, 1) / gain.astype(F32)

    return (
        acts.astype(F32)[None], token_slope.astype(F32)[None],
        gain_slope(w1, w1_out, g1), w1_out, p1_out, gain_slope(win, win_out, g2), win_out, wout_out,
        gain_slope(w3, w3_out, g3), w3_out, p3_out, extra[:, 3], extra[:, 4 : 4 + experts],
        e_slopes[0][None], e_slopes[1][None],
    )


def solution(mesh):
    links = Links(mesh)
    tok = P(("expert", "dp"), "context", None)
    vec, mat = P(ALL), P(ALL, None)
    ein, eout = P("expert", None, "dp"), P("expert", "dp", None)
    dense = (vec, mat, mat, vec, mat, mat, vec, mat, mat, vec, mat, ein, eout)
    return jax.shard_map(
        functools.partial(body, links),
        mesh=mesh,
        in_specs=(tok, tok) + dense + (tok, tok),
        out_specs=(tok, tok) + dense,
        check_vma=False,
    )
```

```python
import functools

import jax
import jax.numpy as jnp
from jax import lax
from jax.experimental import pallas as pl
from jax.experimental.pallas import tpu as pltpu
from jax.sharding import PartitionSpec as P

HEADS = 12
HEAD_DIM = 64
LEN = 577
TOP = 2
ALL = ("expert", "context", "dp")
CHIPS = ("expert", "context")
BF = jnp.bfloat16
F32 = jnp.float32
VM = pl.BlockSpec(memory_space=pltpu.VMEM)
HB = pl.BlockSpec(memory_space=pl.ANY)
SM = pl.BlockSpec(memory_space=pltpu.SMEM)


def up16(n):
    return (n + 15) // 16 * 16


def dot(a, b):
    return jnp.dot(a, b, preferred_element_type=F32)


def dot_t(a, b):
    return lax.dot_general(a, b, (((1,), (1,)), ((), ())), preferred_element_type=F32)


def t_dot(a, b):
    return lax.dot_general(a, b, (((0,), (0,)), ((), ())), preferred_element_type=F32)


def call(kernel, outs, ins, scratch=(), after=(), flops=0, bytes_accessed=0, grid=()):
    n_in, n_after = len(ins), len(after)

    def run(*refs):
        kernel(*refs[:n_in], *refs[n_in + n_after :])

    return pl.pallas_call(
        run,
        grid=grid,
        out_shape=[jax.ShapeDtypeStruct(s, t) for s, t, _ in outs],
        in_specs=[s for _, s in ins] + [HB] * n_after,
        out_specs=[s for _, _, s in outs],
        scratch_shapes=list(scratch),
        compiler_params=pltpu.CompilerParams(vmem_limit_bytes=50 * 2**20),
        cost_estimate=pl.CostEstimate(
            flops=flops, bytes_accessed=bytes_accessed, transcendentals=0
        ),
    )(*[a for a, _ in ins], *after)


def norm_parts(x):
    mean = jnp.mean(x, -1, keepdims=True)
    centre = x - mean
    scale = lax.rsqrt(jnp.mean(centre * centre, -1, keepdims=True) + 1e-06)
    return centre * scale, scale


def layer_norm(x, gain):
    return (norm_parts(x)[0] * gain).astype(BF)


def norm_back(x, gain, slope):
    unit, scale = norm_parts(x)
    terms = slope * unit
    inner = slope * gain
    inner = inner - jnp.mean(inner, -1, keepdims=True) - unit * jnp.mean(inner * unit, -1, keepdims=True)
    return inner * scale, terms


def gelu_both(h):
    k = 0.7978845608028654
    t = jnp.tanh(k * (h + 0.044715 * h * h * h))
    half = 0.5 * (1 + t)
    return h * half, half + 0.5 * h * (1 - t * t) * (k + (3 * 0.044715 * k) * h * h)


def add_both(mine, got, rows):
    return mine + jnp.concatenate([got[rows:], got[:rows]], 0).astype(F32)


def pair_masks():
    lane = lax.broadcasted_iota(jnp.int32, (1, 2 * HEAD_DIM), 1)
    return [(lane < HEAD_DIM).astype(BF), (lane >= HEAD_DIM).astype(BF)]


def key_mask(blk, rows, blk_len, longest):
    pos = lax.broadcasted_iota(jnp.int32, (rows, 1), 0)
    parts = []
    for j in range(4):
        last = jnp.where((blk ^ j) < longest, blk_len, blk_len - 1)
        parts.append(pos < last)
    return jnp.concatenate([jnp.where(p, 1.0, 0.0) for p in parts], 0) > 0.5


def attend_core(where, q, kv_own, kv_far, wp, rows, blk_len, longest, solo, far=None, after=()):
    half = q.shape[1]
    feat = wp.shape[1]
    pairs = half // (2 * HEAD_DIM)
    r2 = 2 * rows

    def kernel(where_ref, q_ref, ko_ref, *refs):
        refs = list(refs)
        take = lambda n: [refs.pop(0) for _ in range(n)]
        given = take(1 if far is None else 3)
        wp_ref, part_ref, low_ref, blend_ref, lse_ref = take(5)
        if far is None:
            kf_ref = given[0]
        else:
            (kf_ref,) = take(1)
            for j in range(2):
                kf_ref[pl.ds(j * rows, rows), :] = dot(given[j][...], given[2][:, half:]).astype(BF)
        ok = key_mask(where_ref[0], rows, blk_len, longest)
        masks = pair_masks()
        for p in range(pairs):
            at, vat = pl.ds(p * 128, 128), pl.ds(half + p * 128, 128)
            k = jnp.concatenate([ko_ref[:, at], kf_ref[:, at]], 0)
            v = jnp.concatenate([ko_ref[:, vat], kf_ref[:, vat]], 0)
            qp = q_ref[:, at]
            acc = None
            for h in range(2):
                s = dot_t(k, qp * masks[h]) * 0.125
                s = jnp.where(ok, s, -1e9)
                top = jnp.max(s, 0, keepdims=True)
                ex = jnp.exp(s - top)
                total = jnp.sum(ex, 0, keepdims=True)
                lse_ref[pl.ds(2 * p + h, 1), :] = top + jnp.log(total)
                shares = (ex * (1.0 / total)).astype(BF)
                out = t_dot(v * masks[h], shares)
                acc = out if acc is None else acc + out
            blend_ref[at, :] = acc.astype(BF)
        part = t_dot(blend_ref[...], wp_ref[...])
        part_ref[...] = part
        low_ref[...] = (part[rows:] if solo else part).astype(BF)

    outs = [
        ((r2, feat), F32, VM), ((rows if solo else r2, feat), BF, VM), ((half, r2), BF, VM), ((8, r2), F32, VM),
    ]
    ins = [(where, SM), (q, VM), (kv_own, VM)]
    if far is None:
        ins.append((kv_far, VM))
    else:
        ins += [(t, VM) for t in far]
        outs.append(((r2, feat), BF, VM))
    return call(
        kernel,
        outs,
        ins + [(wp, VM)],
        after=after,
        flops=2 * r2 * half * (8 * rows + feat),
        bytes_accessed=4 * 2**20,
    )


def attend_core_back(where, u_low, wp, blend, q, kv_own, kv_far, lse, rows, blk_len, longest, after=()):
    half = q.shape[1]
    feat = wp.shape[1]
    pairs = half // (2 * HEAD_DIM)
    r2 = 2 * rows

    def kernel(
        where_ref, u_ref, wp_ref, blend_ref, q_ref, ko_ref, kf_ref, lse_ref,
        dq_ref, own_ref, far_ref, wps_ref, bt_ref, dqt_ref,
    ):
        ok = key_mask(where_ref[0], rows, blk_len, longest)
        masks = pair_masks()
        sub = lax.broadcasted_iota(jnp.int32, (2 * HEAD_DIM, 1), 0)
        row_masks = [(sub < HEAD_DIM).astype(BF), (sub >= HEAD_DIM).astype(BF)]
        u = u_ref[...]
        bt_ref[...] = dot_t(wp_ref[...], u).astype(BF)
        for p in range(pairs):
            at, vat = pl.ds(p * 128, 128), pl.ds(half + p * 128, 128)
            k = jnp.concatenate([ko_ref[:, at], kf_ref[:, at]], 0)
            v = jnp.concatenate([ko_ref[:, vat], kf_ref[:, vat]], 0)
            qp = q_ref[:, at]
            bt = bt_ref[at, :]
            dqt = dk = dv = 0.0
            for h in range(2):
                qm = qp * masks[h]
                s = dot_t(k, qm) * 0.125
                shares = jnp.where(ok, jnp.exp(s - lse_ref[pl.ds(2 * p + h, 1), :]), 0.0)
                slope = dot(v * masks[h], bt)
                t = shares * slope
                ss = (t - shares * jnp.sum(t, 0, keepdims=True)).astype(BF)
                dqt += t_dot(k * masks[h], ss)
                dk += dot(ss, qm)
                dv += dot_t(shares.astype(BF), bt * row_masks[h])
            dqt_ref[at, :] = dqt * 0.125
            dk = dk * 0.125
            own_ref[:, at] = dk[:r2]
            own_ref[:, vat] = dv[:r2]
            far_ref[:, at] = dk[r2:].astype(BF)
            far_ref[:, vat] = dv[r2:].astype(BF)
        dq_ref[...] = dqt_ref[...].T.astype(BF)
        wps_ref[...] = dot(blend_ref[...], u).astype(BF)

    return call(
        kernel,
        [
            ((r2, half), BF, VM), ((r2, 2 * half), F32, VM), ((r2, 2 * half), BF, VM),
            ((half, feat), BF, VM),
        ],
        [
            (where, SM), (u_low, VM), (wp, VM), (blend, VM), (q, VM), (kv_own, VM), (kv_far, VM),
            (lse, VM),
        ],
        scratch=[pltpu.VMEM((half, r2), BF), pltpu.VMEM((half, r2), F32)],
        after=after,
        flops=2 * r2 * half * (20 * rows + 2 * feat),
        bytes_accessed=6 * 2**20,
    )


def start_all(copies):
    for c in copies:
        c.start()


def wait_all(copies):
    for c in copies:
        c.wait()


def attend_copies(e, refs, w_ref, p_ref, small_ref, sems, skip):
    copies = []

    def add(src, dst):
        copies.append(pltpu.make_async_copy(src, dst, sems.at[len(copies)]))

    n = w_ref.shape[0] // 4
    half = p_ref.shape[0]
    m = half // 4
    for j in range(4):
        to = e ^ j
        rows, prows = pl.ds(pl.multiple_of(to * n, 16), n), pl.ds(pl.multiple_of(to * m, 16), m)
        a, b, at = (refs[j], refs[j], 2 * n + skip) if j < 3 else (refs[3], refs[4], 0)
        for g in range(2):
            add(a.at[pl.ds(g * n, n)], w_ref.at[rows, pl.ds(g * half, half)])
        add(b.at[pl.ds(at, n)], w_ref.at[rows, pl.ds(2 * half, half)])
        add(b.at[pl.ds(at + n, m)], p_ref.at[prows, pl.ds(0, half)])
        add(b.at[pl.ds(at + n + m, m)], p_ref.at[prows, pl.ds(half, half)])
        if small_ref is not None:
            for g in range(3):
                srows = pl.ds(pl.multiple_of(to * n + g * (n // 3), 16), n // 3)
                add(b.at[pl.ds(at + n + 2 * m, n // 3), pl.ds(128 * g, 128)], small_ref.at[srows])
    return copies


def attend_first(where, tokens, small_rows, blocks, rows, skip, after=()):
    blk_len, feat = tokens[0].shape
    half = feat // 2
    r2 = 2 * rows

    def kernel(where_ref, *refs):
        refs = list(refs)
        take = lambda n: [refs.pop(0) for _ in range(n)]
        tok, block_refs = take(4), take(5)
        x_ref, normed_ref, q_ref, kv_ref, far_ref, w_ref, p_ref, small_ref, rows_ref, all_ref, sems = take(11)
        copies = attend_copies(where_ref[1], block_refs, w_ref, p_ref, small_ref, sems, skip)
        start_all(copies)
        all_ref[...] = jnp.zeros_like(all_ref)
        for j in range(4):
            all_ref[pl.ds(j * rows, blk_len), :] = tok[j][...].astype(F32)
        x = all_ref[...]
        x_ref[...] = x[:r2]
        unit = norm_parts(x)[0]
        wait_all(copies)
        turned = small_ref[...].astype(F32).T
        rows_ref[...] = turned[: rows_ref.shape[0]]
        normed = (unit * turned[0:1]).astype(BF)
        normed_ref[...] = normed[:r2]
        q_ref[...] = dot(normed[:r2], w_ref[:, :half]).astype(BF)
        kv = dot(normed, w_ref[:, half:]).astype(BF)
        kv_ref[...] = kv[:r2]
        far_ref[...] = kv[r2:]

    return call(
        kernel,
        [
            ((r2, feat), F32, VM), ((r2, feat), BF, VM), ((r2, half), BF, VM), ((r2, feat), BF, VM),
            ((r2, feat), BF, VM), ((feat, 3 * half), BF, VM), ((half, feat), BF, VM),
            ((feat, 128), BF, VM), ((small_rows, feat), F32, VM),
        ],
        [(where, SM)] + [(t, VM) for t in tokens] + [(t, HB) for t in blocks],
        scratch=[pltpu.VMEM((2 * r2, feat), F32), pltpu.SemaphoreType.DMA((32,))],
        after=after,
        flops=2 * r2 * feat * 5 * half,
        bytes_accessed=6 * 2**20,
    )


def norm_next(x, part, got, gains, gain_row, rows, after=()):
    r2, feat = x.shape

    def kernel(x_ref, part_ref, got_ref, gains_ref, x2_ref, normed_ref, own_ref):
        x2 = add_both(x_ref[...] + part_ref[...], got_ref[...], rows)
        x2_ref[...] = x2
        normed = layer_norm(x2, gains_ref[pl.ds(gain_row, 1), :])
        normed_ref[...] = normed
        own_ref[...] = normed[:rows]

    return call(
        kernel,
        [((r2, feat), F32, VM), ((r2, feat), BF, VM), ((rows, feat), BF, VM)],
        [(x, VM), (part, VM), (got, VM), (gains, VM)],
        after=after,
        bytes_accessed=5 * 2**20,
    )


def attend_next(where, normed, source, after=()):
    r2, feat = normed.shape
    half = feat // 2
    packed = source.ndim == 4

    def kernel(where_ref, normed_ref, source_ref, q_ref, kv_ref, *more):
        if packed:
            w_ref, sems = more
            r = source_ref.shape[2] // 4
            copies = []
            for c in range(4):
                for j in range(4):
                    at = pl.multiple_of((where_ref[1] ^ j) * (feat // 4) + c * r, 16)
                    for g in range(3):
                        copies.append(pltpu.make_async_copy(
                            source_ref.at[c, j, pl.ds(g * r, r)],
                            w_ref.at[pl.ds(at, r), pl.ds(g * half, half)], sems.at[len(copies)],
                        ))
            start_all(copies)
            wait_all(copies)
        else:
            w_ref = source_ref
        normed = normed_ref[...]
        q_ref[...] = dot(normed, w_ref[:, :half]).astype(BF)
        kv_ref[...] = dot(normed, w_ref[:, half:]).astype(BF)

    out = call(
        kernel,
        [((r2, half), BF, VM), ((r2, feat), BF, VM)] + ([((feat, 3 * half), BF, VM)] if packed else []),
        [(where, SM), (normed, VM), (source, HB if packed else VM)],
        scratch=[pltpu.SemaphoreType.DMA((48,))] if packed else [],
        after=after,
        flops=2 * r2 * feat * 3 * half,
        bytes_accessed=4 * 2**20,
    )
    return out if packed else [*out, source]


def widen_copies(e, blocks, wi_ref, wo_ref, sems):
    copies = []
    feat = wo_ref.shape[1]
    n = feat // 4
    for h in range(2):
        for j in range(4):
            src = blocks[j].at[h] if j < 3 else blocks[3 + h]
            at = (e ^ j) * n
            for part, dst in (
                (0, wi_ref.at[pl.ds(pl.multiple_of(at, 16), n), pl.ds(h * feat, feat)]),
                (1, wo_ref.at[pl.ds(pl.multiple_of(at + h * feat, 16), n)]),
            ):
                copies.append(pltpu.make_async_copy(src.at[part], dst, sems.at[len(copies)]))
    return copies


def widen_forward(where, x, part, got, gains, blocks, rows, after=()):
    r2, feat = x.shape
    wide = 2 * feat
    tile = 384

    def kernel(
        where_ref, x_ref, part_ref, got_ref, gains_ref, z0, z1, z2, a3, b3,
        x1_ref, normed_ref, hidden_ref, out_ref, low_ref, wi_ref, wo_ref, sems,
    ):
        copies = widen_copies(where_ref[1], (z0, z1, z2, a3, b3), wi_ref, wo_ref, sems)
        start_all(copies)
        x1 = add_both(x_ref[...] + part_ref[...], got_ref[...], rows)
        x1_ref[...] = x1
        normed_ref[...] = layer_norm(x1, gains_ref[pl.ds(1, 1), :])
        out_ref[...] = jnp.zeros_like(out_ref)
        for half in range(2):
            wait_all(copies[8 * half : 8 * half + 8])

            @pl.loop(half * (feat // tile), (half + 1) * (feat // tile))
            def _(t):
                at = pl.ds(pl.multiple_of(t * tile, 128), tile)
                h = dot(normed_ref[...], wi_ref[:, at])
                hidden_ref[:, at] = h.astype(BF)
                out_ref[...] += dot(gelu_both(h)[0].astype(BF), wo_ref[at, :])

        low_ref[...] = out_ref[...].astype(BF)

    return call(
        kernel,
        [
            ((r2, feat), F32, VM), ((r2, feat), BF, VM), ((r2, wide), BF, VM), ((r2, feat), F32, VM),
            ((r2, feat), BF, VM),
        ],
        [(where, SM), (x, VM), (part, VM), (got, VM), (gains, VM)] + [(t, HB) for t in blocks],
        scratch=[
            pltpu.VMEM((feat, wide), BF), pltpu.VMEM((wide, feat), BF), pltpu.SemaphoreType.DMA((16,)),
        ],
        after=after,
        flops=4 * r2 * feat * wide,
        bytes_accessed=16 * 2**20,
    )


def widen_back(where, u, x, gains, part, got, normed, hidden, blocks, first, rows, columns, after=()):
    r2, feat = u.shape
    wide = 2 * feat
    tile = 384
    n = feat // 4

    def kernel(
        where_ref, u_ref, x_ref, gains_ref, part_ref, got_ref, normed_ref, hidden_ref,
        z0, z1, z2, a3, b3, u2_ref, out_ref, low_ref, *more,
    ):
        outs, (ulow_ref, turned_ref, wis_ref, wos_ref, wi_ref, wo_ref, in_sems, sems) = more[:-8], more[-8:]
        arriving = widen_copies(where_ref[1], (z0, z1, z2, a3, b3), wi_ref, wo_ref, in_sems)
        start_all(arriving)
        slope = add_both(part_ref[...], got_ref[...], rows)
        u2 = u_ref[...] + norm_back(x_ref[...], gains_ref[pl.ds(2, 1), :], slope)[0]
        u2_ref[...] = u2
        ulow_ref[...] = u2.astype(BF)
        turned_ref[...] = normed_ref[...].T
        out_ref[...] = jnp.zeros_like(out_ref)

        copies = []
        slots = (0, 3 - first, first, 3)

        def add(h, at, size, dst):
            wide_at = pl.ds(pl.multiple_of(at, 16), size)
            deep_at = pl.ds(pl.multiple_of(at + h * feat, 16), size)
            for i, src in enumerate((wis_ref.at[wide_at, pl.ds(h * feat, feat)], wos_ref.at[deep_at])):
                copies.append(pltpu.make_async_copy(src, dst.at[i], sems.at[len(copies)]))
                copies[-1].start()

        for h in range(2):
            wait_all(arriving[8 * h : 8 * h + 8])

            @pl.loop(h * (feat // tile), (h + 1) * (feat // tile))
            def _(t):
                at = pl.ds(pl.multiple_of(t * tile, 128), tile)
                ulow = ulow_ref[...]
                act, dact = gelu_both(hidden_ref[:, at].astype(F32))
                hs = (dact * dot_t(ulow, wo_ref[at, :])).astype(BF)
                wos_ref[at, :] = t_dot(act.astype(BF), ulow).astype(BF)
                wis_ref[:, at] = dot(turned_ref[...], hs).astype(BF)
                out_ref[...] += dot_t(hs, wi_ref[:, at])

            for i, j in enumerate(slots):
                to = (where_ref[1] ^ j) * n
                if h == 1 and columns:
                    for c in range(4):
                        add(1, to + c * (n // 4), n // 4, outs[2].at[c, i])
                else:
                    add(h, to, n, outs[2 * h + i // 2].at[i % 2])

        low_ref[...] = out_ref[...].astype(BF)
        wait_all(copies)

    block = ((2, 2, n, feat), BF, HB)
    more = [((4, 4, 2, n // 4, feat), BF, HB)] if columns else [block] * 2
    return call(
        kernel,
        [((r2, feat), F32, VM), ((r2, feat), F32, VM), ((r2, feat), BF, VM)] + [block] * 2 + more,
        [
            (where, SM), (u, VM), (x, VM), (gains, VM), (part, VM), (got, VM), (normed, VM),
            (hidden, VM),
        ]
        + [(t, HB) for t in blocks],
        scratch=[
            pltpu.VMEM((r2, feat), BF), pltpu.VMEM((feat, r2), BF), pltpu.VMEM((feat, wide), BF),
            pltpu.VMEM((wide, feat), BF), pltpu.VMEM((feat, wide), BF), pltpu.VMEM((wide, feat), BF),
            pltpu.SemaphoreType.DMA((16,)), pltpu.SemaphoreType.DMA((40,)),
        ],
        after=after,
        flops=10 * r2 * feat * wide,
        bytes_accessed=24 * 2**20,
    )


def attend_proj_back(where, dq, own, got, normed, w, wps, small, firsts, rows, last, after=()):
    r2, feat = normed.shape
    half = feat // 2
    n, m = feat // 4, half // 4
    tile = 384
    extra = 0 if small is None else n // 3

    def kernel(where_ref, dq_ref, own_ref, got_ref, normed_ref, w_ref, wps_ref, *refs):
        refs = list(refs)
        take = lambda k: [refs.pop(0) for _ in range(k)]
        small_ref = take(1)[0] if extra else None
        out_ref, low_ref = take(2)
        sides = [take(2) for _ in firsts]
        packed_ref, turned_ref, ws_ref, sm_ref, sems = take(5)
        packed_ref[:, :half] = dq_ref[...]
        packed_ref[:, half:] = (own_ref[...] + got_ref[...].astype(F32)).astype(BF)
        out = dot_t(packed_ref[...], w_ref[...])
        out_ref[...] = out[: out_ref.shape[0]]
        low_ref[...] = (out[rows:] if last else out).astype(BF)
        turned_ref[...] = normed_ref[...].T

        @pl.loop(0, 3 * half // tile)
        def _(t):
            at = pl.ds(pl.multiple_of(t * tile, 128), tile)
            ws_ref[:, at] = dot(turned_ref[...], packed_ref[:, at]).astype(BF)

        if extra:
            wide = jnp.concatenate(
                [small_ref[...], jnp.zeros((128 - small_ref.shape[0], feat), F32)], 0
            )
            sm_ref[...] = wide.T.astype(BF)
        copies = []

        def add(src, dst):
            copies.append(pltpu.make_async_copy(src, dst, sems.at[len(copies)]))

        for lane, first in enumerate(firsts):
            one = len(firsts) == 1
            skip = 2 * n if lane == 1 else 0
            for ref, js in zip(sides[lane], ((0, 3 - first), (first, 3))):
                for i, j in enumerate(js):
                    to = where_ref[1] ^ j
                    at, pat = pl.ds(pl.multiple_of(to * n, 16), n), pl.ds(pl.multiple_of(to * m, 16), m)
                    for g in range(3):
                        if one or (g == 2) == (lane == 1):
                            add(ws_ref.at[at, pl.ds(g * half, half)], ref.at[i, pl.ds(g * n - skip, n)])
                    for g in range(2):
                        if one or lane == 1:
                            add(
                                wps_ref.at[pat, pl.ds(g * half, half)],
                                ref.at[i, pl.ds(3 * n + g * m - skip, m)],
                            )
                    if extra:
                        for g in range(3):
                            sat = pl.ds(pl.multiple_of(to * n + g * extra, 16), extra)
                            add(sm_ref.at[sat], ref.at[i, pl.ds(3 * n + 2 * m, extra), pl.ds(128 * g, 128)])
        start_all(copies)
        wait_all(copies)

    n_out = rows if last else r2
    deep = 3 * n + 2 * m + extra
    deeps = [deep] * 2 if len(firsts) == 1 else [2 * n] * 2 + [n + 2 * m] * 2
    return call(
        kernel,
        [((n_out, feat), F32, VM), ((n_out, feat), BF, VM)] + [((2, k, half), BF, HB) for k in deeps],
        [(where, SM), (dq, VM), (own, VM), (got, VM), (normed, VM), (w, VM), (wps, VM)]
        + ([(small, VM)] if extra else []),
        scratch=[
            pltpu.VMEM((r2, 3 * half), BF), pltpu.VMEM((feat, r2), BF), pltpu.VMEM((feat, 3 * half), BF),
            pltpu.VMEM((feat, 128), BF), pltpu.SemaphoreType.DMA((32,)),
        ],
        after=after,
        flops=4 * r2 * feat * 3 * half,
        bytes_accessed=10 * 2**20,
    )


def spread_attend_rows(t, store):
    half = t.shape[1]
    n, m = half // 2, half // 4
    r = n // 4
    for z in range(4):
        for g in range(3):
            store(z, g * half, t[g * n + z * r : g * n + (z + 1) * r])
        at = 3 * n + z * (m // 4)
        p = [t[at + g * m : at + g * m + m // 4] for g in range(2)]
        store(z, 3 * half, jnp.concatenate(p, 0))
    if t.shape[0] > 3 * n + 2 * m:
        sm = t[3 * n + 2 * m :]
        sm = jnp.concatenate([sm[:, 128 * g : 128 * (g + 1)] for g in range(3)], 0)
        for z in range(4):
            store(z, 4 * half, sm[z * r : (z + 1) * r])


def spread_pair_rows(t, first, store):
    r = t.shape[1] // 4
    for i in range(2):
        for z in range(4):
            store(z, first + i * t.shape[2], t[i, z * r : (z + 1) * r])


def columns_of(groups, after=()):
    wide = 0
    for t in groups:
        wide += 2 * t.shape[2] if t.ndim == 3 else 4 * t.shape[1] + (128 if t.shape[0] > 2 * t.shape[1] else 0)
    r = groups[0].shape[1] // 4 if groups[0].ndim == 3 else groups[0].shape[1] // 8

    def kernel(*refs):
        out = refs[len(groups)]

        def store(z, lane, value):
            out[z, :, pl.ds(lane, value.shape[1])] = value.astype(BF)

        at = 0
        for ref in refs[: len(groups)]:
            t = ref[...]
            if t.ndim == 3:
                spread_pair_rows(t, at, store)
                at += 2 * t.shape[2]
            else:
                spread_attend_rows(t, lambda z, lane, value, at=at: store(z, at + lane, value))
                at += 4 * t.shape[1] + (128 if t.shape[0] > 2 * t.shape[1] else 0)

    return call(
        kernel, [((4, r, wide), BF, VM)], [(t, VM) for t in groups], after=after,
        bytes_accessed=3 * 2**20,
    )[0]


def last_columns(where, upper, lower, pair, after=()):
    half = upper.shape[1]
    r = half // 8
    wide = 4 * half + 2 * pair.shape[2]

    def kernel(where_ref, upper_ref, lower_ref, pair_ref, *refs):
        outs, scratch = refs[:4], refs[4]

        def store(z, lane, value):
            scratch[z, :, pl.ds(lane, value.shape[1])] = value

        spread_attend_rows(jnp.concatenate([upper_ref[...], lower_ref[...]], 0), store)
        spread_pair_rows(pair_ref[...], 4 * half, store)
        c = where_ref[2]
        outs[0][...] = scratch[c]
        for j in range(1, 4):
            outs[j][...] = scratch[c ^ j].astype(BF)

    return call(
        kernel,
        [((r, wide), F32, VM)] + [((r, wide), BF, VM)] * 3,
        [(where, SM), (upper, VM), (lower, VM), (pair, VM)],
        scratch=[pltpu.VMEM((4, r, wide), F32)],
        after=after,
        bytes_accessed=6 * 2**20,
    )


def join_upstream(u_own, u_sib, rows):
    feat = u_own.shape[1]

    def kernel(o_ref, s_ref, u_ref, low_ref):
        u_ref[pl.ds(0, rows), :] = o_ref[...]
        u_ref[pl.ds(rows, rows), :] = s_ref[...].astype(F32)
        low_ref[pl.ds(0, rows), :] = o_ref[...].astype(BF)
        low_ref[pl.ds(rows, rows), :] = s_ref[...]

    return call(
        kernel, [((2 * rows, feat), F32, VM), ((2 * rows, feat), BF, VM)], [(u_own, VM), (u_sib, VM)],
        bytes_accessed=2**21,
    )


def norm_step(u, x, gains, gain_row, part, got, rows, last, after=()):
    feat = x.shape[1]
    n = rows if last else 2 * rows

    def kernel(u_ref, x_ref, gains_ref, part_ref, got_ref, *outs):
        if last:
            slope = part_ref[...] + got_ref[...].astype(F32)
        else:
            slope = add_both(part_ref[...], got_ref[...], rows)
        u2 = u_ref[:n] + norm_back(x_ref[:n], gains_ref[pl.ds(gain_row, 1), :], slope)[0]
        low = outs[-1]
        low[...] = u2[: low.shape[0]].astype(BF)
        if not last:
            outs[0][...] = u2

    outs = [((last if last else n, feat), BF, VM)]
    return call(
        kernel,
        outs if last else [((n, feat), F32, VM)] + outs,
        [(u, VM), (x, VM), (gains, VM), (part, VM), (got, VM)],
        after=after,
        bytes_accessed=6 * 2**20,
    )


def picks(index, turn, cap, cap_rows, experts):
    at = lax.broadcasted_iota(jnp.int32, (1, experts * cap_rows), 1)
    out = []
    for k in range(TOP):
        chosen, slot = index[:, k : k + 1], index[:, TOP + k : TOP + k + 1]
        place = chosen if turn is None else chosen ^ turn
        target = jnp.where(slot < cap, place * cap_rows + slot, -1)
        out.append(jnp.where(at == target, 1.0, 0.0).astype(BF))
    return out


def lane_at(index, k):
    lane = lax.broadcasted_iota(jnp.int32, (1, 128), 1)
    return jnp.where(lane == index[:, k : k + 1] + 4, 1.0, 0.0)


def present_mask(blk, rows, blk_len, longest):
    pos = lax.broadcasted_iota(jnp.int32, (rows, 1), 0)
    last = jnp.where(blk < longest, blk_len, blk_len - 1)
    return jnp.where(pos < last, 1.0, 0.0)


def route(where, x, part, got, gains, small, cot, index, experts, cap, rows, blk_len, longest, fast, after=()):
    feat = x.shape[1]
    cap_rows = up16(cap)

    def kernel(where_ref, x_ref, part_ref, got_ref, gains_ref, small_ref, cot_ref, index_ref,
               x3_ref, moe_ref, gates_ref, up_ref, *blocks):
        x3 = x_ref[:rows] + part_ref[:rows] + got_ref[...].astype(F32)
        x3_ref[...] = x3
        moe = layer_norm(x3, gains_ref[pl.ds(3, 1), :])
        moe_ref[...] = moe
        lane = lax.broadcasted_iota(jnp.int32, (1, 128), 1)
        logits = dot(moe, small_ref[...])
        logits = jnp.where((lane >= 4) & (lane < 4 + experts), logits, -1e30)
        ex = jnp.exp(logits - jnp.max(logits, -1, keepdims=True))
        gates = ex / jnp.sum(ex, -1, keepdims=True)
        gates_ref[...] = gates
        up_ref[...] = jnp.zeros_like(up_ref)
        up_ref[pl.ds(0, blk_len), :] = cot_ref[...].astype(F32)
        up = up_ref[...] * present_mask(where_ref[0], rows, blk_len, longest)
        up_ref[...] = up
        index = index_ref[...]
        pick = picks(index, where_ref[1] if fast else None, cap, cap_rows, experts)
        sent = t_dot(pick[0] + pick[1], moe).astype(BF)
        slope = 0.0
        for k in range(TOP):
            gate = jnp.sum(gates * lane_at(index, k), -1, keepdims=True)
            slope += t_dot(pick[k], (gate * up).astype(BF))
        slope = slope.astype(BF)
        for j, ref in enumerate(blocks):
            ref[pl.ds(0, cap_rows), :] = sent[j * cap_rows : (j + 1) * cap_rows]
            ref[pl.ds(cap_rows, cap_rows), :] = slope[j * cap_rows : (j + 1) * cap_rows]

    return call(
        kernel,
        [((rows, feat), F32, VM), ((rows, feat), BF, VM), ((rows, 128), F32, VM), ((rows, feat), F32, VM)]
        + [((2 * cap_rows, feat), BF, VM)] * experts,
        [(where, SM), (x, VM), (part, VM), (got, VM), (gains, VM), (small, VM), (cot, VM), (index, VM)],
        after=after,
        flops=6 * rows * experts * cap_rows * feat,
        bytes_accessed=5 * 2**20,
    )


def experts_forward(blocks, own, sib, cap_rows, after=()):
    feat, wide = own[0].shape
    tile = 512 if wide % 512 == 0 else wide
    n = len(blocks) * cap_rows
    steps = wide // tile

    def kernel(*refs):
        refs = list(refs)
        take = lambda k: [refs.pop(0) for _ in range(k)]
        ins, weights = take(len(blocks)), take(4)
        take(len(after))
        outs = take(len(blocks))
        rows_ref, slope_ref, res_ref, back_ref = take(4)
        t = pl.program_id(0)

        @pl.when(t == 0)
        def _():
            for j, ref in enumerate(ins):
                at = pl.ds(j * cap_rows, cap_rows)
                rows_ref[at, :] = ref[pl.ds(0, cap_rows), :]
                slope_ref[at, :] = ref[pl.ds(cap_rows, cap_rows), :]
            res_ref[...] = jnp.zeros_like(res_ref)
            back_ref[...] = jnp.zeros_like(back_ref)

        def step(wi_ref, wo_ref):
            act, dact = gelu_both(dot(rows_ref[...], wi_ref[...]))
            hs = (dact * dot_t(slope_ref[...], wo_ref[...])).astype(BF)
            res_ref[...] += dot(act.astype(BF), wo_ref[...])
            back_ref[...] += dot_t(hs, wi_ref[...])

        @pl.when(t < steps)
        def _():
            step(*weights[:2])

        @pl.when(t >= steps)
        def _():
            step(*weights[2:])

        @pl.when(t == 2 * steps - 1)
        def _():
            for j, ref in enumerate(outs):
                at = pl.ds(j * cap_rows, cap_rows)
                ref[pl.ds(0, cap_rows), :] = res_ref[at, :].astype(BF)
                ref[pl.ds(cap_rows, cap_rows), :] = back_ref[at, :].astype(BF)

    blk = (2 * cap_rows, feat)
    whole = pl.BlockSpec(blk, lambda t: (0, 0))
    first = lambda t: jnp.minimum(t, steps - 1)
    later = lambda t: jnp.maximum(t - steps, 0)
    specs = []
    for place in (first, later):
        specs.append(pl.BlockSpec((feat, tile), lambda t, place=place: (0, place(t))))
        specs.append(pl.BlockSpec((tile, feat), lambda t, place=place: (place(t), 0)))
    return pl.pallas_call(
        kernel,
        grid=(2 * steps,),
        out_shape=[jax.ShapeDtypeStruct(blk, BF)] * len(blocks),
        in_specs=[whole] * len(blocks) + specs + [HB] * len(after),
        out_specs=[whole] * len(blocks),
        scratch_shapes=[
            pltpu.VMEM((n, feat), BF), pltpu.VMEM((n, feat), BF),
            pltpu.VMEM((n, feat), F32), pltpu.VMEM((n, feat), F32),
        ],
        compiler_params=pltpu.CompilerParams(
            vmem_limit_bytes=62 * 2**20, dimension_semantics=("arbitrary",)
        ),
        cost_estimate=pl.CostEstimate(
            flops=16 * n * feat * wide, bytes_accessed=20 * 2**20, transcendentals=0
        ),
    )(*blocks, *own, *sib, *after)


def expert_slopes(every, w_in, w_out, got, after=()):
    feat, wide = w_in.shape
    tile = 512 if wide % 512 == 0 else wide
    steps = wide // tile
    groups, experts, cap_rows = every.shape[0], every.shape[1], every.shape[2] // 2
    total = groups * experts * cap_rows
    kind = BF if got is None else F32

    def kernel(*refs):
        refs = list(refs)
        take = lambda k: [refs.pop(0) for _ in range(k)]
        every_ref, wi_ref, wo_ref = take(3)
        got_refs = take(2) if got is not None else None
        take(len(after))
        wis_ref, wos_ref, rows_ref, slope_ref, turned_ref, sems = take(6)

        @pl.when(pl.program_id(0) == 0)
        def _():
            copies = []
            for k in range(groups):
                for j in range(experts):
                    at = pl.ds((k * experts + j) * cap_rows, cap_rows)
                    for i, ref in enumerate((rows_ref, slope_ref)):
                        copies.append(pltpu.make_async_copy(
                            every_ref.at[k, j, pl.ds(i * cap_rows, cap_rows)], ref.at[at],
                            sems.at[len(copies)],
                        ))
            start_all(copies)
            per = total // groups
            for k in range(groups):
                wait_all(copies[k * 2 * experts : (k + 1) * 2 * experts])
                at = pl.ds(k * per, per)
                turned_ref[:, at] = rows_ref[at, :].T

        act, dact = gelu_both(dot(rows_ref[...], wi_ref[...]))
        hs = (dact * dot_t(slope_ref[...], wo_ref[...])).astype(BF)
        wis = dot(turned_ref[...], hs)
        wos = t_dot(act.astype(BF), slope_ref[...])
        if got is not None:
            wis, wos = wis + got_refs[0][...].astype(F32), wos + got_refs[1][...].astype(F32)
        wis_ref[...] = wis.astype(kind)
        wos_ref[...] = wos.astype(kind)

    wi_spec = pl.BlockSpec((feat, tile), lambda t: (0, t))
    wo_spec = pl.BlockSpec((tile, feat), lambda t: (t, 0))
    return pl.pallas_call(
        kernel,
        grid=(steps,),
        out_shape=[jax.ShapeDtypeStruct((feat, wide), kind), jax.ShapeDtypeStruct((wide, feat), kind)],
        in_specs=[HB] + [wi_spec, wo_spec] * (1 if got is None else 2) + [HB] * len(after),
        out_specs=[wi_spec, wo_spec],
        scratch_shapes=[
            pltpu.VMEM((total, feat), BF), pltpu.VMEM((total, feat), BF), pltpu.VMEM((feat, total), BF),
            pltpu.SemaphoreType.DMA((2 * groups * experts,)),
        ],
        compiler_params=pltpu.CompilerParams(
            vmem_limit_bytes=56 * 2**20, dimension_semantics=("arbitrary",)
        ),
        cost_estimate=pl.CostEstimate(
            flops=8 * total * feat * wide, bytes_accessed=20 * 2**20, transcendentals=0
        ),
    )(every, w_in, w_out, *(got or ()), *after)


def combine(where, blocks, x3, moe, gates, up, index, small, gains, small_rows, experts, cap, rows, blk_len, longest, fast, after=()):
    feat = x3.shape[1]
    cap_rows = up16(cap)
    n = experts * cap_rows

    def kernel(where_ref, *refs):
        refs = list(refs)
        take = lambda k: [refs.pop(0) for _ in range(k)]
        ins = take(experts)
        x3_ref, moe_ref, gates_ref, up_ref, index_ref, small_ref, gains_ref = take(7)
        acts_ref, u_ref, low_ref, slopes_ref, result_ref, back_ref = take(6)
        for j, ref in enumerate(ins):
            at = pl.ds(j * cap_rows, cap_rows)
            result_ref[at, :] = ref[pl.ds(0, cap_rows), :]
            back_ref[at, :] = ref[pl.ds(cap_rows, cap_rows), :]
        index, gates, up, moe = index_ref[...], gates_ref[...], up_ref[...], moe_ref[...]
        pick = picks(index, where_ref[1] if fast else None, cap, cap_rows, experts)
        x3 = x3_ref[...]
        acts, all_slope = x3, 0.0
        for k in range(TOP):
            at_k = lane_at(index, k)
            gate = jnp.sum(gates * at_k, -1, keepdims=True)
            picked = dot(pick[k], result_ref[...])
            acts = acts + gate * picked
            all_slope += jnp.sum(up * picked, -1, keepdims=True) * at_k
        acts = acts * present_mask(where_ref[0], rows, blk_len, longest)
        acts_ref[...] = acts[:blk_len].astype(BF)
        logit = (gates * (all_slope - jnp.sum(gates * all_slope, -1, keepdims=True))).astype(BF)
        slope = dot(pick[0] + pick[1], back_ref[...]) + dot_t(logit, small_ref[...])
        dx, terms = norm_back(x3, gains_ref[pl.ds(3, 1), :], slope)
        u = up + dx
        u_ref[...] = u
        low_ref[...] = u.astype(BF)
        slopes_ref[...] = t_dot(logit, moe)[:small_rows]
        slopes_ref[pl.ds(3, 1), :] = jnp.sum(terms, 0, keepdims=True)

    return call(
        kernel,
        [((blk_len, feat), BF, VM), ((rows, feat), F32, VM), ((rows, feat), BF, VM), ((small_rows, feat), F32, VM)],
        [(where, SM)] + [(b, VM) for b in blocks]
        + [(t, VM) for t in (x3, moe, gates, up, index, small, gains)],
        scratch=[pltpu.VMEM((n, feat), BF), pltpu.VMEM((n, feat), BF)],
        after=after,
        flops=6 * rows * n * feat,
        bytes_accessed=5 * 2**20,
    )


def tie(xs, *after):
    return list(lax.optimization_barrier((*xs, *after)))[: len(xs)]


class Links:
    def __init__(self, mesh):
        self.E = mesh.shape["expert"]
        self.C = mesh.shape["context"]
        self.D = mesh.shape["dp"]
        assert self.C == 4 and self.D == 2 and self.E % 2 == 0
        self.fast = self.E == 4
        self.chips = self.E * self.C
        flat = lambda e, c, d: (e * self.C + c) * self.D + d
        self.team = [
            (flat(e, c, d), flat((e // 2) * 2 + c // 2, 2 * (e % 2) + d, c % 2))
            for e in range(self.E)
            for c in range(self.C)
            for d in range(self.D)
        ]
        self.to_lane = [(f, (f % self.chips) * 2 + f // self.chips) for f in range(2 * self.chips)]
        self.from_lane = [(b, a) for a, b in self.to_lane]

    def move(self, x):
        return lax.ppermute(x, ALL, self.team)

    def xor(self, x, axis, j):
        n = {"expert": self.E, "context": self.C, "dp": self.D}[axis]
        return lax.ppermute(x, axis, [(i, i ^ j) for i in range(n)])

    def sib(self, x):
        return self.xor(x, "dp", 1)

    def partner(self, x):
        return self.xor(x, "expert", 1)

    def column(self, x, *hold):
        c = lax.axis_index("context")
        got = tie([x] + [self.xor(x, "context", j) for j in range(1, 4)], *hold)
        pick = lambda k: jnp.where(
            c & 2 == 0, jnp.where(c & 1 == 0, got[k], got[k ^ 1]), jnp.where(c & 1 == 0, got[k ^ 2], got[k ^ 3])
        )
        return jnp.stack([pick(k) for k in range(4)])

    def plane_sum(self, keep, send, first, hold):
        (got,) = tie([self.xor(send, "expert", first)], *hold[0])
        got = got.astype(F32)
        give = (keep[1].astype(F32) + got[1]).astype(BF)
        (far,) = tie([self.xor(give, "expert", 3 - first)], *hold[1])
        return keep[0].astype(F32) + got[0] + far.astype(F32), give

    def column_sum(self, x, *hold):
        c = lax.axis_index("context")
        low = x.astype(BF)
        got = [self.xor(lax.dynamic_index_in_dim(low, c ^ j, 0, False), "context", j) for j in range(1, 4)]
        got = tie(got, *hold)
        total = lax.dynamic_index_in_dim(x, c, 0, False)
        for t in got:
            total = total + t.astype(F32)
        return total

    def swap_blocks(self, x):
        if not self.fast:
            return list(lax.all_to_all(jnp.stack(x), "expert", 0, 0, tiled=True))
        return [x[0]] + [self.xor(x[j], "expert", j) for j in range(1, 4)]


def lane_rows(links, mine, d):
    keep = lax.dynamic_index_in_dim(mine, d, 0, False)
    got = links.sib(lax.dynamic_index_in_dim(mine, 1 - d, 0, False))
    return jnp.where(d == 0, jnp.concatenate([keep, got], 0), jnp.concatenate([got, keep], 0))


def in_order(d, own, other):
    return jnp.where(d == 0, jnp.stack([own, other]), jnp.stack([other, own]))


class Weights:
    def __init__(self, links, rdev, feat, ff):
        self.links, self.rdev, self.feat, self.ff = links, rdev, feat, ff
        self.d = lax.axis_index("dp")
        self.half = feat // 2

    def split_attend(self, w):
        w = w.reshape(self.rdev, 3, 2, self.half).transpose(2, 0, 1, 3)
        return w.reshape(2, self.rdev, 3 * self.half)

    def split_widen(self, w):
        w = w.reshape(self.rdev, self.links.chips, 2, 2, -1).transpose(2, 0, 3, 1, 4)
        return w.reshape(2, self.rdev, self.ff // 2)

    def pack_attend(self, w, p, small):
        parts = [w, jnp.concatenate([p[:, : self.half], p[:, self.half :]], 0)]
        if small is not None:
            parts.append(jnp.pad(small, ((0, 0), (0, 128 - small.shape[1]))))
        return jnp.concatenate(parts, 1)

    def pack_wide(self, wout):
        h = wout.shape[0] // 2
        return jnp.concatenate([wout[:h], wout[h:]], 1)

    def column(self, buf, *hold):
        if self.links.fast:
            return self.links.column(buf, *hold)
        return lax.all_gather(buf, CHIPS, axis=0, tiled=False)

    def cut(self, x):
        return x if self.links.fast else x.reshape(4, -1, x.shape[-1])

    def pack_block(self, quad, between):
        f, h, r = self.feat, self.half, self.rdev
        n = quad.shape[0]
        p = quad[..., f + h : 2 * f].reshape(n, 2, r, h)
        parts = [quad[..., i * h : (i + 1) * h] for i in range(3)] + [p[:, 0], p[:, 1]]
        parts = [self.cut(t.reshape(-1, h)) for t in parts]
        if self.links.fast:
            parts.insert(2, between)
        if quad.shape[2] > 2 * f:
            small = self.cut(quad[..., 2 * f :].reshape(-1, 128))
            small = small.reshape(small.shape[:-2] + (3, -1, 128))
            parts.append(jnp.concatenate([small[..., g, :, :] for g in range(3)], -1))
        return jnp.concatenate(parts, -2)

    def pack_pair(self, quad_in, quad_out):
        f = self.feat
        halves = []
        for i in range(2):
            pair = [self.cut(t[..., i * f : (i + 1) * f].reshape(-1, f)) for t in (quad_in, quad_out)]
            halves.append(jnp.stack(pair, -3))
        return jnp.stack(halves, -4)

    def spread(self, x, cuts, *hold):
        if not self.links.fast:
            return [x[0], x[1], x[2], cuts[0](x[3]), cuts[1](x[3])]
        to = lambda t, j: self.links.xor(t, "expert", j)
        x1, x2 = tie([to(x, 1), to(x, 2)], *hold)
        return [x, x1, x2, to(cuts[0](x1), 2), to(cuts[1](x2), 1)]

    def spread_attend(self, x, skip, *hold):
        n = self.feat // 2 + skip
        return self.spread(x, (lambda t: t[:n], lambda t: t[n:]), *hold)

    def spread_pair(self, x, *hold):
        return self.spread(x, (lambda t: t[0], lambda t: t[1]), *hold)

    def total(self, keep, send, first, hold):
        if self.links.fast:
            out, _ = self.links.plane_sum(keep, send, first, hold)
            return out
        blk = {0: keep[0], 3 - first: keep[1], first: send[0], 3: send[1]}
        return jnp.stack([blk[j] for j in range(4)])

    def all_sum(self, buf):
        return lax.psum_scatter(buf.astype(BF), CHIPS, scatter_dimension=0, tiled=False).astype(F32)

    def exchange(self, w):
        w = w.reshape(2, self.rdev, -1)
        mine = lax.dynamic_index_in_dim(w, self.d, 0, False)
        got = self.links.sib(lax.dynamic_index_in_dim(w, 1 - self.d, 0, False))
        return in_order(self.d, mine, got)

    def to_columns(self, t):
        n, m = self.feat // 4, self.half // 4
        r = self.rdev
        cut = lambda t, k: t.reshape(-1, k * r, t.shape[-1])
        parts = [cut(t[..., g * n : (g + 1) * n, :], 2) for g in range(3)]
        p = [cut(t[..., 3 * n + g * m : 3 * n + (g + 1) * m, :], 1) for g in range(2)]
        parts.append(jnp.concatenate(p, 1))
        if t.shape[-2] > 3 * n + 2 * m:
            sm = t[..., 3 * n + 2 * m :, :]
            sm = jnp.stack([sm[..., 128 * g : 128 * (g + 1)] for g in range(3)], -3)
            parts.append(sm.reshape(-1, 2 * r, 128))
        return jnp.concatenate(parts, 2)

    def owners(self, col1, col3, w2):
        f, h, r = self.feat, self.half, self.rdev
        w = f + h
        p = [jnp.concatenate([c[:r, w : 2 * f], c[r:, w : 2 * f]], 1) for c in (col1, col3)]
        p = lax.ppermute(jnp.concatenate(p, 0), ALL, self.links.from_lane)
        t = self.exchange(jnp.concatenate([col1[:, :w], col3[:, :w], col3[:, 2 * f :], w2], 1))

        def attend(t):
            return t.reshape(2, r, 3, h).transpose(1, 2, 0, 3).reshape(r, 3 * f)

        small = t[..., 2 * w : 2 * w + 128]
        win = t[..., 2 * w + 128 :].reshape(2, r, 2, self.links.chips, -1)
        win = win.transpose(1, 3, 0, 2, 4).reshape(r, self.ff)
        return attend(t[..., :w]), p[:r], attend(t[..., w : 2 * w]), p[r:], small[0] + small[1], win


def body(links, *args):
    (tokens, cotangent, g1, w1, p1, g2, win, wout, g3, w3, p3, g4, router, ein, eout, routes, slots) = args
    e = lax.axis_index("expert")
    d = lax.axis_index("dp")
    blk_len, feat = tokens.shape[1:]
    rows = up16(blk_len)
    half = feat // 2
    rdev = w1.shape[0]
    ff = win.shape[1]
    longest = LEN - (blk_len - 1) * links.C
    experts = router.shape[1]
    assert experts <= 128
    small_rows = (4 + experts + 7) // 8 * 8
    cap = max(2, (5 * TOP * blk_len + 4 * experts - 1) // (4 * experts))
    blk = 2 * (e % 2) + d
    where = jnp.stack([blk, e if links.fast else 0 * e, lax.axis_index("context")]).astype(jnp.int32)
    wt = Weights(links, rdev, feat, ff)
    img = dict(rows=rows, blk_len=blk_len, longest=longest)

    tok = links.move(tokens[0])
    ps = lax.ppermute(jnp.concatenate([p1, p3], 0), ALL, links.to_lane)
    small = jnp.concatenate([g1[:, None], g2[:, None], g3[:, None], g4[:, None], router], 1)
    gsm = small.shape[1]
    lane1 = jnp.concatenate(
        [wt.split_attend(w1), jnp.broadcast_to(small[None], (2, rdev, gsm))], 2
    )
    lane1 = lane_rows(links, lane1, d)
    buf1 = wt.pack_attend(lane1[:, : 3 * half], ps[:rdev], lane1[:, 3 * half :])
    quad1 = wt.column(buf1)
    later = jnp.concatenate([wt.split_widen(win), wt.split_attend(w3)], 2)
    later = lane_rows(links, later, d)
    w_in, w_out = later[:, : ff // 2], wt.pack_wide(wout)
    w3_lane, p3_lane = later[:, ff // 2 :], ps[rdev:]
    block3 = jnp.concatenate(
        [w3_lane[:, g * half : (g + 1) * half] for g in range(3)] + [p3_lane[:, :half], p3_lane[:, half:]], 0
    )
    skip = block3.shape[0] if links.fast else 0
    tok_pair = jnp.stack([tok, links.partner(tok)])
    block1 = wt.pack_block(tie([quad1], tok_pair)[0], block3)
    if links.fast:
        (buf2,) = tie([jnp.concatenate([w_in, w_out], 1)], quad1)
        quad2 = wt.column(buf2)
        blocks1 = wt.spread_attend(block1, skip, quad2)
        (tok_pair,) = tie([tok_pair], *blocks1[1:3])
    else:
        quad2 = None
        blocks1 = wt.spread_attend(block1, skip)
    tok_sib = links.sib(tok_pair)
    toks = [tok_pair[0], tok_sib[0], tok_pair[1], tok_sib[1]]
    raw = jnp.concatenate([routes[0], slots[0]], 1).astype(BF)
    cot = jnp.concatenate([cotangent[0].astype(BF), jnp.pad(raw, ((0, 0), (0, 128 - 2 * TOP)))], 1)
    cot = links.move(tie([cot], *blocks1[1:3])[0])
    if links.fast:
        (quad2,) = tie([quad2], *blocks1[3:], *toks, cot)
        pair2 = wt.pack_pair(quad2[..., : ff // 2], quad2[..., ff // 2 :])
        q, n = feat // 2, block3.shape[0]
        place3 = jnp.stack([t[q : q + n] for t in blocks1[:4]])
        source3 = lax.all_gather(place3, "context", axis=0, tiled=False)
        p3 = source3[:, :, 6 * rdev :].reshape(4, 4, 2, rdev, half)
        p3 = jnp.stack([lax.dynamic_index_in_dim(p3, e ^ k, 1, False) for k in range(4)])
        wp3 = p3.transpose(0, 1, 3, 2, 4).reshape(half, feat)
    else:
        pair2 = wt.pack_pair(wt.column(w_in), wt.column(w_out))
        all3 = lax.all_gather(block3, CHIPS, axis=0, tiled=False)
        source3 = all3[:, : 6 * rdev].reshape(links.chips, 3, 2 * rdev, half)
        source3 = source3.transpose(0, 2, 1, 3).reshape(feat, 3 * half)
        wp3 = all3[:, 6 * rdev :].reshape(links.chips, 2, rdev, half)
        wp3 = wp3.transpose(0, 2, 1, 3).reshape(half, feat)

    x0, normed1, q1, kv1, far1, wa1, wp1, small, gains = attend_first(
        where, toks, small_rows, blocks1, rows, skip
    )
    part, low, blend1, lse1 = attend_core(
        where, q1, kv1, far1, wp1, solo=False, **img
    )
    blocks2 = wt.spread_pair(pair2, part)
    x1, normed2, hidden, part2, low2 = widen_forward(
        where, x0, part, links.sib(low), gains, blocks2, rows
    )
    x2, normed3, own3 = norm_next(x1, part2, links.sib(low2), gains, 2, rows)
    ein_own, eout_own = ein[0], eout[0]
    ein_sib, eout_sib = [links.sib(t) for t in tie([ein_own, eout_own], own3)]
    far_own = links.partner(own3)
    q3, kv3, wa3 = attend_next(where, normed3, source3)
    (far_own,) = tie([far_own], q3)
    part3, low3, blend3, lse3, far3 = attend_core(
        where, q3, kv3, None, wp3, solo=True, far=(far_own, links.sib(far_own), wa3), **img
    )
    moe_args = dict(experts=experts, cap=cap, fast=links.fast, **img)
    index = cot[:, feat : feat + 2 * TOP].astype(jnp.int32)
    index = jnp.pad(index, ((0, rows - blk_len), (0, 0)), constant_values=cap)
    x3, moe, gates, up, *sent = route(
        where, x2, part3, links.sib(low3), gains, small, cot[:, :feat], index,
        after=(ein_sib, eout_sib), **moe_args
    )
    came = links.swap_blocks(sent)
    every = lax.all_gather(jnp.stack(came), "context", axis=0, tiled=False)
    answer = experts_forward(came, (ein_own, eout_own), (ein_sib, eout_sib), up16(cap))
    answer = links.swap_blocks(answer)
    acts, u, u_low, small_slopes = combine(
        where, answer, x3, moe, gates, up, index, small, gains, small_rows, **moe_args
    )

    u, u_low = join_upstream(u, links.sib(u_low), rows)
    dq, own, far, wps = attend_core_back(where, u_low, wp3, blend3, q3, kv3, far3, lse3, **img)
    first3, first2, first1 = (1,), 2, (1, 2)
    part, low, *slopes3 = attend_proj_back(
        where, dq, own, links.partner(far), normed3, wa3, wps, small_slopes, first3, rows, False
    )
    u, part, low, *slopes2 = widen_back(
        where, u, x2, gains, part, links.sib(low), normed2, hidden, blocks2, first2, rows, False
    )
    u1, u_low = norm_step(u, x1, gains, 1, part, links.sib(low), rows, 0)
    dq1, own, far, wps = attend_core_back(where, u_low, wp1, blend1, q1, kv1, far1, lse1, **img)
    part, low, *slopes1 = attend_proj_back(
        where, dq1, own, links.partner(far), normed1, wa1, wps, None, first1, rows, True, after=(every,)
    )
    (u2,) = norm_step(u1, x0, gains, 0, part, links.sib(low), rows, blk_len)
    moved = links.move(jnp.stack([acts, u2]))
    acts, token_slope = moved[0], moved[1]
    e_sib = expert_slopes(every, ein_sib, eout_sib, None, after=(u2,))
    sum3 = wt.total(*slopes3, first3[0], ((low,), (e_sib[0],)))
    sum2a = wt.total(*slopes2[:2], first2, ((low,), (e_sib[0],)))
    sum2b = wt.total(*slopes2[2:], first2, ((e_sib[0],), ()))
    sum1 = [wt.total(*slopes1[2 * i : 2 * i + 2], first1[i], ((e_sib[0],), ())) for i in range(2)]
    if links.fast:
        early = columns_of([sum3, sum2a])
        early = lax.psum_scatter(tie([early], every)[0], "context", scatter_dimension=0, tiled=False)
        own, *away = last_columns(where, *sum1, sum2b, after=(moved,))
        e_slopes = expert_slopes(every, ein_own, eout_own, [links.sib(t) for t in e_sib], after=(own,))
        for t in tie([links.xor(t, "context", j + 1) for j, t in enumerate(away)], e_slopes[0]):
            own = own + t.astype(F32)
        early = tie([early], e_slopes[0])[0].astype(F32)
        col1, col2b = own[:, : 2 * feat], own[:, 2 * feat :]
        col3, col2a = early[:, : early.shape[1] - 2 * feat], early[:, early.shape[1] - 2 * feat :]
        w2 = jnp.concatenate([col2a[:, :feat], col2b[:, :feat]], 1)
        wout_out = jnp.concatenate([col2a[:, feat:], col2b[:, feat:]], 0)
    else:
        e_slopes = expert_slopes(every, ein_own, eout_own, [links.sib(t) for t in e_sib])
        col3, col1 = wt.to_columns(sum3), wt.to_columns(jnp.concatenate(sum1, -2))
        col3, col1 = wt.all_sum(col3), wt.all_sum(col1)
        hid = ff // (4 * links.chips)
        w2 = [t[..., 0, :, :].reshape(-1, 2 * rdev, feat) for t in (sum2a, sum2b)]
        w2_out = [t[..., 1, :, :].reshape(-1, hid, feat) for t in (sum2a, sum2b)]
        w2, w2_out = [wt.all_sum(jnp.concatenate(t, 2)) for t in (w2, w2_out)]
        wout_out = jnp.concatenate([w2_out[:, :feat], w2_out[:, feat:]], 0)
    w1_out, p1_out, w3_out, p3_out, extra, win_out = wt.owners(col1, col3, w2)

    def gain_slope(w, slope, gain):
        return jnp.sum(w.astype(F32) * slope, 1) / gain.astype(F32)

    return (
        acts.astype(F32)[None], token_slope.astype(F32)[None],
        gain_slope(w1, w1_out, g1), w1_out, p1_out, gain_slope(win, win_out, g2), win_out, wout_out,
        gain_slope(w3, w3_out, g3), w3_out, p3_out, extra[:, 3], extra[:, 4 : 4 + experts],
        e_slopes[0][None], e_slopes[1][None],
    )


def solution(mesh):
    links = Links(mesh)
    tok = P(("expert", "dp"), "context", None)
    vec, mat = P(ALL), P(ALL, None)
    ein, eout = P("expert", None, "dp"), P("expert", "dp", None)
    dense = (vec, mat, mat, vec, mat, mat, vec, mat, mat, vec, mat, ein, eout)
    return jax.shard_map(
        functools.partial(body, links),
        mesh=mesh,
        in_specs=(tok, tok) + dense + (tok, tok),
        out_specs=(tok, tok) + dense,
        check_vma=False,
    )
```

```python
import functools

import jax
import jax.numpy as jnp
from jax import lax
from jax.experimental import pallas as pl
from jax.experimental.pallas import tpu as pltpu
from jax.sharding import PartitionSpec as P

HEADS = 12
HEAD_DIM = 64
LEN = 577
TOP = 2
ALL = ("expert", "context", "dp")
CHIPS = ("expert", "context")
BF = jnp.bfloat16
F32 = jnp.float32
VM = pl.BlockSpec(memory_space=pltpu.VMEM)
HB = pl.BlockSpec(memory_space=pl.ANY)
SM = pl.BlockSpec(memory_space=pltpu.SMEM)


def up16(n):
    return (n + 15) // 16 * 16


def dot(a, b):
    return jnp.dot(a, b, preferred_element_type=F32)


def dot_t(a, b):
    return lax.dot_general(a, b, (((1,), (1,)), ((), ())), preferred_element_type=F32)


def t_dot(a, b):
    return lax.dot_general(a, b, (((0,), (0,)), ((), ())), preferred_element_type=F32)


def call(kernel, outs, ins, scratch=(), after=(), flops=0, bytes_accessed=0, grid=()):
    n_in, n_after = len(ins), len(after)

    def run(*refs):
        kernel(*refs[:n_in], *refs[n_in + n_after :])

    return pl.pallas_call(
        run,
        grid=grid,
        out_shape=[jax.ShapeDtypeStruct(s, t) for s, t, _ in outs],
        in_specs=[s for _, s in ins] + [HB] * n_after,
        out_specs=[s for _, _, s in outs],
        scratch_shapes=list(scratch),
        compiler_params=pltpu.CompilerParams(vmem_limit_bytes=50 * 2**20),
        cost_estimate=pl.CostEstimate(
            flops=flops, bytes_accessed=bytes_accessed, transcendentals=0
        ),
    )(*[a for a, _ in ins], *after)


def norm_parts(x):
    mean = jnp.mean(x, -1, keepdims=True)
    centre = x - mean
    scale = lax.rsqrt(jnp.mean(centre * centre, -1, keepdims=True) + 1e-06)
    return centre * scale, scale


def layer_norm(x, gain):
    return (norm_parts(x)[0] * gain).astype(BF)


def norm_back(x, gain, slope):
    unit, scale = norm_parts(x)
    terms = slope * unit
    inner = slope * gain
    inner = inner - jnp.mean(inner, -1, keepdims=True) - unit * jnp.mean(inner * unit, -1, keepdims=True)
    return inner * scale, terms


def gelu_both(h):
    k = 0.7978845608028654
    t = jnp.tanh(k * (h + 0.044715 * h * h * h))
    half = 0.5 * (1 + t)
    return h * half, half + 0.5 * h * (1 - t * t) * (k + (3 * 0.044715 * k) * h * h)


def add_both(mine, got, rows):
    return mine + jnp.concatenate([got[rows:], got[:rows]], 0).astype(F32)


def pair_masks():
    lane = lax.broadcasted_iota(jnp.int32, (1, 2 * HEAD_DIM), 1)
    return [(lane < HEAD_DIM).astype(BF), (lane >= HEAD_DIM).astype(BF)]


def key_mask(blk, rows, blk_len, longest):
    pos = lax.broadcasted_iota(jnp.int32, (rows, 1), 0)
    parts = []
    for j in range(4):
        last = jnp.where((blk ^ j) < longest, blk_len, blk_len - 1)
        parts.append(pos < last)
    return jnp.concatenate([jnp.where(p, 1.0, 0.0) for p in parts], 0) > 0.5


def attend_core(where, q, kv_own, kv_far, wp, rows, blk_len, longest, solo, far=None, after=()):
    half = q.shape[1]
    feat = wp.shape[1]
    pairs = half // (2 * HEAD_DIM)
    r2 = 2 * rows

    def kernel(where_ref, q_ref, ko_ref, *refs):
        refs = list(refs)
        take = lambda n: [refs.pop(0) for _ in range(n)]
        given = take(1 if far is None else 3)
        wp_ref, part_ref, low_ref, blend_ref, lse_ref = take(5)
        if far is None:
            kf_ref = given[0]
        else:
            (kf_ref,) = take(1)
            for j in range(2):
                kf_ref[pl.ds(j * rows, rows), :] = dot(given[j][...], given[2][:, half:]).astype(BF)
        ok = key_mask(where_ref[0], rows, blk_len, longest)
        masks = pair_masks()
        for p in range(pairs):
            at, vat = pl.ds(p * 128, 128), pl.ds(half + p * 128, 128)
            k = jnp.concatenate([ko_ref[:, at], kf_ref[:, at]], 0)
            v = jnp.concatenate([ko_ref[:, vat], kf_ref[:, vat]], 0)
            qp = q_ref[:, at]
            acc = None
            for h in range(2):
                s = dot_t(k, qp * masks[h]) * 0.125
                s = jnp.where(ok, s, -1e9)
                top = jnp.max(s, 0, keepdims=True)
                ex = jnp.exp(s - top)
                total = jnp.sum(ex, 0, keepdims=True)
                lse_ref[pl.ds(2 * p + h, 1), :] = top + jnp.log(total)
                shares = (ex * (1.0 / total)).astype(BF)
                out = t_dot(v * masks[h], shares)
                acc = out if acc is None else acc + out
            blend_ref[at, :] = acc.astype(BF)
        part = t_dot(blend_ref[...], wp_ref[...])
        part_ref[...] = part
        low_ref[...] = (part[rows:] if solo else part).astype(BF)

    outs = [
        ((r2, feat), F32, VM), ((rows if solo else r2, feat), BF, VM), ((half, r2), BF, VM), ((8, r2), F32, VM),
    ]
    ins = [(where, SM), (q, VM), (kv_own, VM)]
    if far is None:
        ins.append((kv_far, VM))
    else:
        ins += [(t, VM) for t in far]
        outs.append(((r2, feat), BF, VM))
    return call(
        kernel,
        outs,
        ins + [(wp, VM)],
        after=after,
        flops=2 * r2 * half * (8 * rows + feat),
        bytes_accessed=4 * 2**20,
    )


def attend_core_back(where, u_low, wp, blend, q, kv_own, kv_far, lse, rows, blk_len, longest, after=()):
    half = q.shape[1]
    feat = wp.shape[1]
    pairs = half // (2 * HEAD_DIM)
    r2 = 2 * rows

    def kernel(
        where_ref, u_ref, wp_ref, blend_ref, q_ref, ko_ref, kf_ref, lse_ref,
        dq_ref, own_ref, far_ref, wps_ref, bt_ref, dqt_ref,
    ):
        ok = key_mask(where_ref[0], rows, blk_len, longest)
        masks = pair_masks()
        sub = lax.broadcasted_iota(jnp.int32, (2 * HEAD_DIM, 1), 0)
        row_masks = [(sub < HEAD_DIM).astype(BF), (sub >= HEAD_DIM).astype(BF)]
        u = u_ref[...]
        bt_ref[...] = dot_t(wp_ref[...], u).astype(BF)
        for p in range(pairs):
            at, vat = pl.ds(p * 128, 128), pl.ds(half + p * 128, 128)
            k = jnp.concatenate([ko_ref[:, at], kf_ref[:, at]], 0)
            v = jnp.concatenate([ko_ref[:, vat], kf_ref[:, vat]], 0)
            qp = q_ref[:, at]
            bt = bt_ref[at, :]
            dqt = dk = dv = 0.0
            for h in range(2):
                qm = qp * masks[h]
                s = dot_t(k, qm) * 0.125
                shares = jnp.where(ok, jnp.exp(s - lse_ref[pl.ds(2 * p + h, 1), :]), 0.0)
                slope = dot(v * masks[h], bt)
                t = shares * slope
                ss = (t - shares * jnp.sum(t, 0, keepdims=True)).astype(BF)
                dqt += t_dot(k * masks[h], ss)
                dk += dot(ss, qm)
                dv += dot_t(shares.astype(BF), bt * row_masks[h])
            dqt_ref[at, :] = dqt * 0.125
            dk = dk * 0.125
            own_ref[:, at] = dk[:r2]
            own_ref[:, vat] = dv[:r2]
            far_ref[:, at] = dk[r2:].astype(BF)
            far_ref[:, vat] = dv[r2:].astype(BF)
        dq_ref[...] = dqt_ref[...].T.astype(BF)
        wps_ref[...] = dot(blend_ref[...], u).astype(BF)

    return call(
        kernel,
        [
            ((r2, half), BF, VM), ((r2, 2 * half), F32, VM), ((r2, 2 * half), BF, VM),
            ((half, feat), BF, VM),
        ],
        [
            (where, SM), (u_low, VM), (wp, VM), (blend, VM), (q, VM), (kv_own, VM), (kv_far, VM),
            (lse, VM),
        ],
        scratch=[pltpu.VMEM((half, r2), BF), pltpu.VMEM((half, r2), F32)],
        after=after,
        flops=2 * r2 * half * (20 * rows + 2 * feat),
        bytes_accessed=6 * 2**20,
    )


def start_all(copies):
    for c in copies:
        c.start()


def wait_all(copies):
    for c in copies:
        c.wait()


def attend_copies(e, refs, w_ref, p_ref, small_ref, sems, skip):
    copies = []

    def add(src, dst):
        copies.append(pltpu.make_async_copy(src, dst, sems.at[len(copies)]))

    n = w_ref.shape[0] // 4
    half = p_ref.shape[0]
    m = half // 4
    for j in range(4):
        to = e ^ j
        rows, prows = pl.ds(pl.multiple_of(to * n, 16), n), pl.ds(pl.multiple_of(to * m, 16), m)
        a, b, at = (refs[j], refs[j], 2 * n + skip) if j < 3 else (refs[3], refs[4], 0)
        for g in range(2):
            add(a.at[pl.ds(g * n, n)], w_ref.at[rows, pl.ds(g * half, half)])
        add(b.at[pl.ds(at, n)], w_ref.at[rows, pl.ds(2 * half, half)])
        add(b.at[pl.ds(at + n, m)], p_ref.at[prows, pl.ds(0, half)])
        add(b.at[pl.ds(at + n + m, m)], p_ref.at[prows, pl.ds(half, half)])
        if small_ref is not None:
            for g in range(3):
                srows = pl.ds(pl.multiple_of(to * n + g * (n // 3), 16), n // 3)
                add(b.at[pl.ds(at + n + 2 * m, n // 3), pl.ds(128 * g, 128)], small_ref.at[srows])
    return copies


def attend_first(where, tokens, small_rows, blocks, rows, skip, after=()):
    blk_len, feat = tokens[0].shape
    half = feat // 2
    r2 = 2 * rows

    def kernel(where_ref, *refs):
        refs = list(refs)
        take = lambda n: [refs.pop(0) for _ in range(n)]
        tok, block_refs = take(4), take(5)
        x_ref, normed_ref, q_ref, kv_ref, far_ref, w_ref, p_ref, small_ref, rows_ref, all_ref, sems = take(11)
        copies = attend_copies(where_ref[1], block_refs, w_ref, p_ref, small_ref, sems, skip)
        start_all(copies)
        all_ref[...] = jnp.zeros_like(all_ref)
        for j in range(4):
            all_ref[pl.ds(j * rows, blk_len), :] = tok[j][...].astype(F32)
        x = all_ref[...]
        x_ref[...] = x[:r2]
        unit = norm_parts(x)[0]
        wait_all(copies)
        turned = small_ref[...].astype(F32).T
        rows_ref[...] = turned[: rows_ref.shape[0]]
        normed = (unit * turned[0:1]).astype(BF)
        normed_ref[...] = normed[:r2]
        q_ref[...] = dot(normed[:r2], w_ref[:, :half]).astype(BF)
        kv = dot(normed, w_ref[:, half:]).astype(BF)
        kv_ref[...] = kv[:r2]
        far_ref[...] = kv[r2:]

    return call(
        kernel,
        [
            ((r2, feat), F32, VM), ((r2, feat), BF, VM), ((r2, half), BF, VM), ((r2, feat), BF, VM),
            ((r2, feat), BF, VM), ((feat, 3 * half), BF, VM), ((half, feat), BF, VM),
            ((feat, 128), BF, VM), ((small_rows, feat), F32, VM),
        ],
        [(where, SM)] + [(t, VM) for t in tokens] + [(t, HB) for t in blocks],
        scratch=[pltpu.VMEM((2 * r2, feat), F32), pltpu.SemaphoreType.DMA((32,))],
        after=after,
        flops=2 * r2 * feat * 5 * half,
        bytes_accessed=6 * 2**20,
    )


def norm_next(x, part, got, gains, gain_row, rows, after=()):
    r2, feat = x.shape

    def kernel(x_ref, part_ref, got_ref, gains_ref, x2_ref, normed_ref, own_ref):
        x2 = add_both(x_ref[...] + part_ref[...], got_ref[...], rows)
        x2_ref[...] = x2
        normed = layer_norm(x2, gains_ref[pl.ds(gain_row, 1), :])
        normed_ref[...] = normed
        own_ref[...] = normed[:rows]

    return call(
        kernel,
        [((r2, feat), F32, VM), ((r2, feat), BF, VM), ((rows, feat), BF, VM)],
        [(x, VM), (part, VM), (got, VM), (gains, VM)],
        after=after,
        bytes_accessed=5 * 2**20,
    )


def attend_next(where, normed, source, after=()):
    r2, feat = normed.shape
    half = feat // 2
    packed = source.ndim == 4

    def kernel(where_ref, normed_ref, source_ref, q_ref, kv_ref, *more):
        if packed:
            w_ref, sems = more
            r = source_ref.shape[2] // 4
            copies = []
            for c in range(4):
                for j in range(4):
                    at = pl.multiple_of((where_ref[1] ^ j) * (feat // 4) + c * r, 16)
                    for g in range(3):
                        copies.append(pltpu.make_async_copy(
                            source_ref.at[c, j, pl.ds(g * r, r)],
                            w_ref.at[pl.ds(at, r), pl.ds(g * half, half)], sems.at[len(copies)],
                        ))
            start_all(copies)
            wait_all(copies)
        else:
            w_ref = source_ref
        normed = normed_ref[...]
        q_ref[...] = dot(normed, w_ref[:, :half]).astype(BF)
        kv_ref[...] = dot(normed, w_ref[:, half:]).astype(BF)

    out = call(
        kernel,
        [((r2, half), BF, VM), ((r2, feat), BF, VM)] + ([((feat, 3 * half), BF, VM)] if packed else []),
        [(where, SM), (normed, VM), (source, HB if packed else VM)],
        scratch=[pltpu.SemaphoreType.DMA((48,))] if packed else [],
        after=after,
        flops=2 * r2 * feat * 3 * half,
        bytes_accessed=4 * 2**20,
    )
    return out if packed else [*out, source]


def widen_copies(e, blocks, wi_ref, wo_ref, sems):
    copies = []
    feat = wo_ref.shape[1]
    n = feat // 4
    for h in range(2):
        for j in range(4):
            src = blocks[j].at[h] if j < 3 else blocks[3 + h]
            at = (e ^ j) * n
            for part, dst in (
                (0, wi_ref.at[pl.ds(pl.multiple_of(at, 16), n), pl.ds(h * feat, feat)]),
                (1, wo_ref.at[pl.ds(pl.multiple_of(at + h * feat, 16), n)]),
            ):
                copies.append(pltpu.make_async_copy(src.at[part], dst, sems.at[len(copies)]))
    return copies


def widen_forward(where, x, part, got, gains, blocks, rows, after=()):
    r2, feat = x.shape
    wide = 2 * feat
    tile = 384

    def kernel(
        where_ref, x_ref, part_ref, got_ref, gains_ref, z0, z1, z2, a3, b3,
        x1_ref, normed_ref, hidden_ref, out_ref, low_ref, wi_ref, wo_ref, sems,
    ):
        copies = widen_copies(where_ref[1], (z0, z1, z2, a3, b3), wi_ref, wo_ref, sems)
        start_all(copies)
        x1 = add_both(x_ref[...] + part_ref[...], got_ref[...], rows)
        x1_ref[...] = x1
        normed_ref[...] = layer_norm(x1, gains_ref[pl.ds(1, 1), :])
        out_ref[...] = jnp.zeros_like(out_ref)
        for half in range(2):
            wait_all(copies[8 * half : 8 * half + 8])

            @pl.loop(half * (feat // tile), (half + 1) * (feat // tile))
            def _(t):
                at = pl.ds(pl.multiple_of(t * tile, 128), tile)
                h = dot(normed_ref[...], wi_ref[:, at])
                hidden_ref[:, at] = h.astype(BF)
                out_ref[...] += dot(gelu_both(h)[0].astype(BF), wo_ref[at, :])

        low_ref[...] = out_ref[...].astype(BF)

    return call(
        kernel,
        [
            ((r2, feat), F32, VM), ((r2, feat), BF, VM), ((r2, wide), BF, VM), ((r2, feat), F32, VM),
            ((r2, feat), BF, VM),
        ],
        [(where, SM), (x, VM), (part, VM), (got, VM), (gains, VM)] + [(t, HB) for t in blocks],
        scratch=[
            pltpu.VMEM((feat, wide), BF), pltpu.VMEM((wide, feat), BF), pltpu.SemaphoreType.DMA((16,)),
        ],
        after=after,
        flops=4 * r2 * feat * wide,
        bytes_accessed=16 * 2**20,
    )


def widen_back(where, u, x, gains, part, got, normed, hidden, blocks, first, rows, columns, after=()):
    r2, feat = u.shape
    wide = 2 * feat
    tile = 384
    n = feat // 4

    def kernel(
        where_ref, u_ref, x_ref, gains_ref, part_ref, got_ref, normed_ref, hidden_ref,
        z0, z1, z2, a3, b3, u2_ref, out_ref, low_ref, *more,
    ):
        outs, (ulow_ref, turned_ref, wis_ref, wos_ref, wi_ref, wo_ref, in_sems, sems) = more[:-8], more[-8:]
        arriving = widen_copies(where_ref[1], (z0, z1, z2, a3, b3), wi_ref, wo_ref, in_sems)
        start_all(arriving)
        slope = add_both(part_ref[...], got_ref[...], rows)
        u2 = u_ref[...] + norm_back(x_ref[...], gains_ref[pl.ds(2, 1), :], slope)[0]
        u2_ref[...] = u2
        ulow_ref[...] = u2.astype(BF)
        turned_ref[...] = normed_ref[...].T
        out_ref[...] = jnp.zeros_like(out_ref)

        copies = []
        slots = (0, 3 - first, first, 3)

        def add(h, at, size, dst):
            wide_at = pl.ds(pl.multiple_of(at, 16), size)
            deep_at = pl.ds(pl.multiple_of(at + h * feat, 16), size)
            for i, src in enumerate((wis_ref.at[wide_at, pl.ds(h * feat, feat)], wos_ref.at[deep_at])):
                copies.append(pltpu.make_async_copy(src, dst.at[i], sems.at[len(copies)]))
                copies[-1].start()

        for h in range(2):
            wait_all(arriving[8 * h : 8 * h + 8])

            @pl.loop(h * (feat // tile), (h + 1) * (feat // tile))
            def _(t):
                at = pl.ds(pl.multiple_of(t * tile, 128), tile)
                ulow = ulow_ref[...]
                act, dact = gelu_both(hidden_ref[:, at].astype(F32))
                hs = (dact * dot_t(ulow, wo_ref[at, :])).astype(BF)
                wos_ref[at, :] = t_dot(act.astype(BF), ulow).astype(BF)
                wis_ref[:, at] = dot(turned_ref[...], hs).astype(BF)
                out_ref[...] += dot_t(hs, wi_ref[:, at])

            for i, j in enumerate(slots):
                to = (where_ref[1] ^ j) * n
                if h == 1 and columns:
                    for c in range(4):
                        add(1, to + c * (n // 4), n // 4, outs[2].at[c, i])
                else:
                    add(h, to, n, outs[2 * h + i // 2].at[i % 2])

        low_ref[...] = out_ref[...].astype(BF)
        wait_all(copies)

    block = ((2, 2, n, feat), BF, HB)
    more = [((4, 4, 2, n // 4, feat), BF, HB)] if columns else [block] * 2
    return call(
        kernel,
        [((r2, feat), F32, VM), ((r2, feat), F32, VM), ((r2, feat), BF, VM)] + [block] * 2 + more,
        [
            (where, SM), (u, VM), (x, VM), (gains, VM), (part, VM), (got, VM), (normed, VM),
            (hidden, VM),
        ]
        + [(t, HB) for t in blocks],
        scratch=[
            pltpu.VMEM((r2, feat), BF), pltpu.VMEM((feat, r2), BF), pltpu.VMEM((feat, wide), BF),
            pltpu.VMEM((wide, feat), BF), pltpu.VMEM((feat, wide), BF), pltpu.VMEM((wide, feat), BF),
            pltpu.SemaphoreType.DMA((16,)), pltpu.SemaphoreType.DMA((40,)),
        ],
        after=after,
        flops=10 * r2 * feat * wide,
        bytes_accessed=24 * 2**20,
    )


def attend_proj_back(where, dq, own, got, normed, w, wps, small, firsts, rows, last, after=()):
    r2, feat = normed.shape
    half = feat // 2
    n, m = feat // 4, half // 4
    tile = 384
    extra = 0 if small is None else n // 3

    def kernel(where_ref, dq_ref, own_ref, got_ref, normed_ref, w_ref, wps_ref, *refs):
        refs = list(refs)
        take = lambda k: [refs.pop(0) for _ in range(k)]
        small_ref = take(1)[0] if extra else None
        out_ref, low_ref = take(2)
        sides = [take(2) for _ in firsts]
        packed_ref, turned_ref, ws_ref, sm_ref, sems = take(5)
        packed_ref[:, :half] = dq_ref[...]
        packed_ref[:, half:] = (own_ref[...] + got_ref[...].astype(F32)).astype(BF)
        turned_ref[...] = normed_ref[...].T

        @pl.loop(0, 3 * half // tile)
        def _(t):
            at = pl.ds(pl.multiple_of(t * tile, 128), tile)
            ws_ref[:, at] = dot(turned_ref[...], packed_ref[:, at]).astype(BF)

        if extra:
            wide = jnp.concatenate(
                [small_ref[...], jnp.zeros((128 - small_ref.shape[0], feat), F32)], 0
            )
            sm_ref[...] = wide.T.astype(BF)
        copies = []

        def add(src, dst):
            copies.append(pltpu.make_async_copy(src, dst, sems.at[len(copies)]))

        for lane, first in enumerate(firsts):
            one = len(firsts) == 1
            skip = 2 * n if lane == 1 else 0
            for ref, js in zip(sides[lane], ((0, 3 - first), (first, 3))):
                for i, j in enumerate(js):
                    to = where_ref[1] ^ j
                    at, pat = pl.ds(pl.multiple_of(to * n, 16), n), pl.ds(pl.multiple_of(to * m, 16), m)
                    for g in range(3):
                        if one or (g == 2) == (lane == 1):
                            add(ws_ref.at[at, pl.ds(g * half, half)], ref.at[i, pl.ds(g * n - skip, n)])
                    for g in range(2):
                        if one or lane == 1:
                            add(
                                wps_ref.at[pat, pl.ds(g * half, half)],
                                ref.at[i, pl.ds(3 * n + g * m - skip, m)],
                            )
                    if extra:
                        for g in range(3):
                            sat = pl.ds(pl.multiple_of(to * n + g * extra, 16), extra)
                            add(sm_ref.at[sat], ref.at[i, pl.ds(3 * n + 2 * m, extra), pl.ds(128 * g, 128)])
        start_all(copies)
        out = dot_t(packed_ref[...], w_ref[...])
        out_ref[...] = out[: out_ref.shape[0]]
        low_ref[...] = (out[rows:] if last else out).astype(BF)
        wait_all(copies)

    n_out = rows if last else r2
    deep = 3 * n + 2 * m + extra
    deeps = [deep] * 2 if len(firsts) == 1 else [2 * n] * 2 + [n + 2 * m] * 2
    return call(
        kernel,
        [((n_out, feat), F32, VM), ((n_out, feat), BF, VM)] + [((2, k, half), BF, HB) for k in deeps],
        [(where, SM), (dq, VM), (own, VM), (got, VM), (normed, VM), (w, VM), (wps, VM)]
        + ([(small, VM)] if extra else []),
        scratch=[
            pltpu.VMEM((r2, 3 * half), BF), pltpu.VMEM((feat, r2), BF), pltpu.VMEM((feat, 3 * half), BF),
            pltpu.VMEM((feat, 128), BF), pltpu.SemaphoreType.DMA((32,)),
        ],
        after=after,
        flops=4 * r2 * feat * 3 * half,
        bytes_accessed=10 * 2**20,
    )


def spread_attend_rows(t, store):
    half = t.shape[1]
    n, m = half // 2, half // 4
    r = n // 4
    for z in range(4):
        for g in range(3):
            store(z, g * half, t[g * n + z * r : g * n + (z + 1) * r])
        at = 3 * n + z * (m // 4)
        p = [t[at + g * m : at + g * m + m // 4] for g in range(2)]
        store(z, 3 * half, jnp.concatenate(p, 0))
    if t.shape[0] > 3 * n + 2 * m:
        sm = t[3 * n + 2 * m :]
        sm = jnp.concatenate([sm[:, 128 * g : 128 * (g + 1)] for g in range(3)], 0)
        for z in range(4):
            store(z, 4 * half, sm[z * r : (z + 1) * r])


def spread_pair_rows(t, first, store):
    r = t.shape[1] // 4
    for i in range(2):
        for z in range(4):
            store(z, first + i * t.shape[2], t[i, z * r : (z + 1) * r])


def columns_of(groups, after=()):
    wide = 0
    for t in groups:
        wide += 2 * t.shape[2] if t.ndim == 3 else 4 * t.shape[1] + (128 if t.shape[0] > 2 * t.shape[1] else 0)
    r = groups[0].shape[1] // 4 if groups[0].ndim == 3 else groups[0].shape[1] // 8

    def kernel(*refs):
        out = refs[len(groups)]

        def store(z, lane, value):
            out[z, :, pl.ds(lane, value.shape[1])] = value.astype(BF)

        at = 0
        for ref in refs[: len(groups)]:
            t = ref[...]
            if t.ndim == 3:
                spread_pair_rows(t, at, store)
                at += 2 * t.shape[2]
            else:
                spread_attend_rows(t, lambda z, lane, value, at=at: store(z, at + lane, value))
                at += 4 * t.shape[1] + (128 if t.shape[0] > 2 * t.shape[1] else 0)

    return call(
        kernel, [((4, r, wide), BF, VM)], [(t, VM) for t in groups], after=after,
        bytes_accessed=3 * 2**20,
    )[0]


def last_columns(where, upper, lower, pair, after=()):
    half = upper.shape[1]
    r = half // 8
    wide = 4 * half + 2 * pair.shape[2]

    def kernel(where_ref, upper_ref, lower_ref, pair_ref, *refs):
        outs, scratch = refs[:4], refs[4]

        def store(z, lane, value):
            scratch[z, :, pl.ds(lane, value.shape[1])] = value

        spread_attend_rows(jnp.concatenate([upper_ref[...], lower_ref[...]], 0), store)
        spread_pair_rows(pair_ref[...], 4 * half, store)
        c = where_ref[2]
        outs[0][...] = scratch[c]
        for j in range(1, 4):
            outs[j][...] = scratch[c ^ j].astype(BF)

    return call(
        kernel,
        [((r, wide), F32, VM)] + [((r, wide), BF, VM)] * 3,
        [(where, SM), (upper, VM), (lower, VM), (pair, VM)],
        scratch=[pltpu.VMEM((4, r, wide), F32)],
        after=after,
        bytes_accessed=6 * 2**20,
    )


def join_upstream(u_own, u_sib, rows):
    feat = u_own.shape[1]

    def kernel(o_ref, s_ref, u_ref, low_ref):
        u_ref[pl.ds(0, rows), :] = o_ref[...]
        u_ref[pl.ds(rows, rows), :] = s_ref[...].astype(F32)
        low_ref[pl.ds(0, rows), :] = o_ref[...].astype(BF)
        low_ref[pl.ds(rows, rows), :] = s_ref[...]

    return call(
        kernel, [((2 * rows, feat), F32, VM), ((2 * rows, feat), BF, VM)], [(u_own, VM), (u_sib, VM)],
        bytes_accessed=2**21,
    )


def norm_step(u, x, gains, gain_row, part, got, rows, last, after=()):
    feat = x.shape[1]
    n = rows if last else 2 * rows

    def kernel(u_ref, x_ref, gains_ref, part_ref, got_ref, *outs):
        if last:
            slope = part_ref[...] + got_ref[...].astype(F32)
        else:
            slope = add_both(part_ref[...], got_ref[...], rows)
        u2 = u_ref[:n] + norm_back(x_ref[:n], gains_ref[pl.ds(gain_row, 1), :], slope)[0]
        low = outs[-1]
        low[...] = u2[: low.shape[0]].astype(BF)
        if not last:
            outs[0][...] = u2

    outs = [((last if last else n, feat), BF, VM)]
    return call(
        kernel,
        outs if last else [((n, feat), F32, VM)] + outs,
        [(u, VM), (x, VM), (gains, VM), (part, VM), (got, VM)],
        after=after,
        bytes_accessed=6 * 2**20,
    )


def picks(index, turn, cap, cap_rows, experts):
    at = lax.broadcasted_iota(jnp.int32, (1, experts * cap_rows), 1)
    out = []
    for k in range(TOP):
        chosen, slot = index[:, k : k + 1], index[:, TOP + k : TOP + k + 1]
        place = chosen if turn is None else chosen ^ turn
        target = jnp.where(slot < cap, place * cap_rows + slot, -1)
        out.append(jnp.where(at == target, 1.0, 0.0).astype(BF))
    return out


def lane_at(index, k):
    lane = lax.broadcasted_iota(jnp.int32, (1, 128), 1)
    return jnp.where(lane == index[:, k : k + 1] + 4, 1.0, 0.0)


def present_mask(blk, rows, blk_len, longest):
    pos = lax.broadcasted_iota(jnp.int32, (rows, 1), 0)
    last = jnp.where(blk < longest, blk_len, blk_len - 1)
    return jnp.where(pos < last, 1.0, 0.0)


def route(where, x, part, got, gains, small, cot, index, experts, cap, rows, blk_len, longest, fast, after=()):
    feat = x.shape[1]
    cap_rows = up16(cap)

    def kernel(where_ref, x_ref, part_ref, got_ref, gains_ref, small_ref, cot_ref, index_ref,
               x3_ref, moe_ref, gates_ref, up_ref, *blocks):
        x3 = x_ref[:rows] + part_ref[:rows] + got_ref[...].astype(F32)
        x3_ref[...] = x3
        moe = layer_norm(x3, gains_ref[pl.ds(3, 1), :])
        moe_ref[...] = moe
        lane = lax.broadcasted_iota(jnp.int32, (1, 128), 1)
        logits = dot(moe, small_ref[...])
        logits = jnp.where((lane >= 4) & (lane < 4 + experts), logits, -1e30)
        ex = jnp.exp(logits - jnp.max(logits, -1, keepdims=True))
        gates = ex / jnp.sum(ex, -1, keepdims=True)
        gates_ref[...] = gates
        up_ref[...] = jnp.zeros_like(up_ref)
        up_ref[pl.ds(0, blk_len), :] = cot_ref[...].astype(F32)
        up = up_ref[...] * present_mask(where_ref[0], rows, blk_len, longest)
        up_ref[...] = up
        index = index_ref[...]
        pick = picks(index, where_ref[1] if fast else None, cap, cap_rows, experts)
        sent = t_dot(pick[0] + pick[1], moe).astype(BF)
        slope = 0.0
        for k in range(TOP):
            gate = jnp.sum(gates * lane_at(index, k), -1, keepdims=True)
            slope += t_dot(pick[k], (gate * up).astype(BF))
        slope = slope.astype(BF)
        for j, ref in enumerate(blocks):
            ref[pl.ds(0, cap_rows), :] = sent[j * cap_rows : (j + 1) * cap_rows]
            ref[pl.ds(cap_rows, cap_rows), :] = slope[j * cap_rows : (j + 1) * cap_rows]

    return call(
        kernel,
        [((rows, feat), F32, VM), ((rows, feat), BF, VM), ((rows, 128), F32, VM), ((rows, feat), F32, VM)]
        + [((2 * cap_rows, feat), BF, VM)] * experts,
        [(where, SM), (x, VM), (part, VM), (got, VM), (gains, VM), (small, VM), (cot, VM), (index, VM)],
        after=after,
        flops=6 * rows * experts * cap_rows * feat,
        bytes_accessed=5 * 2**20,
    )


def experts_forward(blocks, own, sib, cap_rows, after=()):
    feat, wide = own[0].shape
    tile = 512 if wide % 512 == 0 else wide
    n = len(blocks) * cap_rows
    steps = wide // tile

    def kernel(*refs):
        refs = list(refs)
        take = lambda k: [refs.pop(0) for _ in range(k)]
        ins, weights = take(len(blocks)), take(4)
        take(len(after))
        outs = take(len(blocks))
        rows_ref, slope_ref, res_ref, back_ref = take(4)
        t = pl.program_id(0)

        @pl.when(t == 0)
        def _():
            for j, ref in enumerate(ins):
                at = pl.ds(j * cap_rows, cap_rows)
                rows_ref[at, :] = ref[pl.ds(0, cap_rows), :]
                slope_ref[at, :] = ref[pl.ds(cap_rows, cap_rows), :]
            res_ref[...] = jnp.zeros_like(res_ref)
            back_ref[...] = jnp.zeros_like(back_ref)

        def step(wi_ref, wo_ref):
            act, dact = gelu_both(dot(rows_ref[...], wi_ref[...]))
            hs = (dact * dot_t(slope_ref[...], wo_ref[...])).astype(BF)
            res_ref[...] += dot(act.astype(BF), wo_ref[...])
            back_ref[...] += dot_t(hs, wi_ref[...])

        @pl.when(t < steps)
        def _():
            step(*weights[:2])

        @pl.when(t >= steps)
        def _():
            step(*weights[2:])

        @pl.when(t == 2 * steps - 1)
        def _():
            for j, ref in enumerate(outs):
                at = pl.ds(j * cap_rows, cap_rows)
                ref[pl.ds(0, cap_rows), :] = res_ref[at, :].astype(BF)
                ref[pl.ds(cap_rows, cap_rows), :] = back_ref[at, :].astype(BF)

    blk = (2 * cap_rows, feat)
    whole = pl.BlockSpec(blk, lambda t: (0, 0))
    first = lambda t: jnp.minimum(t, steps - 1)
    later = lambda t: jnp.maximum(t - steps, 0)
    specs = []
    for place in (first, later):
        specs.append(pl.BlockSpec((feat, tile), lambda t, place=place: (0, place(t))))
        specs.append(pl.BlockSpec((tile, feat), lambda t, place=place: (place(t), 0)))
    return pl.pallas_call(
        kernel,
        grid=(2 * steps,),
        out_shape=[jax.ShapeDtypeStruct(blk, BF)] * len(blocks),
        in_specs=[whole] * len(blocks) + specs + [HB] * len(after),
        out_specs=[whole] * len(blocks),
        scratch_shapes=[
            pltpu.VMEM((n, feat), BF), pltpu.VMEM((n, feat), BF),
            pltpu.VMEM((n, feat), F32), pltpu.VMEM((n, feat), F32),
        ],
        compiler_params=pltpu.CompilerParams(
            vmem_limit_bytes=62 * 2**20, dimension_semantics=("arbitrary",)
        ),
        cost_estimate=pl.CostEstimate(
            flops=16 * n * feat * wide, bytes_accessed=20 * 2**20, transcendentals=0
        ),
    )(*blocks, *own, *sib, *after)


def expert_slopes(every, w_in, w_out, got, after=()):
    feat, wide = w_in.shape
    tile = 512 if wide % 512 == 0 else wide
    steps = wide // tile
    groups, experts, cap_rows = every.shape[0], every.shape[1], every.shape[2] // 2
    total = groups * experts * cap_rows
    kind = BF if got is None else F32

    def kernel(*refs):
        refs = list(refs)
        take = lambda k: [refs.pop(0) for _ in range(k)]
        every_ref, wi_ref, wo_ref = take(3)
        got_refs = take(2) if got is not None else None
        take(len(after))
        wis_ref, wos_ref, rows_ref, slope_ref, turned_ref, sems = take(6)

        @pl.when(pl.program_id(0) == 0)
        def _():
            copies = []
            for k in range(groups):
                for j in range(experts):
                    at = pl.ds((k * experts + j) * cap_rows, cap_rows)
                    for i, ref in enumerate((rows_ref, slope_ref)):
                        copies.append(pltpu.make_async_copy(
                            every_ref.at[k, j, pl.ds(i * cap_rows, cap_rows)], ref.at[at],
                            sems.at[len(copies)],
                        ))
            start_all(copies)
            per = total // groups
            for k in range(groups):
                wait_all(copies[k * 2 * experts : (k + 1) * 2 * experts])
                at = pl.ds(k * per, per)
                turned_ref[:, at] = rows_ref[at, :].T

        act, dact = gelu_both(dot(rows_ref[...], wi_ref[...]))
        hs = (dact * dot_t(slope_ref[...], wo_ref[...])).astype(BF)
        wis = dot(turned_ref[...], hs)
        wos = t_dot(act.astype(BF), slope_ref[...])
        if got is not None:
            wis, wos = wis + got_refs[0][...].astype(F32), wos + got_refs[1][...].astype(F32)
        wis_ref[...] = wis.astype(kind)
        wos_ref[...] = wos.astype(kind)

    wi_spec = pl.BlockSpec((feat, tile), lambda t: (0, t))
    wo_spec = pl.BlockSpec((tile, feat), lambda t: (t, 0))
    return pl.pallas_call(
        kernel,
        grid=(steps,),
        out_shape=[jax.ShapeDtypeStruct((feat, wide), kind), jax.ShapeDtypeStruct((wide, feat), kind)],
        in_specs=[HB] + [wi_spec, wo_spec] * (1 if got is None else 2) + [HB] * len(after),
        out_specs=[wi_spec, wo_spec],
        scratch_shapes=[
            pltpu.VMEM((total, feat), BF), pltpu.VMEM((total, feat), BF), pltpu.VMEM((feat, total), BF),
            pltpu.SemaphoreType.DMA((2 * groups * experts,)),
        ],
        compiler_params=pltpu.CompilerParams(
            vmem_limit_bytes=56 * 2**20, dimension_semantics=("arbitrary",)
        ),
        cost_estimate=pl.CostEstimate(
            flops=8 * total * feat * wide, bytes_accessed=20 * 2**20, transcendentals=0
        ),
    )(every, w_in, w_out, *(got or ()), *after)


def combine(where, blocks, x3, moe, gates, up, index, small, gains, small_rows, experts, cap, rows, blk_len, longest, fast, after=()):
    feat = x3.shape[1]
    cap_rows = up16(cap)
    n = experts * cap_rows

    def kernel(where_ref, *refs):
        refs = list(refs)
        take = lambda k: [refs.pop(0) for _ in range(k)]
        ins = take(experts)
        x3_ref, moe_ref, gates_ref, up_ref, index_ref, small_ref, gains_ref = take(7)
        acts_ref, u_ref, low_ref, slopes_ref, result_ref, back_ref = take(6)
        for j, ref in enumerate(ins):
            at = pl.ds(j * cap_rows, cap_rows)
            result_ref[at, :] = ref[pl.ds(0, cap_rows), :]
            back_ref[at, :] = ref[pl.ds(cap_rows, cap_rows), :]
        index, gates, up, moe = index_ref[...], gates_ref[...], up_ref[...], moe_ref[...]
        pick = picks(index, where_ref[1] if fast else None, cap, cap_rows, experts)
        x3 = x3_ref[...]
        acts, all_slope = x3, 0.0
        for k in range(TOP):
            at_k = lane_at(index, k)
            gate = jnp.sum(gates * at_k, -1, keepdims=True)
            picked = dot(pick[k], result_ref[...])
            acts = acts + gate * picked
            all_slope += jnp.sum(up * picked, -1, keepdims=True) * at_k
        acts = acts * present_mask(where_ref[0], rows, blk_len, longest)
        acts_ref[...] = acts[:blk_len].astype(BF)
        logit = (gates * (all_slope - jnp.sum(gates * all_slope, -1, keepdims=True))).astype(BF)
        slope = dot(pick[0] + pick[1], back_ref[...]) + dot_t(logit, small_ref[...])
        dx, terms = norm_back(x3, gains_ref[pl.ds(3, 1), :], slope)
        u = up + dx
        u_ref[...] = u
        low_ref[...] = u.astype(BF)
        slopes_ref[...] = t_dot(logit, moe)[:small_rows]
        slopes_ref[pl.ds(3, 1), :] = jnp.sum(terms, 0, keepdims=True)

    return call(
        kernel,
        [((blk_len, feat), BF, VM), ((rows, feat), F32, VM), ((rows, feat), BF, VM), ((small_rows, feat), F32, VM)],
        [(where, SM)] + [(b, VM) for b in blocks]
        + [(t, VM) for t in (x3, moe, gates, up, index, small, gains)],
        scratch=[pltpu.VMEM((n, feat), BF), pltpu.VMEM((n, feat), BF)],
        after=after,
        flops=6 * rows * n * feat,
        bytes_accessed=5 * 2**20,
    )


def tie(xs, *after):
    return list(lax.optimization_barrier((*xs, *after)))[: len(xs)]


class Links:
    def __init__(self, mesh):
        self.E = mesh.shape["expert"]
        self.C = mesh.shape["context"]
        self.D = mesh.shape["dp"]
        assert self.C == 4 and self.D == 2 and self.E % 2 == 0
        self.fast = self.E == 4
        self.chips = self.E * self.C
        flat = lambda e, c, d: (e * self.C + c) * self.D + d
        self.team = [
            (flat(e, c, d), flat((e // 2) * 2 + c // 2, 2 * (e % 2) + d, c % 2))
            for e in range(self.E)
            for c in range(self.C)
            for d in range(self.D)
        ]
        self.to_lane = [(f, (f % self.chips) * 2 + f // self.chips) for f in range(2 * self.chips)]
        self.from_lane = [(b, a) for a, b in self.to_lane]

    def move(self, x):
        return lax.ppermute(x, ALL, self.team)

    def xor(self, x, axis, j):
        n = {"expert": self.E, "context": self.C, "dp": self.D}[axis]
        return lax.ppermute(x, axis, [(i, i ^ j) for i in range(n)])

    def sib(self, x):
        return self.xor(x, "dp", 1)

    def partner(self, x):
        return self.xor(x, "expert", 1)

    def column(self, x, *hold):
        c = lax.axis_index("context")
        got = tie([x] + [self.xor(x, "context", j) for j in range(1, 4)], *hold)
        pick = lambda k: jnp.where(
            c & 2 == 0, jnp.where(c & 1 == 0, got[k], got[k ^ 1]), jnp.where(c & 1 == 0, got[k ^ 2], got[k ^ 3])
        )
        return jnp.stack([pick(k) for k in range(4)])

    def plane_sum(self, keep, send, first, hold):
        (got,) = tie([self.xor(send, "expert", first)], *hold[0])
        got = got.astype(F32)
        give = (keep[1].astype(F32) + got[1]).astype(BF)
        (far,) = tie([self.xor(give, "expert", 3 - first)], *hold[1])
        return keep[0].astype(F32) + got[0] + far.astype(F32), give

    def column_sum(self, x, *hold):
        c = lax.axis_index("context")
        low = x.astype(BF)
        got = [self.xor(lax.dynamic_index_in_dim(low, c ^ j, 0, False), "context", j) for j in range(1, 4)]
        got = tie(got, *hold)
        total = lax.dynamic_index_in_dim(x, c, 0, False)
        for t in got:
            total = total + t.astype(F32)
        return total

    def swap_blocks(self, x):
        if not self.fast:
            return list(lax.all_to_all(jnp.stack(x), "expert", 0, 0, tiled=True))
        return [x[0]] + [self.xor(x[j], "expert", j) for j in range(1, 4)]


def lane_rows(links, mine, d):
    keep = lax.dynamic_index_in_dim(mine, d, 0, False)
    got = links.sib(lax.dynamic_index_in_dim(mine, 1 - d, 0, False))
    return jnp.where(d == 0, jnp.concatenate([keep, got], 0), jnp.concatenate([got, keep], 0))


def in_order(d, own, other):
    return jnp.where(d == 0, jnp.stack([own, other]), jnp.stack([other, own]))


class Weights:
    def __init__(self, links, rdev, feat, ff):
        self.links, self.rdev, self.feat, self.ff = links, rdev, feat, ff
        self.d = lax.axis_index("dp")
        self.half = feat // 2

    def split_attend(self, w):
        w = w.reshape(self.rdev, 3, 2, self.half).transpose(2, 0, 1, 3)
        return w.reshape(2, self.rdev, 3 * self.half)

    def split_widen(self, w):
        w = w.reshape(self.rdev, self.links.chips, 2, 2, -1).transpose(2, 0, 3, 1, 4)
        return w.reshape(2, self.rdev, self.ff // 2)

    def pack_attend(self, w, p, small):
        parts = [w, jnp.concatenate([p[:, : self.half], p[:, self.half :]], 0)]
        if small is not None:
            parts.append(jnp.pad(small, ((0, 0), (0, 128 - small.shape[1]))))
        return jnp.concatenate(parts, 1)

    def pack_wide(self, wout):
        h = wout.shape[0] // 2
        return jnp.concatenate([wout[:h], wout[h:]], 1)

    def column(self, buf, *hold):
        if self.links.fast:
            return self.links.column(buf, *hold)
        return lax.all_gather(buf, CHIPS, axis=0, tiled=False)

    def cut(self, x):
        return x if self.links.fast else x.reshape(4, -1, x.shape[-1])

    def pack_block(self, quad, between):
        f, h, r = self.feat, self.half, self.rdev
        n = quad.shape[0]
        p = quad[..., f + h : 2 * f].reshape(n, 2, r, h)
        parts = [quad[..., i * h : (i + 1) * h] for i in range(3)] + [p[:, 0], p[:, 1]]
        parts = [self.cut(t.reshape(-1, h)) for t in parts]
        if self.links.fast:
            parts.insert(2, between)
        if quad.shape[2] > 2 * f:
            small = self.cut(quad[..., 2 * f :].reshape(-1, 128))
            small = small.reshape(small.shape[:-2] + (3, -1, 128))
            parts.append(jnp.concatenate([small[..., g, :, :] for g in range(3)], -1))
        return jnp.concatenate(parts, -2)

    def pack_pair(self, quad_in, quad_out):
        f = self.feat
        halves = []
        for i in range(2):
            pair = [self.cut(t[..., i * f : (i + 1) * f].reshape(-1, f)) for t in (quad_in, quad_out)]
            halves.append(jnp.stack(pair, -3))
        return jnp.stack(halves, -4)

    def spread(self, x, cuts, *hold):
        if not self.links.fast:
            return [x[0], x[1], x[2], cuts[0](x[3]), cuts[1](x[3])]
        to = lambda t, j: self.links.xor(t, "expert", j)
        x1, x2 = tie([to(x, 1), to(x, 2)], *hold)
        return [x, x1, x2, to(cuts[0](x1), 2), to(cuts[1](x2), 1)]

    def spread_attend(self, x, skip, *hold):
        n = self.feat // 2 + skip
        return self.spread(x, (lambda t: t[:n], lambda t: t[n:]), *hold)

    def spread_pair(self, x, *hold):
        return self.spread(x, (lambda t: t[0], lambda t: t[1]), *hold)

    def total(self, keep, send, first, hold):
        if self.links.fast:
            out, _ = self.links.plane_sum(keep, send, first, hold)
            return out
        blk = {0: keep[0], 3 - first: keep[1], first: send[0], 3: send[1]}
        return jnp.stack([blk[j] for j in range(4)])

    def all_sum(self, buf):
        return lax.psum_scatter(buf.astype(BF), CHIPS, scatter_dimension=0, tiled=False).astype(F32)

    def exchange(self, w):
        w = w.reshape(2, self.rdev, -1)
        mine = lax.dynamic_index_in_dim(w, self.d, 0, False)
        got = self.links.sib(lax.dynamic_index_in_dim(w, 1 - self.d, 0, False))
        return in_order(self.d, mine, got)

    def to_columns(self, t):
        n, m = self.feat // 4, self.half // 4
        r = self.rdev
        cut = lambda t, k: t.reshape(-1, k * r, t.shape[-1])
        parts = [cut(t[..., g * n : (g + 1) * n, :], 2) for g in range(3)]
        p = [cut(t[..., 3 * n + g * m : 3 * n + (g + 1) * m, :], 1) for g in range(2)]
        parts.append(jnp.concatenate(p, 1))
        if t.shape[-2] > 3 * n + 2 * m:
            sm = t[..., 3 * n + 2 * m :, :]
            sm = jnp.stack([sm[..., 128 * g : 128 * (g + 1)] for g in range(3)], -3)
            parts.append(sm.reshape(-1, 2 * r, 128))
        return jnp.concatenate(parts, 2)

    def owners(self, col1, col3, w2):
        f, h, r = self.feat, self.half, self.rdev
        w = f + h
        p = [jnp.concatenate([c[:r, w : 2 * f], c[r:, w : 2 * f]], 1) for c in (col1, col3)]
        p = lax.ppermute(jnp.concatenate(p, 0), ALL, self.links.from_lane)
        t = self.exchange(jnp.concatenate([col1[:, :w], col3[:, :w], col3[:, 2 * f :], w2], 1))

        def attend(t):
            return t.reshape(2, r, 3, h).transpose(1, 2, 0, 3).reshape(r, 3 * f)

        small = t[..., 2 * w : 2 * w + 128]
        win = t[..., 2 * w + 128 :].reshape(2, r, 2, self.links.chips, -1)
        win = win.transpose(1, 3, 0, 2, 4).reshape(r, self.ff)
        return attend(t[..., :w]), p[:r], attend(t[..., w : 2 * w]), p[r:], small[0] + small[1], win


def body(links, *args):
    (tokens, cotangent, g1, w1, p1, g2, win, wout, g3, w3, p3, g4, router, ein, eout, routes, slots) = args
    e = lax.axis_index("expert")
    d = lax.axis_index("dp")
    blk_len, feat = tokens.shape[1:]
    rows = up16(blk_len)
    half = feat // 2
    rdev = w1.shape[0]
    ff = win.shape[1]
    longest = LEN - (blk_len - 1) * links.C
    experts = router.shape[1]
    assert experts <= 128
    small_rows = (4 + experts + 7) // 8 * 8
    cap = max(2, (5 * TOP * blk_len + 4 * experts - 1) // (4 * experts))
    blk = 2 * (e % 2) + d
    where = jnp.stack([blk, e if links.fast else 0 * e, lax.axis_index("context")]).astype(jnp.int32)
    wt = Weights(links, rdev, feat, ff)
    img = dict(rows=rows, blk_len=blk_len, longest=longest)

    tok = links.move(tokens[0])
    ps = lax.ppermute(jnp.concatenate([p1, p3], 0), ALL, links.to_lane)
    small = jnp.concatenate([g1[:, None], g2[:, None], g3[:, None], g4[:, None], router], 1)
    gsm = small.shape[1]
    lane1 = jnp.concatenate(
        [wt.split_attend(w1), jnp.broadcast_to(small[None], (2, rdev, gsm))], 2
    )
    lane1 = lane_rows(links, lane1, d)
    buf1 = wt.pack_attend(lane1[:, : 3 * half], ps[:rdev], lane1[:, 3 * half :])
    quad1 = wt.column(buf1)
    later = jnp.concatenate([wt.split_widen(win), wt.split_attend(w3)], 2)
    later = lane_rows(links, later, d)
    w_in, w_out = later[:, : ff // 2], wt.pack_wide(wout)
    w3_lane, p3_lane = later[:, ff // 2 :], ps[rdev:]
    block3 = jnp.concatenate(
        [w3_lane[:, g * half : (g + 1) * half] for g in range(3)] + [p3_lane[:, :half], p3_lane[:, half:]], 0
    )
    skip = block3.shape[0] if links.fast else 0
    tok_pair = jnp.stack([tok, links.partner(tok)])
    block1 = wt.pack_block(tie([quad1], tok_pair)[0], block3)
    if links.fast:
        (buf2,) = tie([jnp.concatenate([w_in, w_out], 1)], quad1)
        quad2 = wt.column(buf2)
        blocks1 = wt.spread_attend(block1, skip, quad2)
        (tok_pair,) = tie([tok_pair], *blocks1[1:3])
    else:
        quad2 = None
        blocks1 = wt.spread_attend(block1, skip)
    tok_sib = links.sib(tok_pair)
    toks = [tok_pair[0], tok_sib[0], tok_pair[1], tok_sib[1]]
    raw = jnp.concatenate([routes[0], slots[0]], 1).astype(BF)
    cot = jnp.concatenate([cotangent[0].astype(BF), jnp.pad(raw, ((0, 0), (0, 128 - 2 * TOP)))], 1)
    cot = links.move(tie([cot], *blocks1[1:3])[0])
    if links.fast:
        (quad2,) = tie([quad2], *blocks1[3:], *toks, cot)
        pair2 = wt.pack_pair(quad2[..., : ff // 2], quad2[..., ff // 2 :])
        q, n = feat // 2, block3.shape[0]
        place3 = jnp.stack([t[q : q + n] for t in blocks1[:4]])
        source3 = lax.all_gather(place3, "context", axis=0, tiled=False)
        p3 = source3[:, :, 6 * rdev :].reshape(4, 4, 2, rdev, half)
        p3 = jnp.stack([lax.dynamic_index_in_dim(p3, e ^ k, 1, False) for k in range(4)])
        wp3 = p3.transpose(0, 1, 3, 2, 4).reshape(half, feat)
    else:
        pair2 = wt.pack_pair(wt.column(w_in), wt.column(w_out))
        all3 = lax.all_gather(block3, CHIPS, axis=0, tiled=False)
        source3 = all3[:, : 6 * rdev].reshape(links.chips, 3, 2 * rdev, half)
        source3 = source3.transpose(0, 2, 1, 3).reshape(feat, 3 * half)
        wp3 = all3[:, 6 * rdev :].reshape(links.chips, 2, rdev, half)
        wp3 = wp3.transpose(0, 2, 1, 3).reshape(half, feat)

    x0, normed1, q1, kv1, far1, wa1, wp1, small, gains = attend_first(
        where, toks, small_rows, blocks1, rows, skip
    )
    part, low, blend1, lse1 = attend_core(
        where, q1, kv1, far1, wp1, solo=False, **img
    )
    blocks2 = wt.spread_pair(pair2, part)
    x1, normed2, hidden, part2, low2 = widen_forward(
        where, x0, part, links.sib(low), gains, blocks2, rows
    )
    x2, normed3, own3 = norm_next(x1, part2, links.sib(low2), gains, 2, rows)
    ein_own, eout_own = ein[0], eout[0]
    ein_sib, eout_sib = [links.sib(t) for t in tie([ein_own, eout_own], own3)]
    far_own = links.partner(own3)
    q3, kv3, wa3 = attend_next(where, normed3, source3)
    (far_own,) = tie([far_own], q3)
    part3, low3, blend3, lse3, far3 = attend_core(
        where, q3, kv3, None, wp3, solo=True, far=(far_own, links.sib(far_own), wa3), **img
    )
    moe_args = dict(experts=experts, cap=cap, fast=links.fast, **img)
    index = cot[:, feat : feat + 2 * TOP].astype(jnp.int32)
    index = jnp.pad(index, ((0, rows - blk_len), (0, 0)), constant_values=cap)
    x3, moe, gates, up, *sent = route(
        where, x2, part3, links.sib(low3), gains, small, cot[:, :feat], index,
        after=(ein_sib, eout_sib), **moe_args
    )
    came = links.swap_blocks(sent)
    every = lax.all_gather(jnp.stack(came), "context", axis=0, tiled=False)
    answer = experts_forward(came, (ein_own, eout_own), (ein_sib, eout_sib), up16(cap))
    answer = links.swap_blocks(answer)
    acts, u, u_low, small_slopes = combine(
        where, answer, x3, moe, gates, up, index, small, gains, small_rows, **moe_args
    )

    u, u_low = join_upstream(u, links.sib(u_low), rows)
    dq, own, far, wps = attend_core_back(where, u_low, wp3, blend3, q3, kv3, far3, lse3, **img)
    first3, first2, first1 = (1,), 2, (1, 2)
    part, low, *slopes3 = attend_proj_back(
        where, dq, own, links.partner(far), normed3, wa3, wps, small_slopes, first3, rows, False
    )
    u, part, low, *slopes2 = widen_back(
        where, u, x2, gains, part, links.sib(low), normed2, hidden, blocks2, first2, rows, False
    )
    u1, u_low = norm_step(u, x1, gains, 1, part, links.sib(low), rows, 0)
    dq1, own, far, wps = attend_core_back(where, u_low, wp1, blend1, q1, kv1, far1, lse1, **img)
    part, low, *slopes1 = attend_proj_back(
        where, dq1, own, links.partner(far), normed1, wa1, wps, None, first1, rows, True, after=(every,)
    )
    (u2,) = norm_step(u1, x0, gains, 0, part, links.sib(low), rows, blk_len)
    moved = links.move(jnp.stack([acts, u2]))
    acts, token_slope = moved[0], moved[1]
    e_sib = expert_slopes(every, ein_sib, eout_sib, None, after=(u2,))
    sum3 = wt.total(*slopes3, first3[0], ((low,), (e_sib[0],)))
    sum2a = wt.total(*slopes2[:2], first2, ((low,), (e_sib[0],)))
    sum2b = wt.total(*slopes2[2:], first2, ((e_sib[0],), ()))
    sum1 = [wt.total(*slopes1[2 * i : 2 * i + 2], first1[i], ((e_sib[0],), ())) for i in range(2)]
    if links.fast:
        early = columns_of([sum3, sum2a])
        early = lax.psum_scatter(tie([early], every)[0], "context", scatter_dimension=0, tiled=False)
        own, *away = last_columns(where, *sum1, sum2b, after=(moved,))
        e_slopes = expert_slopes(every, ein_own, eout_own, [links.sib(t) for t in e_sib], after=(own,))
        for t in tie([links.xor(t, "context", j + 1) for j, t in enumerate(away)], e_slopes[0]):
            own = own + t.astype(F32)
        early = tie([early], e_slopes[0])[0].astype(F32)
        col1, col2b = own[:, : 2 * feat], own[:, 2 * feat :]
        col3, col2a = early[:, : early.shape[1] - 2 * feat], early[:, early.shape[1] - 2 * feat :]
        w2 = jnp.concatenate([col2a[:, :feat], col2b[:, :feat]], 1)
        wout_out = jnp.concatenate([col2a[:, feat:], col2b[:, feat:]], 0)
    else:
        e_slopes = expert_slopes(every, ein_own, eout_own, [links.sib(t) for t in e_sib])
        col3, col1 = wt.to_columns(sum3), wt.to_columns(jnp.concatenate(sum1, -2))
        col3, col1 = wt.all_sum(col3), wt.all_sum(col1)
        hid = ff // (4 * links.chips)
        w2 = [t[..., 0, :, :].reshape(-1, 2 * rdev, feat) for t in (sum2a, sum2b)]
        w2_out = [t[..., 1, :, :].reshape(-1, hid, feat) for t in (sum2a, sum2b)]
        w2, w2_out = [wt.all_sum(jnp.concatenate(t, 2)) for t in (w2, w2_out)]
        wout_out = jnp.concatenate([w2_out[:, :feat], w2_out[:, feat:]], 0)
    w1_out, p1_out, w3_out, p3_out, extra, win_out = wt.owners(col1, col3, w2)

    def gain_slope(w, slope, gain):
        return jnp.sum(w.astype(F32) * slope, 1) / gain.astype(F32)

    return (
        acts.astype(F32)[None], token_slope.astype(F32)[None],
        gain_slope(w1, w1_out, g1), w1_out, p1_out, gain_slope(win, win_out, g2), win_out, wout_out,
        gain_slope(w3, w3_out, g3), w3_out, p3_out, extra[:, 3], extra[:, 4 : 4 + experts],
        e_slopes[0][None], e_slopes[1][None],
    )


def solution(mesh):
    links = Links(mesh)
    tok = P(("expert", "dp"), "context", None)
    vec, mat = P(ALL), P(ALL, None)
    ein, eout = P("expert", None, "dp"), P("expert", "dp", None)
    dense = (vec, mat, mat, vec, mat, mat, vec, mat, mat, vec, mat, ein, eout)
    return jax.shard_map(
        functools.partial(body, links),
        mesh=mesh,
        in_specs=(tok, tok) + dense + (tok, tok),
        out_specs=(tok, tok) + dense,
        check_vma=False,
    )
```
